32 devices in a mesh: groups: 2 (over x), row: 16 (over z, y, core).
Axes of the slice: x: 2, y: 2, z: 4, core: 2. Of those that a mesh axis runs over, the one named last changes fastest.
Arguments:
- h_blocks: float32 [32, 14, 128, 128], P(('groups', 'row')), parts along dimension 0, may hold values from -0.09375 to 0.09375
- h_cols: int32 [32, 14], P(('groups', 'row')), parts along dimension 0, may hold values from 0 to 15, as said below
- term_prev: float32 [32, 14, 128, 128], P(('groups', 'row')), parts along dimension 0, may hold values from -6 to 6
- term_cur: float32 [32, 14, 128, 128], P(('groups', 'row')), parts along dimension 0, may hold values from -6 to 6
- t_cols: int32 [32, 14], P(('groups', 'row')), parts along dimension 0, may hold values from 0 to 15, as said below
- density_in: float32 [32, 14, 128, 128], P(('groups', 'row')), parts along dimension 0, may hold values from -6 to 6
- coefs: float32 [3], replicated, may hold values from -1 to 1
Outputs:
- density: float32 [32, 14, 128, 128], P(('groups', 'row')), parts along dimension 0
- term_last: float32 [32, 14, 128, 128], P(('groups', 'row')), parts along dimension 0
- term_before: float32 [32, 14, 128, 128], P(('groups', 'row')), parts along dimension 0
The draws below stay inside these ranges and needn't reach their ends.
There are 2 independent parts, one for each index of `groups`. The reference program is written for one: setup_inputs(seed, part) draws one part's arguments, and reference() takes and returns one part's arrays. A program takes and returns all parts, laid end to end along the dimension named above; an argument that names none is the same for every part. Nothing has to cross between parts.
Inputs may be any that keep to these rules, and one draw needn't show every extreme that they name: `h_cols`: each row i names 14 distinct block columns (i + o) mod 16, with offsets o taken from -7 to 7 (all but one of them), in rising order of o; offset 0 is always named. `t_cols`: same law as h_cols, drawn independently.
All inputs are finite; a program needn't handle non-finite values.
Results may differ from the reference program's by a relative error of at most 0.0003.
Values sent between devices are 32-bit elements; how exact they have to be, the bound alone decides.
No kernel may reach another device: no remote copies, remote signals or barrier semaphores. Data moves between devices by JAX's collectives and lax.ppermute only.
A program may use at most 128 MiB of HBM per device.

```python
import jax
import jax.numpy as jnp
from jax import lax

B = 128
REACH = 7
K = 14
STEPS = 3
NB = 16


def pattern_cols(key):
    count = 2 * REACH
    base = jnp.arange(-REACH, REACH + 1, dtype=jnp.int32)
    dropped = jax.random.randint(key, (NB, 1), 0, count).astype(jnp.int32)
    dropped = dropped + (dropped >= REACH).astype(jnp.int32)
    places = jnp.arange(count, dtype=jnp.int32)[None, :]
    places = places + (places >= dropped).astype(jnp.int32)
    offsets = base[places]
    rows_index = jnp.arange(NB, dtype=jnp.int32)[:, None]
    return jnp.mod(rows_index + offsets, NB).astype(jnp.int32)


def draw_h_cols(key, part):
    key = jax.random.fold_in(key, 11)
    return pattern_cols(key)


def draw_t_cols(key, part):
    key = jax.random.fold_in(key, 23)
    return pattern_cols(key)


def block_levels(rng, extent, split, smallest, top_value):
    def one(dim, parts):
        heights = jax.random.uniform(jax.random.fold_in(jax.random.fold_in(rng, 6), dim), (parts,), jnp.float32, smallest / len(split), top_value / len(split))
        return jnp.repeat(jnp.exp(heights), extent[dim] // parts).reshape((-1,) + (1,) * (len(extent) - dim - 1))

    loudness = one(*split[0])
    for cut in split[1:]:
        loudness = loudness * one(*cut)
    return loudness


def noise(key, extent, scale, most, shards=(), kind=jnp.bfloat16):
    factor_of = block_levels(key, extent, shards, -0.22, 0.18) if shards else 1.0
    result = jax.random.normal(key, extent, jnp.float32) * scale * factor_of
    return jnp.minimum(jnp.maximum(result, -most), most).astype(kind)


def setup_inputs(seed: int = 0, part: int = 0) -> dict:
    splits = jax.random.split(jax.random.key(seed), 8)
    own_keys = jax.random.split(jax.random.fold_in(splits[7], part), 8)
    h_blocks = noise(own_keys[0], (NB, K, B, B), (2 * K * B) ** -0.5, 0.09375, ((0, 16),), jnp.float32)
    h_cols = draw_h_cols(jax.random.fold_in(jax.random.fold_in(splits[7], part), 71), part)
    term_prev = noise(own_keys[2], (NB, K, B, B), 1.0, 6.0, ((0, 16),), jnp.float32)
    term_cur = noise(own_keys[3], (NB, K, B, B), 1.0, 6.0, ((0, 16),), jnp.float32)
    t_cols = draw_t_cols(jax.random.fold_in(jax.random.fold_in(splits[7], part), 71), part)
    density_in = noise(own_keys[5], (NB, K, B, B), 1.0, 6.0, ((0, 16),), jnp.float32)
    coefs = jnp.clip(jax.random.uniform(splits[6], (STEPS,), jnp.float32, -1.0, 1.0), -1.0, 1.0)
    return {"h_blocks": h_blocks, "h_cols": h_cols, "term_prev": term_prev, "term_cur": term_cur, "t_cols": t_cols, "density_in": density_in, "coefs": coefs}


def apply_row(current, t_cols, hrow, hcol, tcol):
    picked = current[hcol]
    match = (t_cols[hcol][:, None, :] == tcol[None, :, None]).astype(jnp.float32)
    chosen = jnp.einsum('atm,amxy->atxy', match, picked, precision=lax.Precision.HIGHEST)
    return jnp.einsum('axy,atyz->txz', hrow, chosen, precision=lax.Precision.HIGHEST)


def reference(h_blocks, h_cols, term_prev, term_cur, t_cols, density_in, coefs):
    previous = term_prev
    current = term_cur
    density = density_in
    for step in range(STEPS):
        product = lax.map(lambda row: apply_row(current, t_cols, row[0], row[1], row[2]), (h_blocks, h_cols, t_cols))
        newest = 2.0 * product - previous
        density = density + coefs[step] * newest
        previous = current
        current = newest
    return density, current, previous
```

```python
import functools

import jax
import jax.numpy as jnp
from jax import lax
from jax.experimental import pallas as pl
from jax.experimental.pallas import tpu as pltpu
from jax.sharding import PartitionSpec as P

REACH = 7
STEPS = 3
STAGES = 4


def place_of(offset, dropped):
    named = jnp.logical_and(offset <= 2 * REACH, offset != dropped)
    slot = offset - jnp.where(offset > dropped, 1, 0)
    return jnp.clip(slot, 0, 2 * REACH - 1), named


def dropped_offset(cols, row, total):
    offsets = jnp.mod(cols - row + REACH, total)
    return REACH * (2 * REACH + 1) - jnp.sum(offsets, axis=1)


def pack_kernel(total, row_ref, cols_ref, cur_ref, prev_ref, send_ref, zeros, sem):
    row = row_ref[0]
    drop = row_ref[1]
    zeros[...] = jnp.zeros_like(zeros)
    for k in range(cols_ref.shape[0]):
        col = cols_ref[k]
        pltpu.make_async_copy(cur_ref.at[k], send_ref.at[col, 0], sem).start()
        pltpu.make_async_copy(prev_ref.at[k], send_ref.at[col, 1], sem).start()

    def fill(j, carry):
        offset = lax.rem(j - row + REACH + total, total)
        _, named = place_of(offset, drop)

        @pl.when(jnp.logical_not(named))
        def _():
            pltpu.make_async_copy(zeros, send_ref.at[j], sem).start()

        return carry

    lax.fori_loop(0, total, fill, 0)
    pltpu.make_async_copy(send_ref, send_ref, sem).wait()


def split(x):
    high = x.astype(jnp.bfloat16)
    low = (x - high.astype(jnp.float32)).astype(jnp.bfloat16)
    return high, low


def column_kernel(
    total, window, drops_ref, base_ref, coefs_ref, h_ref, t_ref, out_ref,
    stage, dense, pair, terms, h_sem, t_sem, out_sem,
):
    size = h_ref.shape[-1]
    base = base_ref[0]
    column = base_ref[1]

    def row_of(w):
        return lax.rem(base + w, total)

    def h_copy(w):
        slot = lax.rem(w, STAGES)
        return pltpu.make_async_copy(h_ref.at[row_of(w)], stage.at[slot], h_sem.at[slot])

    def t_copy(w):
        return pltpu.make_async_copy(t_ref.at[row_of(w)], terms.at[w, pl.ds(0, 2)], t_sem)

    def kept(w):
        row = row_of(w)
        offset = lax.rem(column - row + REACH + total, total)
        _, named = place_of(offset, drops_ref[2 * row + 1])
        return named

    for w in range(window):
        t_copy(w).start()
    for w in range(STAGES):
        h_copy(jnp.int32(w)).start()
    pltpu.make_async_copy(terms.at[:, pl.ds(0, 2)], terms.at[:, pl.ds(0, 2)], t_sem).wait()
    for w in range(window):
        high, low = split(jnp.where(kept(w), terms[w, 0], 0.0))
        pair[0, pl.ds(w * size, size), pl.ds(0, size)] = high
        pair[0, pl.ds(w * size, size), pl.ds(size, size)] = low

    def densify(w):
        row = row_of(w)
        drop = drops_ref[2 * row]
        slot = lax.rem(w, STAGES)
        for p in range(window):
            offset = lax.rem(row_of(p) - row + REACH + total, total)
            k, named = place_of(offset, drop)
            high, low = split(jnp.where(named, stage[slot, k], 0.0))
            dense[w, pl.ds(0, size), pl.ds(p * size, size)] = high
            dense[w, pl.ds(size, size), pl.ds(p * size, size)] = low

    def advance(step, w, source):
        older = 1 if step % 2 == 0 else 0
        parts = jnp.dot(dense[w], source, preferred_element_type=jnp.float32)
        parts = parts[:size] + parts[size:]
        product = parts[:, :size] + parts[:, size:]
        newest = jnp.where(kept(w), 2.0 * product - terms[w, older], 0.0)
        terms[w, older] = newest
        gain = coefs_ref[step] * newest
        terms[w, 2] = gain if step == 0 else terms[w, 2] + gain
        if step < STEPS - 1:
            high, low = split(newest)
            into = 1 - step % 2
            at = pl.ds(pl.multiple_of(w * size, size), size)
            pair[into, at, pl.ds(0, size)] = high
            pair[into, at, pl.ds(size, size)] = low

    def first(w, carry):
        h_copy(w).wait()
        densify(w)

        @pl.when(w + STAGES < window)
        def _():
            h_copy(w + STAGES).start()

        advance(0, w, pair[0])
        return carry

    lax.fori_loop(0, window, first, 0)
    for step in range(1, STEPS):

        def later(w, carry, step=step):
            advance(step, w, pair[step % 2])
            if step == STEPS - 1:
                pltpu.make_async_copy(terms.at[w], out_ref.at[row_of(w)], out_sem).start()
            return carry

        lax.fori_loop(0, window, later, 0)
    pltpu.make_async_copy(terms, terms, out_sem).wait()


def unpack_kernel(
    cols_ref, recv_ref, density_ref, out_density, out_last, out_before, gains, total, sems
):
    count = cols_ref.shape[0]
    load = pltpu.make_async_copy(density_ref, total, sems.at[0])
    load.start()
    for k in range(count):
        pltpu.make_async_copy(recv_ref.at[cols_ref[k], 2], gains.at[k], sems.at[1]).start()
    for k in range(count):
        col = cols_ref[k]
        pltpu.make_async_copy(recv_ref.at[col, 0], out_before.at[k], sems.at[2]).start()
        pltpu.make_async_copy(recv_ref.at[col, 1], out_last.at[k], sems.at[3]).start()
    load.wait()
    pltpu.make_async_copy(gains, gains, sems.at[1]).wait()
    total[...] += gains[...]
    store = pltpu.make_async_copy(total, out_density, sems.at[0])
    store.start()
    pltpu.make_async_copy(out_before, out_before, sems.at[2]).wait()
    pltpu.make_async_copy(out_last, out_last, sems.at[3]).wait()
    store.wait()


SMEM = pl.BlockSpec(memory_space=pltpu.SMEM)
ANY = pl.BlockSpec(memory_space=pl.ANY)


def per_device(h_blocks, h_cols, term_prev, term_cur, t_cols, density_in, coefs):
    total = lax.axis_size("row")
    me = lax.axis_index("row")
    count, size = h_blocks.shape[1:3]
    window = total if total <= 2 * REACH + 2 else 2 * REACH + 1
    base = jnp.int32(0) if window == total else jnp.mod(me - REACH, total)
    drop_h = dropped_offset(h_cols, me, total)
    drop_t = dropped_offset(t_cols, me, total)
    block = (size, size)

    h_all = lax.all_gather(h_blocks, "row", axis=0, tiled=True)
    drops = lax.all_gather(jnp.stack([drop_h, drop_t], axis=1), "row", axis=0, tiled=True)
    send = pl.pallas_call(
        functools.partial(pack_kernel, total),
        out_shape=jax.ShapeDtypeStruct((total, 2) + block, jnp.float32),
        in_specs=[SMEM, SMEM, ANY, ANY],
        out_specs=ANY,
        scratch_shapes=[pltpu.VMEM((2,) + block, jnp.float32), pltpu.SemaphoreType.DMA],
        name="pack",
    )(jnp.stack([me, drop_t[0]]), t_cols[0], term_cur[0], term_prev[0])
    columns = lax.all_to_all(send, "row", 0, 0, tiled=True)
    result = pl.pallas_call(
        functools.partial(column_kernel, total, window),
        out_shape=jax.ShapeDtypeStruct((total, 3) + block, jnp.float32),
        in_specs=[SMEM, SMEM, SMEM, ANY, ANY],
        out_specs=ANY,
        scratch_shapes=[
            pltpu.VMEM((STAGES, count) + block, jnp.float32),
            pltpu.VMEM((window, 2 * size, window * size), jnp.bfloat16),
            pltpu.VMEM((2, window * size, 2 * size), jnp.bfloat16),
            pltpu.VMEM((window, 3) + block, jnp.float32),
            pltpu.SemaphoreType.DMA((STAGES,)),
            pltpu.SemaphoreType.DMA,
            pltpu.SemaphoreType.DMA,
        ],
        compiler_params=pltpu.CompilerParams(vmem_limit_bytes=44 * 1024 * 1024),
        name="steps",
    )(drops.reshape(-1), jnp.stack([base, me]), coefs, h_all, columns)
    back = lax.all_to_all(result, "row", 0, 0, tiled=True)
    row_shape = jax.ShapeDtypeStruct((count,) + block, jnp.float32)
    density, last, before = pl.pallas_call(
        unpack_kernel,
        out_shape=(row_shape, row_shape, row_shape),
        in_specs=[SMEM, ANY, ANY],
        out_specs=(ANY, ANY, ANY),
        scratch_shapes=[
            pltpu.VMEM((count,) + block, jnp.float32),
            pltpu.VMEM((count,) + block, jnp.float32),
            pltpu.SemaphoreType.DMA((4,)),
        ],
        name="unpack",
    )(t_cols[0], back, density_in[0])
    return density[None], last[None], before[None]


def solution(mesh):
    blocks = P(("groups", "row"), None, None, None)
    cols = P(("groups", "row"), None)
    return jax.shard_map(
        per_device,
        mesh=mesh,
        in_specs=(blocks, cols, blocks, blocks, cols, blocks, P()),
        out_specs=(blocks, blocks, blocks),
        check_vma=False,
    )
```

```python
import functools

import jax
import jax.numpy as jnp
from jax import lax
from jax.experimental import pallas as pl
from jax.experimental.pallas import tpu as pltpu
from jax.sharding import PartitionSpec as P

REACH = 7
STEPS = 3
NOTE = 8


def place_of(offset, dropped):
    named = jnp.logical_and(offset <= 2 * REACH, offset != dropped)
    slot = offset - jnp.where(offset > dropped, 1, 0)
    return jnp.clip(slot, 0, 2 * REACH - 1), named


def dropped_offset(cols, row, total):
    offsets = jnp.mod(cols - row + REACH, total)
    return REACH * (2 * REACH + 1) - jnp.sum(offsets, axis=1)


def pack_kernel(total, info_ref, cols_ref, cur_ref, prev_ref, send_ref, cur, prev, zeros, note, sems):
    row = info_ref[0]
    drop = info_ref[2]
    count, size = cur.shape[:2]
    loads = (
        pltpu.make_async_copy(cur_ref, cur, sems.at[0]),
        pltpu.make_async_copy(prev_ref, prev, sems.at[1]),
    )
    for load in loads:
        load.start()
    zeros[...] = jnp.zeros_like(zeros)
    line = lax.broadcasted_iota(jnp.int32, note.shape, 0)
    note[...] = jnp.where(line == 0, info_ref[1], drop).astype(jnp.float32)

    def fill(j, carry):
        offset = lax.rem(j - row + REACH + total, total)
        _, named = place_of(offset, drop)
        pltpu.make_async_copy(note, send_ref.at[j, pl.ds(2 * size, NOTE)], sems.at[2]).start()

        @pl.when(jnp.logical_not(named))
        def _():
            pltpu.make_async_copy(zeros, send_ref.at[j, pl.ds(0, 2 * size)], sems.at[2]).start()

        return carry

    lax.fori_loop(0, total, fill, 0)
    for which, held in enumerate((cur, prev)):
        loads[which].wait()
        for k in range(count):
            place = send_ref.at[cols_ref[k], pl.ds(which * size, size)]
            pltpu.make_async_copy(held.at[k], place, sems.at[2]).start()
    pltpu.make_async_copy(send_ref, send_ref, sems.at[2]).wait()


def split(x):
    high = x.astype(jnp.bfloat16)
    low = (x - high.astype(jnp.float32)).astype(jnp.bfloat16)
    return high, low


def column_kernel(
    total, window, group, drops_ref, base_ref, coefs_ref, h_ref, t_ref, out_ref,
    stage, dense, pair, terms, h_sem, t_sem, out_sem,
):
    size = h_ref.shape[-1]
    base = base_ref[0]
    column = base_ref[1]
    groups = window // group

    def row_of(w):
        return lax.rem(base + w, total)

    def h_copy(w):
        slot = lax.rem(w, 2 * group)
        return pltpu.make_async_copy(h_ref.at[row_of(w)], stage.at[slot], h_sem.at[slot])

    def kept(w):
        row = row_of(w)
        offset = lax.rem(column - row + REACH + total, total)
        _, named = place_of(offset, drops_ref[2 * row + 1])
        return named

    for w in range(2 * group):
        h_copy(jnp.int32(w)).start()
    for w in range(window):
        for which in range(2):
            block = t_ref.at[row_of(w), pl.ds(which * size, size)]
            pltpu.make_async_copy(block, terms.at[w, which], t_sem).start()
    pltpu.make_async_copy(terms.at[:, pl.ds(0, 2)], terms.at[:, pl.ds(0, 2)], t_sem).wait()
    for w in range(window):
        high, low = split(jnp.where(kept(w), terms[w, 0], 0.0))
        pair[0, pl.ds(w * size, size), pl.ds(0, size)] = high
        pair[0, pl.ds(w * size, size), pl.ds(size, size)] = low

    def densify(w):
        row = row_of(w)
        drop = drops_ref[2 * row]
        slot = lax.rem(w, 2 * group)
        for p in range(window):
            offset = lax.rem(row_of(p) - row + REACH + total, total)
            k, named = place_of(offset, drop)
            high, low = split(jnp.where(named, stage[slot, k], 0.0))
            dense[w, pl.ds(0, size), pl.ds(p * size, size)] = high
            dense[w, pl.ds(size, size), pl.ds(p * size, size)] = low

    def advance(step, g):
        older = 1 if step % 2 == 0 else 0
        rows = dense[pl.ds(g * group, group)].reshape(group * 2 * size, window * size)
        products = jnp.dot(rows, pair[step % 2], preferred_element_type=jnp.float32)
        for r in range(group):
            w = g * group + r
            parts = products[2 * r * size:(2 * r + 1) * size] + products[(2 * r + 1) * size:(2 * r + 2) * size]
            product = parts[:, :size] + parts[:, size:]
            newest = jnp.where(kept(w), 2.0 * product - terms[w, older], 0.0)
            terms[w, older] = newest
            gain = coefs_ref[step] * newest
            terms[w, 2] = gain if step == 0 else terms[w, 2] + gain
            if step < STEPS - 1:
                high, low = split(newest)
                into = 1 - step % 2
                at = pl.ds(pl.multiple_of(w * size, size), size)
                pair[into, at, pl.ds(0, size)] = high
                pair[into, at, pl.ds(size, size)] = low
            else:
                pltpu.make_async_copy(terms.at[w], out_ref.at[row_of(w)], out_sem).start()

    def first(g, carry):
        for r in range(group):
            w = g * group + r
            h_copy(w).wait()
            densify(w)

            @pl.when(w + 2 * group < window)
            def _():
                h_copy(w + 2 * group).start()

        advance(0, g)
        return carry

    lax.fori_loop(0, groups, first, 0)
    for step in range(1, STEPS):

        def later(g, carry, step=step):
            advance(step, g)
            return carry

        lax.fori_loop(0, groups, later, 0)
    pltpu.make_async_copy(terms, terms, out_sem).wait()


def unpack_kernel(
    cols_ref, recv_ref, density_ref, out_density, out_last, out_before, sums, blocks, sems
):
    count = cols_ref.shape[0]
    load = pltpu.make_async_copy(density_ref, sums, sems.at[3])
    load.start()
    for which in range(3):
        for k in range(count):
            block = recv_ref.at[cols_ref[k], which]
            pltpu.make_async_copy(block, blocks.at[which, k], sems.at[which]).start()

    def arrived(which):
        pltpu.make_async_copy(blocks.at[which], blocks.at[which], sems.at[which]).wait()

    arrived(0)
    before = pltpu.make_async_copy(blocks.at[0], out_before, sems.at[0])
    before.start()
    arrived(1)
    last = pltpu.make_async_copy(blocks.at[1], out_last, sems.at[1])
    last.start()
    load.wait()
    arrived(2)
    sums[...] += blocks[2]
    density = pltpu.make_async_copy(sums, out_density, sems.at[2])
    density.start()
    before.wait()
    last.wait()
    density.wait()


SMEM = pl.BlockSpec(memory_space=pltpu.SMEM)
ANY = pl.BlockSpec(memory_space=pl.ANY)


def per_device(h_blocks, h_cols, term_prev, term_cur, t_cols, density_in, coefs):
    total = lax.axis_size("row")
    me = lax.axis_index("row")
    count, size = h_blocks.shape[1:3]
    window = total if total <= 2 * REACH + 2 else 2 * REACH + 1
    base = jnp.int32(0) if window == total else jnp.mod(me - REACH, total)
    drop_h = dropped_offset(h_cols, me, total)
    drop_t = dropped_offset(t_cols, me, total)
    block = (size, size)

    h_all = lax.all_gather(h_blocks, "row", axis=0, tiled=True)
    send = pl.pallas_call(
        functools.partial(pack_kernel, total),
        out_shape=jax.ShapeDtypeStruct((total, 2 * size + NOTE, size), jnp.float32),
        in_specs=[SMEM, SMEM, ANY, ANY],
        out_specs=ANY,
        scratch_shapes=[
            pltpu.VMEM((count,) + block, jnp.float32),
            pltpu.VMEM((count,) + block, jnp.float32),
            pltpu.VMEM((2 * size, size), jnp.float32),
            pltpu.VMEM((NOTE, size), jnp.float32),
            pltpu.SemaphoreType.DMA((3,)),
        ],
        name="pack",
    )(jnp.stack([me, drop_h[0], drop_t[0]]), t_cols[0], term_cur[0], term_prev[0])
    columns = lax.all_to_all(send, "row", 0, 0, tiled=True)
    drops = columns[:, 2 * size:2 * size + 2, 0].astype(jnp.int32)
    group = max(g for g in (3, 4) if window % g == 0)
    result = pl.pallas_call(
        functools.partial(column_kernel, total, window, group),
        out_shape=jax.ShapeDtypeStruct((total, 3) + block, jnp.float32),
        in_specs=[SMEM, SMEM, SMEM, ANY, ANY],
        out_specs=ANY,
        scratch_shapes=[
            pltpu.VMEM((2 * group, count) + block, jnp.float32),
            pltpu.VMEM((window, 2 * size, window * size), jnp.bfloat16),
            pltpu.VMEM((2, window * size, 2 * size), jnp.bfloat16),
            pltpu.VMEM((window, 3) + block, jnp.float32),
            pltpu.SemaphoreType.DMA((2 * group,)),
            pltpu.SemaphoreType.DMA,
            pltpu.SemaphoreType.DMA,
        ],
        compiler_params=pltpu.CompilerParams(vmem_limit_bytes=48 * 1024 * 1024),
        name="steps",
    )(drops.reshape(-1), jnp.stack([base, me]), coefs, h_all, columns)
    back = lax.all_to_all(result, "row", 0, 0, tiled=True)
    row_shape = jax.ShapeDtypeStruct((count,) + block, jnp.float32)
    density, last, before = pl.pallas_call(
        unpack_kernel,
        out_shape=(row_shape, row_shape, row_shape),
        in_specs=[SMEM, ANY, ANY],
        out_specs=(ANY, ANY, ANY),
        scratch_shapes=[
            pltpu.VMEM((count,) + block, jnp.float32),
            pltpu.VMEM((3, count) + block, jnp.float32),
            pltpu.SemaphoreType.DMA((4,)),
        ],
        name="unpack",
    )(t_cols[0], back, density_in[0])
    return density[None], last[None], before[None]


def solution(mesh):
    blocks = P(("groups", "row"), None, None, None)
    cols = P(("groups", "row"), None)
    return jax.shard_map(
        per_device,
        mesh=mesh,
        in_specs=(blocks, cols, blocks, blocks, cols, blocks, P()),
        out_specs=(blocks, blocks, blocks),
        check_vma=False,
    )
```

```python
import functools

import jax
import jax.numpy as jnp
from jax import lax
from jax.experimental import pallas as pl
from jax.experimental.pallas import tpu as pltpu
from jax.sharding import PartitionSpec as P

REACH = 7
STEPS = 3
NOTE = 8


def cycle_of(total):
    if total != 16:
        return list(range(total))
    chips = [0, 2, 4, 6, 7, 5, 3, 1]
    return [2 * chip + core for chip in chips for core in (0, 1)]


def place_of(offset, dropped):
    named = jnp.logical_and(offset <= 2 * REACH, offset != dropped)
    slot = offset - jnp.where(offset > dropped, 1, 0)
    return jnp.clip(slot, 0, 2 * REACH - 1), named


def dropped_offset(cols, row, total):
    offsets = jnp.mod(cols - row + REACH, total)
    return REACH * (2 * REACH + 1) - jnp.sum(offsets, axis=1)


def pack_kernel(total, info_ref, cols_ref, cur_ref, prev_ref, send_ref, cur, prev, zeros, note, sems):
    row = info_ref[0]
    drop = info_ref[2]
    count, size = cur.shape[:2]
    loads = (
        pltpu.make_async_copy(cur_ref, cur, sems.at[0]),
        pltpu.make_async_copy(prev_ref, prev, sems.at[1]),
    )
    for load in loads:
        load.start()
    zeros[...] = jnp.zeros_like(zeros)
    line = lax.broadcasted_iota(jnp.int32, note.shape, 0)
    note[...] = jnp.where(line == 0, info_ref[1], drop).astype(jnp.float32)

    def fill(j, carry):
        offset = lax.rem(j - row + REACH + total, total)
        _, named = place_of(offset, drop)
        pltpu.make_async_copy(note, send_ref.at[j, pl.ds(2 * size, NOTE)], sems.at[2]).start()

        @pl.when(jnp.logical_not(named))
        def _():
            pltpu.make_async_copy(zeros, send_ref.at[j, pl.ds(0, 2 * size)], sems.at[2]).start()

        return carry

    lax.fori_loop(0, total, fill, 0)
    for which, held in enumerate((cur, prev)):
        loads[which].wait()
        for k in range(count):
            place = send_ref.at[cols_ref[k], pl.ds(which * size, size)]
            pltpu.make_async_copy(held.at[k], place, sems.at[2]).start()
    pltpu.make_async_copy(send_ref, send_ref, sems.at[2]).wait()


def split(x):
    high = x.astype(jnp.bfloat16)
    low = (x - high.astype(jnp.float32)).astype(jnp.bfloat16)
    return high, low


def column_kernel(
    total, window, group, drops_ref, base_ref, place_ref, coefs_ref, h_ref, t_ref, out_ref,
    stage, dense, pair, terms, h_sem, t_sem, out_sem,
):
    size = h_ref.shape[-1]
    base = base_ref[0]
    column = base_ref[1]
    groups = window // group

    def row_of(w):
        return lax.rem(base + w, total)

    def h_copy(w):
        slot = lax.rem(w, 2 * group)
        return pltpu.make_async_copy(h_ref.at[place_ref[row_of(w)]], stage.at[slot], h_sem.at[slot])

    def kept(w):
        row = row_of(w)
        offset = lax.rem(column - row + REACH + total, total)
        _, named = place_of(offset, drops_ref[2 * row + 1])
        return named

    for w in range(2 * group):
        h_copy(jnp.int32(w)).start()
    for w in range(window):
        for which in range(2):
            block = t_ref.at[row_of(w), pl.ds(which * size, size)]
            pltpu.make_async_copy(block, terms.at[w, which], t_sem).start()
    pltpu.make_async_copy(terms.at[:, pl.ds(0, 2)], terms.at[:, pl.ds(0, 2)], t_sem).wait()
    for w in range(window):
        high, low = split(jnp.where(kept(w), terms[w, 0], 0.0))
        pair[0, pl.ds(w * size, size), pl.ds(0, size)] = high
        pair[0, pl.ds(w * size, size), pl.ds(size, size)] = low

    def densify(w):
        row = row_of(w)
        drop = drops_ref[2 * row]
        slot = lax.rem(w, 2 * group)
        for p in range(window):
            offset = lax.rem(row_of(p) - row + REACH + total, total)
            k, named = place_of(offset, drop)
            high, low = split(jnp.where(named, stage[slot, k], 0.0))
            dense[w, pl.ds(0, size), pl.ds(p * size, size)] = high
            dense[w, pl.ds(size, size), pl.ds(p * size, size)] = low

    def advance(step, g):
        older = 1 if step % 2 == 0 else 0
        rows = dense[pl.ds(g * group, group)].reshape(group * 2 * size, window * size)
        products = jnp.dot(rows, pair[step % 2], preferred_element_type=jnp.float32)
        for r in range(group):
            w = g * group + r
            parts = products[2 * r * size:(2 * r + 1) * size] + products[(2 * r + 1) * size:(2 * r + 2) * size]
            product = parts[:, :size] + parts[:, size:]
            newest = jnp.where(kept(w), 2.0 * product - terms[w, older], 0.0)
            terms[w, older] = newest
            gain = coefs_ref[step] * newest
            terms[w, 2] = gain if step == 0 else terms[w, 2] + gain
            if step < STEPS - 1:
                high, low = split(newest)
                into = 1 - step % 2
                at = pl.ds(pl.multiple_of(w * size, size), size)
                pair[into, at, pl.ds(0, size)] = high
                pair[into, at, pl.ds(size, size)] = low
            else:
                pltpu.make_async_copy(terms.at[w], out_ref.at[row_of(w)], out_sem).start()

    def first(g, carry):
        for r in range(group):
            w = g * group + r
            h_copy(w).wait()
            densify(w)

            @pl.when(w + 2 * group < window)
            def _():
                h_copy(w + 2 * group).start()

        advance(0, g)
        return carry

    lax.fori_loop(0, groups, first, 0)
    for step in range(1, STEPS):

        def later(g, carry, step=step):
            advance(step, g)
            return carry

        lax.fori_loop(0, groups, later, 0)
    pltpu.make_async_copy(terms, terms, out_sem).wait()


def unpack_kernel(
    cols_ref, recv_ref, density_ref, out_density, out_last, out_before, sums, blocks, sems
):
    count = cols_ref.shape[0]
    load = pltpu.make_async_copy(density_ref, sums, sems.at[3])
    load.start()
    for which in range(3):
        for k in range(count):
            block = recv_ref.at[cols_ref[k], which]
            pltpu.make_async_copy(block, blocks.at[which, k], sems.at[which]).start()

    def arrived(which):
        pltpu.make_async_copy(blocks.at[which], blocks.at[which], sems.at[which]).wait()

    arrived(0)
    before = pltpu.make_async_copy(blocks.at[0], out_before, sems.at[0])
    before.start()
    arrived(1)
    last = pltpu.make_async_copy(blocks.at[1], out_last, sems.at[1])
    last.start()
    load.wait()
    arrived(2)
    sums[...] += blocks[2]
    density = pltpu.make_async_copy(sums, out_density, sems.at[2])
    density.start()
    before.wait()
    last.wait()
    density.wait()


SMEM = pl.BlockSpec(memory_space=pltpu.SMEM)
ANY = pl.BlockSpec(memory_space=pl.ANY)


def per_device(h_blocks, h_cols, term_prev, term_cur, t_cols, density_in, coefs):
    total = lax.axis_size("row")
    me = lax.axis_index("row")
    count, size = h_blocks.shape[1:3]
    window = total if total <= 2 * REACH + 2 else 2 * REACH + 1
    base = jnp.int32(0) if window == total else jnp.mod(me - REACH, total)
    drop_h = dropped_offset(h_cols, me, total)
    drop_t = dropped_offset(t_cols, me, total)
    block = (size, size)

    cycle = cycle_of(total)
    places = [cycle.index(row) for row in range(total)]
    h_all = lax.all_gather(h_blocks, "row", axis=0, tiled=True, axis_index_groups=[cycle])
    send = pl.pallas_call(
        functools.partial(pack_kernel, total),
        out_shape=jax.ShapeDtypeStruct((total, 2 * size + NOTE, size), jnp.float32),
        in_specs=[SMEM, SMEM, ANY, ANY],
        out_specs=ANY,
        scratch_shapes=[
            pltpu.VMEM((count,) + block, jnp.float32),
            pltpu.VMEM((count,) + block, jnp.float32),
            pltpu.VMEM((2 * size, size), jnp.float32),
            pltpu.VMEM((NOTE, size), jnp.float32),
            pltpu.SemaphoreType.DMA((3,)),
        ],
        name="pack",
    )(jnp.stack([me, drop_h[0], drop_t[0]]), t_cols[0], term_cur[0], term_prev[0])
    columns = lax.all_to_all(send, "row", 0, 0, tiled=True)
    drops = columns[:, 2 * size:2 * size + 2, 0].astype(jnp.int32)
    group = max(g for g in (3, 4) if window % g == 0)
    result = pl.pallas_call(
        functools.partial(column_kernel, total, window, group),
        out_shape=jax.ShapeDtypeStruct((total, 3) + block, jnp.float32),
        in_specs=[SMEM, SMEM, SMEM, SMEM, ANY, ANY],
        out_specs=ANY,
        scratch_shapes=[
            pltpu.VMEM((2 * group, count) + block, jnp.float32),
            pltpu.VMEM((window, 2 * size, window * size), jnp.bfloat16),
            pltpu.VMEM((2, window * size, 2 * size), jnp.bfloat16),
            pltpu.VMEM((window, 3) + block, jnp.float32),
            pltpu.SemaphoreType.DMA((2 * group,)),
            pltpu.SemaphoreType.DMA,
            pltpu.SemaphoreType.DMA,
        ],
        compiler_params=pltpu.CompilerParams(vmem_limit_bytes=48 * 1024 * 1024),
        name="steps",
    )(drops.reshape(-1), jnp.stack([base, me]), jnp.array(places, jnp.int32), coefs, h_all, columns)
    back = lax.all_to_all(result, "row", 0, 0, tiled=True)
    row_shape = jax.ShapeDtypeStruct((count,) + block, jnp.float32)
    density, last, before = pl.pallas_call(
        unpack_kernel,
        out_shape=(row_shape, row_shape, row_shape),
        in_specs=[SMEM, ANY, ANY],
        out_specs=(ANY, ANY, ANY),
        scratch_shapes=[
            pltpu.VMEM((count,) + block, jnp.float32),
            pltpu.VMEM((3, count) + block, jnp.float32),
            pltpu.SemaphoreType.DMA((4,)),
        ],
        name="unpack",
    )(t_cols[0], back, density_in[0])
    return density[None], last[None], before[None]


def solution(mesh):
    blocks = P(("groups", "row"), None, None, None)
    cols = P(("groups", "row"), None)
    return jax.shard_map(
        per_device,
        mesh=mesh,
        in_specs=(blocks, cols, blocks, blocks, cols, blocks, P()),
        out_specs=(blocks, blocks, blocks),
        check_vma=False,
    )
```

```python
import functools

import jax
import jax.numpy as jnp
from jax import lax
from jax.experimental import pallas as pl
from jax.experimental.pallas import tpu as pltpu
from jax.sharding import PartitionSpec as P

REACH = 7
STEPS = 3
NOTE = 8


def permute(x, target):
    devices = lax.axis_size("row")
    return lax.ppermute(x, "row", [(i, target(i)) for i in range(devices)])


def gathered_rows(x, me, total, window):
    if total != 16:
        rows = [x]
        for hop in range(1, REACH + 1):
            rows.insert(0, permute(x, lambda i, hop=hop: (i + hop) % total))
            rows.append(permute(x, lambda i, hop=hop: (i - hop) % total))
        return rows, jnp.mod(me + jnp.arange(-REACH, REACH + 1, dtype=jnp.int32), total)
    rows, indices = [], []
    along, level = x, me
    for hop in range(4):
        if hop:
            along, level = permute(along, lambda i: (i + 4) % 16), jnp.mod(level - 4, 16)
        across = permute(along, lambda i: i ^ 2)
        for row, index in ((along, level), (across, level ^ 2)):
            rows += [row, permute(row, lambda i: i ^ 1)]
            indices += [index, index ^ 1]
    return rows, jnp.stack(indices)


def place_of(offset, dropped):
    named = jnp.logical_and(offset <= 2 * REACH, offset != dropped)
    slot = offset - jnp.where(offset > dropped, 1, 0)
    return jnp.clip(slot, 0, 2 * REACH - 1), named


def dropped_offset(cols, row, total):
    offsets = jnp.mod(cols - row + REACH, total)
    return REACH * (2 * REACH + 1) - jnp.sum(offsets, axis=1)


def pack_kernel(total, info_ref, cols_ref, cur_ref, prev_ref, send_ref, cur, prev, zeros, note, sems):
    row = info_ref[0]
    drop = info_ref[2]
    count, size = cur.shape[:2]
    loads = (
        pltpu.make_async_copy(cur_ref, cur, sems.at[0]),
        pltpu.make_async_copy(prev_ref, prev, sems.at[1]),
    )
    for load in loads:
        load.start()
    zeros[...] = jnp.zeros_like(zeros)
    line = lax.broadcasted_iota(jnp.int32, note.shape, 0)
    note[...] = jnp.where(line == 0, info_ref[1], drop).astype(jnp.float32)

    def fill(j, carry):
        offset = lax.rem(j - row + REACH + total, total)
        _, named = place_of(offset, drop)
        pltpu.make_async_copy(note, send_ref.at[j, pl.ds(2 * size, NOTE)], sems.at[2]).start()

        @pl.when(jnp.logical_not(named))
        def _():
            pltpu.make_async_copy(zeros, send_ref.at[j, pl.ds(0, 2 * size)], sems.at[2]).start()

        return carry

    lax.fori_loop(0, total, fill, 0)
    for which, held in enumerate((cur, prev)):
        loads[which].wait()
        for k in range(count):
            place = send_ref.at[cols_ref[k], pl.ds(which * size, size)]
            pltpu.make_async_copy(held.at[k], place, sems.at[2]).start()
    pltpu.make_async_copy(send_ref, send_ref, sems.at[2]).wait()


def split(x):
    high = x.astype(jnp.bfloat16)
    low = (x - high.astype(jnp.float32)).astype(jnp.bfloat16)
    return high, low


def column_kernel(total, window, group, drops_ref, rows_ref, coefs_ref, *refs):
    h_refs = refs[:window]
    t_ref, out_ref, stage, dense, pair, terms, h_sem, t_sem, out_sem = refs[window:]
    size = t_ref.shape[-1]
    column = rows_ref[window]
    groups = window // group

    def row_of(w):
        return rows_ref[w]

    def kept(w):
        row = row_of(w)
        offset = lax.rem(column - row + REACH + total, total)
        _, named = place_of(offset, drops_ref[2 * row + 1])
        return named

    for w in range(window):
        pltpu.make_async_copy(h_refs[w], stage.at[w], h_sem.at[w]).start()
    for w in range(window):
        for which in range(2):
            block = t_ref.at[row_of(w), pl.ds(which * size, size)]
            pltpu.make_async_copy(block, terms.at[w, which], t_sem).start()
    pltpu.make_async_copy(terms.at[:, pl.ds(0, 2)], terms.at[:, pl.ds(0, 2)], t_sem).wait()
    for w in range(window):
        high, low = split(jnp.where(kept(w), terms[w, 0], 0.0))
        pair[0, pl.ds(w * size, size), pl.ds(0, size)] = high
        pair[0, pl.ds(w * size, size), pl.ds(size, size)] = low

    def densify(w):
        row = row_of(w)
        drop = drops_ref[2 * row]
        for p in range(window):
            offset = lax.rem(row_of(p) - row + REACH + total, total)
            k, named = place_of(offset, drop)
            high, low = split(jnp.where(named, stage[w, k], 0.0))
            dense[w, pl.ds(0, size), pl.ds(p * size, size)] = high
            dense[w, pl.ds(size, size), pl.ds(p * size, size)] = low

    def advance(step, g):
        older = 1 if step % 2 == 0 else 0
        rows = dense[pl.ds(g * group, group)].reshape(group * 2 * size, window * size)
        products = jnp.dot(rows, pair[step % 2], preferred_element_type=jnp.float32)
        for r in range(group):
            w = g * group + r
            parts = products[2 * r * size:(2 * r + 1) * size] + products[(2 * r + 1) * size:(2 * r + 2) * size]
            product = parts[:, :size] + parts[:, size:]
            newest = jnp.where(kept(w), 2.0 * product - terms[w, older], 0.0)
            terms[w, older] = newest
            gain = coefs_ref[step] * newest
            terms[w, 2] = gain if step == 0 else terms[w, 2] + gain
            if step < STEPS - 1:
                high, low = split(newest)
                into = 1 - step % 2
                at = pl.ds(pl.multiple_of(w * size, size), size)
                pair[into, at, pl.ds(0, size)] = high
                pair[into, at, pl.ds(size, size)] = low
            else:
                pltpu.make_async_copy(terms.at[w], out_ref.at[row_of(w)], out_sem).start()

    def first(g, carry):
        for r in range(group):
            w = g * group + r
            pltpu.make_async_copy(stage.at[w], stage.at[w], h_sem.at[w]).wait()
            densify(w)

        advance(0, g)
        return carry

    lax.fori_loop(0, groups, first, 0)
    for step in range(1, STEPS):

        def later(g, carry, step=step):
            advance(step, g)
            return carry

        lax.fori_loop(0, groups, later, 0)
    pltpu.make_async_copy(terms, terms, out_sem).wait()


def unpack_kernel(
    cols_ref, recv_ref, density_ref, out_density, out_last, out_before, sums, blocks, sems
):
    count = cols_ref.shape[0]
    load = pltpu.make_async_copy(density_ref, sums, sems.at[3])
    load.start()
    for which in range(3):
        for k in range(count):
            block = recv_ref.at[cols_ref[k], which]
            pltpu.make_async_copy(block, blocks.at[which, k], sems.at[which]).start()

    def arrived(which):
        pltpu.make_async_copy(blocks.at[which], blocks.at[which], sems.at[which]).wait()

    arrived(0)
    before = pltpu.make_async_copy(blocks.at[0], out_before, sems.at[0])
    before.start()
    arrived(1)
    last = pltpu.make_async_copy(blocks.at[1], out_last, sems.at[1])
    last.start()
    load.wait()
    arrived(2)
    sums[...] += blocks[2]
    density = pltpu.make_async_copy(sums, out_density, sems.at[2])
    density.start()
    before.wait()
    last.wait()
    density.wait()


SMEM = pl.BlockSpec(memory_space=pltpu.SMEM)
ANY = pl.BlockSpec(memory_space=pl.ANY)


def per_device(h_blocks, h_cols, term_prev, term_cur, t_cols, density_in, coefs):
    total = lax.axis_size("row")
    me = lax.axis_index("row")
    count, size = h_blocks.shape[1:3]
    window = total if total <= 2 * REACH + 2 else 2 * REACH + 1
    drop_h = dropped_offset(h_cols, me, total)
    drop_t = dropped_offset(t_cols, me, total)
    block = (size, size)

    h_rows, rows = gathered_rows(h_blocks[0], me, total, window)
    send = pl.pallas_call(
        functools.partial(pack_kernel, total),
        out_shape=jax.ShapeDtypeStruct((total, 2 * size + NOTE, size), jnp.float32),
        in_specs=[SMEM, SMEM, ANY, ANY],
        out_specs=ANY,
        scratch_shapes=[
            pltpu.VMEM((count,) + block, jnp.float32),
            pltpu.VMEM((count,) + block, jnp.float32),
            pltpu.VMEM((2 * size, size), jnp.float32),
            pltpu.VMEM((NOTE, size), jnp.float32),
            pltpu.SemaphoreType.DMA((3,)),
        ],
        name="pack",
    )(jnp.stack([me, drop_h[0], drop_t[0]]), t_cols[0], term_cur[0], term_prev[0])
    columns = lax.all_to_all(send, "row", 0, 0, tiled=True)
    drops = columns[:, 2 * size:2 * size + 2, 0].astype(jnp.int32)
    group = max(g for g in (3, 4) if window % g == 0)
    result = pl.pallas_call(
        functools.partial(column_kernel, total, window, group),
        out_shape=jax.ShapeDtypeStruct((total, 3) + block, jnp.float32),
        in_specs=[SMEM] * 3 + [ANY] * (window + 1),
        out_specs=ANY,
        scratch_shapes=[
            pltpu.VMEM((window, count) + block, jnp.float32),
            pltpu.VMEM((window, 2 * size, window * size), jnp.bfloat16),
            pltpu.VMEM((2, window * size, 2 * size), jnp.bfloat16),
            pltpu.VMEM((window, 3) + block, jnp.float32),
            pltpu.SemaphoreType.DMA((window,)),
            pltpu.SemaphoreType.DMA,
            pltpu.SemaphoreType.DMA,
        ],
        compiler_params=pltpu.CompilerParams(vmem_limit_bytes=50 * 1024 * 1024),
        name="steps",
    )(drops.reshape(-1), jnp.concatenate([rows, me[None]]), coefs, *h_rows, columns)
    back = lax.all_to_all(result, "row", 0, 0, tiled=True)
    row_shape = jax.ShapeDtypeStruct((count,) + block, jnp.float32)
    density, last, before = pl.pallas_call(
        unpack_kernel,
        out_shape=(row_shape, row_shape, row_shape),
        in_specs=[SMEM, ANY, ANY],
        out_specs=(ANY, ANY, ANY),
        scratch_shapes=[
            pltpu.VMEM((count,) + block, jnp.float32),
            pltpu.VMEM((3, count) + block, jnp.float32),
            pltpu.SemaphoreType.DMA((4,)),
        ],
        name="unpack",
    )(t_cols[0], back, density_in[0])
    return density[None], last[None], before[None]


def solution(mesh):
    blocks = P(("groups", "row"), None, None, None)
    cols = P(("groups", "row"), None)
    return jax.shard_map(
        per_device,
        mesh=mesh,
        in_specs=(blocks, cols, blocks, blocks, cols, blocks, P()),
        out_specs=(blocks, blocks, blocks),
        check_vma=False,
    )
```

```python
import functools

import jax
import jax.numpy as jnp
from jax import lax
from jax.experimental import pallas as pl
from jax.experimental.pallas import tpu as pltpu
from jax.sharding import PartitionSpec as P

REACH = 7
STEPS = 3
NOTE = 8
SMEM = pl.BlockSpec(memory_space=pltpu.SMEM)
ANY = pl.BlockSpec(memory_space=pl.ANY)
VMEM_LIMIT = 50 * 1024 * 1024


def permute(x, target):
    devices = lax.axis_size("row")
    return lax.ppermute(x, "row", [(i, target(i)) for i in range(devices)])


def nothing(*refs):
    pass


def after(x, *others):
    return pl.pallas_call(
        nothing,
        out_shape=jax.ShapeDtypeStruct(x.shape, x.dtype),
        in_specs=[ANY] * (1 + len(others)),
        out_specs=ANY,
        input_output_aliases={0: 0},
        name="after",
    )(x, *others)


def gathered_rows(x, me, total):
    if total != 16:
        rows = [x]
        for hop in range(1, REACH + 1):
            rows.insert(0, permute(x, lambda i, hop=hop: (i + hop) % total))
            rows.append(permute(x, lambda i, hop=hop: (i - hop) % total))
        return rows, jnp.mod(me + jnp.arange(-REACH, REACH + 1, dtype=jnp.int32), total), x
    rows, indices = [], []
    along, level = x, me
    for hop in range(4):
        if hop:
            along, level = permute(along, lambda i: (i + 4) % 16), jnp.mod(level - 4, 16)
        across = permute(along, lambda i: i ^ 2)
        for row, index in ((along, level), (across, level ^ 2)):
            rows += [row, permute(row, lambda i: i ^ 1)]
            indices += [index, index ^ 1]
    return rows, jnp.stack(indices), along


def place_of(offset, dropped):
    named = jnp.logical_and(offset <= 2 * REACH, offset != dropped)
    slot = offset - jnp.where(offset > dropped, 1, 0)
    return jnp.clip(slot, 0, 2 * REACH - 1), named


def dropped_offset(cols, row, total):
    offsets = jnp.mod(cols - row + REACH, total)
    return REACH * (2 * REACH + 1) - jnp.sum(offsets, axis=1)


def pack_kernel(total, info_ref, cols_ref, cur_ref, prev_ref, cur_out, prev_out, cur, prev, zeros, note, sems):
    row = info_ref[0]
    drop = info_ref[2]
    count, size = cur.shape[:2]
    loads = (
        pltpu.make_async_copy(cur_ref, cur, sems.at[0]),
        pltpu.make_async_copy(prev_ref, prev, sems.at[1]),
    )
    for load in loads:
        load.start()
    zeros[...] = jnp.zeros_like(zeros)
    line = lax.broadcasted_iota(jnp.int32, note.shape, 0)
    note[...] = jnp.where(line == 0, info_ref[1], drop).astype(jnp.float32)

    def fill(j, carry):
        offset = lax.rem(j - row + REACH + total, total)
        _, named = place_of(offset, drop)
        pltpu.make_async_copy(note, cur_out.at[j, pl.ds(size, NOTE)], sems.at[2]).start()

        @pl.when(jnp.logical_not(named))
        def _():
            pltpu.make_async_copy(zeros, cur_out.at[j, pl.ds(0, size)], sems.at[2]).start()
            pltpu.make_async_copy(zeros, prev_out.at[j], sems.at[3]).start()

        return carry

    lax.fori_loop(0, total, fill, 0)
    loads[0].wait()
    for k in range(count):
        pltpu.make_async_copy(cur.at[k], cur_out.at[cols_ref[k], pl.ds(0, size)], sems.at[2]).start()
    loads[1].wait()
    for k in range(count):
        pltpu.make_async_copy(prev.at[k], prev_out.at[cols_ref[k]], sems.at[3]).start()
    pltpu.make_async_copy(cur_out, cur_out, sems.at[2]).wait()
    pltpu.make_async_copy(prev_out, prev_out, sems.at[3]).wait()


def split(x):
    high = x.astype(jnp.bfloat16)
    low = (x - high.astype(jnp.float32)).astype(jnp.bfloat16)
    return high, low


def kept_rows(total, rows_ref, drops_ref, w):
    row = rows_ref[w]
    offset = lax.rem(rows_ref[rows_ref.shape[0] - 1] - row + REACH + total, total)
    _, named = place_of(offset, drops_ref[2 * row + 1])
    return named


def fill_pair(pair, blocks, kept):
    size = blocks.shape[-1]
    for w in range(blocks.shape[0]):
        high, low = split(jnp.where(kept(w), blocks[w], 0.0))
        pair[pl.ds(w * size, size), pl.ds(0, size)] = high
        pair[pl.ds(w * size, size), pl.ds(size, size)] = low


def products_of(rows, pair, size):
    group = rows.shape[0]
    flat = rows.reshape(group * 2 * size, rows.shape[2])
    products = jnp.dot(flat, pair, preferred_element_type=jnp.float32)
    for r in range(group):
        parts = products[2 * r * size:(2 * r + 1) * size] + products[(2 * r + 1) * size:(2 * r + 2) * size]
        yield parts[:, :size] + parts[:, size:]


def first_kernel(total, window, group, drops_ref, rows_ref, *refs):
    h_refs = refs[:window]
    t_ref, dense_ref, out_ref, stage, dense, blocks, pair, h_sem, t_sem, dense_sem, out_sem = refs[window:]
    size = t_ref.shape[-1]
    kept = functools.partial(kept_rows, total, rows_ref, drops_ref)

    for w in range(window):
        pltpu.make_async_copy(t_ref.at[rows_ref[w], pl.ds(0, size)], blocks.at[w], t_sem).start()
    for w in range(window):
        pltpu.make_async_copy(h_refs[w], stage.at[w], h_sem.at[w]).start()
    pltpu.make_async_copy(blocks, blocks, t_sem).wait()
    fill_pair(pair, blocks, kept)

    def densify(w, slot, r):
        row = rows_ref[w]
        drop = drops_ref[2 * row]
        for p in range(window):
            offset = lax.rem(rows_ref[p] - row + REACH + total, total)
            k, named = place_of(offset, drop)
            high, low = split(jnp.where(named, stage[w, k], 0.0))
            dense[slot, r, pl.ds(0, size), pl.ds(p * size, size)] = high
            dense[slot, r, pl.ds(size, size), pl.ds(p * size, size)] = low

    def store(g, slot):
        return pltpu.make_async_copy(dense.at[slot], dense_ref.at[pl.ds(g * group, group)], dense_sem.at[slot])

    def one(g, carry):
        slot = lax.rem(g, 2)

        @pl.when(g >= 2)
        def _():
            store(g - 2, slot).wait()

        for r in range(group):
            w = g * group + r
            pltpu.make_async_copy(stage.at[w], stage.at[w], h_sem.at[w]).wait()
            densify(w, slot, r)
        store(g, slot).start()
        for r, product in enumerate(products_of(dense[slot], pair[...], size)):
            w = g * group + r
            blocks[w] = 2.0 * product
            pltpu.make_async_copy(blocks.at[w], out_ref.at[rows_ref[w]], out_sem).start()
        return carry

    groups = window // group
    lax.fori_loop(0, groups, one, 0)
    for g in range(groups - 2, groups):
        store(g, g % 2).wait()
    pltpu.make_async_copy(blocks, blocks, out_sem).wait()


def step_kernel(
    total, window, group, drops_ref, rows_ref, dense_ref, cur_ref, prev_ref, out_ref,
    dense, cur, prev, pair, dense_sem, cur_sem, prev_sem, out_sem,
):
    size = cur.shape[-1]
    groups = window // group
    kept = functools.partial(kept_rows, total, rows_ref, drops_ref)
    for w in range(window):
        pltpu.make_async_copy(cur_ref.at[rows_ref[w], pl.ds(0, size)], cur.at[w], cur_sem).start()
    for g in range(groups):
        at = pl.ds(g * group, group)
        pltpu.make_async_copy(dense_ref.at[at], dense.at[at], dense_sem.at[g]).start()
    for w in range(window):
        pltpu.make_async_copy(prev_ref.at[rows_ref[w], pl.ds(0, size)], prev.at[w], prev_sem).start()
    pltpu.make_async_copy(cur, cur, cur_sem).wait()
    fill_pair(pair, cur, kept)
    pltpu.make_async_copy(prev, prev, prev_sem).wait()

    def one(g, carry):
        rows = dense.at[pl.ds(g * group, group)]
        pltpu.make_async_copy(rows, rows, dense_sem.at[g]).wait()
        for r, product in enumerate(products_of(rows[...], pair[...], size)):
            w = g * group + r
            prev[w] = jnp.where(kept(w), 2.0 * product - prev[w], 0.0)
            pltpu.make_async_copy(prev.at[w], out_ref.at[rows_ref[w]], out_sem).start()
        return carry

    lax.fori_loop(0, groups, one, 0)
    pltpu.make_async_copy(prev, prev, out_sem).wait()


def unpack_two_kernel(
    cols_ref, coefs_ref, first_ref, second_ref, density_ref, sum_ref, second_out, sums, one, two, sems
):
    load = pltpu.make_async_copy(density_ref, sums, sems.at[0])
    load.start()
    for k in range(cols_ref.shape[0]):
        pltpu.make_async_copy(first_ref.at[cols_ref[k]], one.at[k], sems.at[1]).start()
        pltpu.make_async_copy(second_ref.at[cols_ref[k]], two.at[k], sems.at[2]).start()
    pltpu.make_async_copy(two, two, sems.at[2]).wait()
    before = pltpu.make_async_copy(two, second_out, sems.at[2])
    before.start()
    load.wait()
    pltpu.make_async_copy(one, one, sems.at[1]).wait()
    sums[...] = sums[...] + coefs_ref[0] * one[...] + coefs_ref[1] * two[...]
    density = pltpu.make_async_copy(sums, sum_ref, sems.at[0])
    density.start()
    before.wait()
    density.wait()


def unpack_last_kernel(cols_ref, coefs_ref, third_ref, sum_ref, density_ref, third_out, sums, three, sems):
    load = pltpu.make_async_copy(sum_ref, sums, sems.at[0])
    load.start()
    for k in range(cols_ref.shape[0]):
        pltpu.make_async_copy(third_ref.at[cols_ref[k]], three.at[k], sems.at[1]).start()
    pltpu.make_async_copy(three, three, sems.at[1]).wait()
    last = pltpu.make_async_copy(three, third_out, sems.at[1])
    last.start()
    load.wait()
    sums[...] += coefs_ref[2] * three[...]
    density = pltpu.make_async_copy(sums, density_ref, sems.at[0])
    density.start()
    last.wait()
    density.wait()


def per_device(h_blocks, h_cols, term_prev, term_cur, t_cols, density_in, coefs):
    total = lax.axis_size("row")
    me = lax.axis_index("row")
    count, size = h_blocks.shape[1:3]
    window = total if total <= 2 * REACH + 2 else 2 * REACH + 1
    group = max(g for g in (3, 4) if window % g == 0)
    drop_h = dropped_offset(h_cols, me, total)
    drop_t = dropped_offset(t_cols, me, total)
    f32 = jnp.float32
    dma = pltpu.SemaphoreType.DMA
    column = jax.ShapeDtypeStruct((total, size, size), f32)
    row = jax.ShapeDtypeStruct((count, size, size), f32)
    row_scratch = pltpu.VMEM(row.shape, f32)
    window_scratch = pltpu.VMEM((window, size, size), f32)
    pair_scratch = pltpu.VMEM((window * size, 2 * size), jnp.bfloat16)
    dense_shape = (window, 2 * size, window * size)
    params = pltpu.CompilerParams(vmem_limit_bytes=VMEM_LIMIT)

    def exchange(x):
        return lax.all_to_all(x, "row", 0, 0, tiled=True)

    send_cur, send_prev = pl.pallas_call(
        functools.partial(pack_kernel, total),
        out_shape=(jax.ShapeDtypeStruct((total, size + NOTE, size), f32), column),
        in_specs=[SMEM, SMEM, ANY, ANY],
        out_specs=(ANY, ANY),
        scratch_shapes=[
            row_scratch,
            row_scratch,
            pltpu.VMEM((size, size), f32),
            pltpu.VMEM((NOTE, size), f32),
            dma((4,)),
        ],
        name="pack",
    )(jnp.stack([me, drop_h[0], drop_t[0]]), t_cols[0], term_cur[0], term_prev[0])

    h_rows, indices, last_hop = gathered_rows(h_blocks[0], me, total)
    rows = jnp.concatenate([indices, me[None]])
    cur = exchange(after(send_cur, last_hop))
    prev = exchange(after(send_prev, cur))
    notes = cur[:, size:size + 2, 0].astype(jnp.int32)
    drops = notes.reshape(-1)
    dense, doubled = pl.pallas_call(
        functools.partial(first_kernel, total, window, group),
        out_shape=(jax.ShapeDtypeStruct(dense_shape, jnp.bfloat16), column),
        in_specs=[SMEM, SMEM] + [ANY] * (window + 1),
        out_specs=(ANY, ANY),
        scratch_shapes=[
            pltpu.VMEM((window, count, size, size), f32),
            pltpu.VMEM((2, group) + dense_shape[1:], jnp.bfloat16),
            window_scratch,
            pair_scratch,
            dma((window,)),
            dma,
            dma((2,)),
            dma,
        ],
        compiler_params=params,
        name="first",
    )(drops, rows, *h_rows, cur)

    offsets = jnp.mod(me - jnp.arange(total, dtype=jnp.int32) + REACH, total)
    _, named = place_of(offsets, notes[:, 1])

    def step(current, previous):
        return pl.pallas_call(
            functools.partial(step_kernel, total, window, group),
            out_shape=column,
            in_specs=[SMEM, SMEM, ANY, ANY, ANY],
            out_specs=ANY,
            scratch_shapes=[
                pltpu.VMEM(dense_shape, jnp.bfloat16),
                window_scratch,
                window_scratch,
                pair_scratch,
                dma((window // group,)),
                dma,
                dma,
                dma,
            ],
            compiler_params=params,
            name="step",
        )(drops, rows, dense, current, previous)

    term1 = jnp.where(named[:, None, None], doubled - prev, 0.0)
    back1 = exchange(term1)
    term2 = step(term1, cur)
    back2 = exchange(term2)
    term3 = step(term2, term1)
    back3 = exchange(term3)
    sums, before = pl.pallas_call(
        unpack_two_kernel,
        out_shape=(row, row),
        in_specs=[SMEM, SMEM, ANY, ANY, ANY],
        out_specs=(ANY, ANY),
        scratch_shapes=[row_scratch, row_scratch, row_scratch, dma((3,))],
        name="unpack_two",
    )(t_cols[0], coefs, back1, back2, density_in[0])
    density, last = pl.pallas_call(
        unpack_last_kernel,
        out_shape=(row, row),
        in_specs=[SMEM, SMEM, ANY, ANY],
        out_specs=(ANY, ANY),
        scratch_shapes=[row_scratch, row_scratch, dma((2,))],
        name="unpack_last",
    )(t_cols[0], coefs, back3, sums)
    return density[None], last[None], before[None]


def solution(mesh):
    blocks = P(("groups", "row"), None, None, None)
    cols = P(("groups", "row"), None)
    return jax.shard_map(
        per_device,
        mesh=mesh,
        in_specs=(blocks, cols, blocks, blocks, cols, blocks, P()),
        out_specs=(blocks, blocks, blocks),
        check_vma=False,
    )
```

```python
import functools

import jax
import jax.numpy as jnp
from jax import lax
from jax.experimental import pallas as pl
from jax.experimental.pallas import tpu as pltpu
from jax.sharding import PartitionSpec as P

REACH = 7
WINDOW = 2 * REACH + 1
GROUP = 5
NOTE = 8
SMEM = pl.BlockSpec(memory_space=pltpu.SMEM)
ANY = pl.BlockSpec(memory_space=pl.ANY)
VMEM_LIMIT = 50 * 1024 * 1024


def cycle_of(total):
    if total != 16:
        return list(range(total))
    chips = [0, 2, 4, 6, 7, 5, 3, 1]
    return [2 * chip + core for chip in chips for core in (0, 1)]


def shifted(x, by):
    devices = lax.axis_size("row")
    if by == 0:
        return x
    return lax.ppermute(x, "row", [(i, (i + by) % devices) for i in range(devices)])


def place_of(offset, dropped):
    named = jnp.logical_and(offset < WINDOW, offset != dropped)
    slot = offset - jnp.where(offset > dropped, 1, 0)
    return jnp.clip(slot, 0, WINDOW - 2), named


def dropped_offset(cols, row, total):
    offsets = jnp.mod(cols - row + REACH, total)
    return REACH * WINDOW - jnp.sum(offsets)


def pack_kernel(drops_ref, cur_ref, prev_ref, *refs):
    outs = refs[:WINDOW]
    cur, prev, zeros, note, sems = refs[WINDOW:]
    size = cur.shape[1]
    loads = (
        pltpu.make_async_copy(cur_ref, cur, sems.at[0]),
        pltpu.make_async_copy(prev_ref, prev, sems.at[1]),
    )
    for load in loads:
        load.start()
    drop = drops_ref[1]
    zeros[...] = jnp.zeros_like(zeros)
    line = lax.broadcasted_iota(jnp.int32, note.shape, 0)
    note[...] = jnp.where(line == 0, drops_ref[0], drop).astype(jnp.float32)
    for offset in range(WINDOW):
        pltpu.make_async_copy(note, outs[offset].at[pl.ds(2 * size, NOTE)], sems.at[2]).start()
    for which, held in enumerate((cur, prev)):
        loads[which].wait()
        for offset in range(WINDOW):
            slot, named = place_of(jnp.int32(offset), drop)
            place = outs[offset].at[pl.ds(which * size, size)]

            @pl.when(named)
            def _(slot=slot, place=place, held=held):
                pltpu.make_async_copy(held.at[slot], place, sems.at[2]).start()

            @pl.when(jnp.logical_not(named))
            def _(place=place):
                pltpu.make_async_copy(zeros, place, sems.at[2]).start()

    for out in outs:
        pltpu.make_async_copy(out, out, sems.at[2]).wait()


def split(x):
    high = x.astype(jnp.bfloat16)
    low = (x - high.astype(jnp.float32)).astype(jnp.bfloat16)
    return high, low


def kept(drops_ref, w):
    return 2 * REACH - w != drops_ref[2 * w + 1]


def fill_pair(pair, block, w):
    size = block.shape[-1]
    high, low = split(block)
    at = pl.ds(pl.multiple_of(w * size, size), size)
    pair[at, pl.ds(0, size)] = high
    pair[at, pl.ds(size, size)] = low


def products_of(rows, pair):
    group, double = rows.shape[:2]
    size = double // 2
    products = jnp.dot(rows.reshape(group * double, rows.shape[2]), pair, preferred_element_type=jnp.float32)
    for r in range(group):
        parts = products[r * double:r * double + size] + products[r * double + size:(r + 1) * double]
        yield parts[:, :size] + parts[:, size:]


def first_kernel(total, drops_ref, places_ref, h_ref, *refs):
    t_refs = refs[:WINDOW]
    dense_ref = refs[WINDOW]
    outs = refs[WINDOW + 1:2 * WINDOW + 1]
    stage, dense, blocks, pair, h_sem, t_sem, dense_sem, out_sem = refs[2 * WINDOW + 1:]
    size = h_ref.shape[-1]

    for w in range(WINDOW):
        for which in range(2):
            pltpu.make_async_copy(t_refs[w].at[pl.ds(which * size, size)], blocks.at[which, w], t_sem).start()
    for w in range(WINDOW):
        pltpu.make_async_copy(h_ref.at[places_ref[w]], stage.at[w], h_sem.at[w]).start()
    pltpu.make_async_copy(blocks, blocks, t_sem).wait()
    for w in range(WINDOW):
        fill_pair(pair, jnp.where(kept(drops_ref, w), blocks[0, w], 0.0), w)

    def densify(w, slot, r):
        drop = drops_ref[2 * w]
        for p in range(WINDOW):
            k, named = place_of(lax.rem(p - w + REACH + total, total), drop)
            high, low = split(jnp.where(named, stage[w, k], 0.0))
            dense[slot, r, pl.ds(0, size), pl.ds(p * size, size)] = high
            dense[slot, r, pl.ds(size, size), pl.ds(p * size, size)] = low

    def store(g, slot):
        return pltpu.make_async_copy(dense.at[slot], dense_ref.at[pl.ds(g * GROUP, GROUP)], dense_sem.at[slot])

    def one(g, carry):
        slot = lax.rem(g, 2)

        @pl.when(g >= 2)
        def _():
            store(g - 2, slot).wait()

        for r in range(GROUP):
            w = g * GROUP + r
            pltpu.make_async_copy(stage.at[w], stage.at[w], h_sem.at[w]).wait()
            densify(w, slot, r)
        store(g, slot).start()
        for r, product in enumerate(products_of(dense[slot], pair[...])):
            w = g * GROUP + r
            blocks[1, w] = jnp.where(kept(drops_ref, w), 2.0 * product - blocks[1, w], 0.0)
        return carry

    groups = WINDOW // GROUP
    lax.fori_loop(0, groups, one, 0)
    for w in range(WINDOW):
        pltpu.make_async_copy(blocks.at[1, w], outs[w], out_sem).start()
    for g in range(groups - 2, groups):
        store(g, g % 2).wait()
    pltpu.make_async_copy(blocks.at[1], blocks.at[1], out_sem).wait()


def later_kernel(drops_ref, dense_ref, *refs):
    t_refs = refs[:WINDOW]
    first_refs = refs[WINDOW:2 * WINDOW]
    outs = refs[2 * WINDOW:3 * WINDOW]
    dense, terms, pairs, dense_sem, t_sem, first_sem, out_sem = refs[3 * WINDOW:]
    size = terms.shape[-1]
    groups = WINDOW // GROUP
    for w in range(WINDOW):
        pltpu.make_async_copy(first_refs[w], terms.at[1, w], first_sem).start()
    for g in range(groups):
        at = pl.ds(g * GROUP, GROUP)
        pltpu.make_async_copy(dense_ref.at[at], dense.at[at], dense_sem.at[g]).start()
    for w in range(WINDOW):
        pltpu.make_async_copy(t_refs[w].at[pl.ds(0, size)], terms.at[0, w], t_sem).start()
    pltpu.make_async_copy(terms.at[1], terms.at[1], first_sem).wait()
    for w in range(WINDOW):
        fill_pair(pairs.at[0], terms[1, w], w)
    pltpu.make_async_copy(terms.at[0], terms.at[0], t_sem).wait()

    def one(g, carry, step):
        rows = dense.at[pl.ds(g * GROUP, GROUP)]
        if step == 0:
            pltpu.make_async_copy(rows, rows, dense_sem.at[g]).wait()
        for r, product in enumerate(products_of(rows[...], pairs[step])):
            w = g * GROUP + r
            newest = jnp.where(kept(drops_ref, w), 2.0 * product - terms[step, w], 0.0)
            terms[step, w] = newest
            if step == 0:
                fill_pair(pairs.at[1], newest, w)
        return carry

    for step in range(2):
        lax.fori_loop(0, groups, functools.partial(one, step=step), 0)
        for w in range(WINDOW):
            pltpu.make_async_copy(terms.at[step, w], outs[w].at[pl.ds(step * size, size)], out_sem).start()
    pltpu.make_async_copy(terms, terms, out_sem).wait()


def collect(drops_ref, held_refs, place, sem, rows=None):
    for k in range(place.shape[0]):
        for skipped in (0, 1):
            held = held_refs[2 * REACH - k - skipped]
            source = held if rows is None else held.at[rows]

            @pl.when((k >= drops_ref[1]) == bool(skipped))
            def _(source=source, k=k):
                pltpu.make_async_copy(source, place.at[k], sem).start()


def unpack_first_kernel(drops_ref, coefs_ref, density_ref, *refs):
    held = refs[:WINDOW]
    out_ref, sums, one, sems = refs[WINDOW:]
    load = pltpu.make_async_copy(density_ref, sums, sems.at[0])
    load.start()
    collect(drops_ref, held, one, sems.at[1])
    load.wait()
    pltpu.make_async_copy(one, one, sems.at[1]).wait()
    sums[...] += coefs_ref[0] * one[...]
    store = pltpu.make_async_copy(sums, out_ref, sems.at[0])
    store.start()
    store.wait()


def unpack_last_kernel(drops_ref, coefs_ref, sum_ref, *refs):
    held = refs[:WINDOW]
    density_ref, last_ref, before_ref, sums, two, three, sems = refs[WINDOW:]
    size = two.shape[-1]
    load = pltpu.make_async_copy(sum_ref, sums, sems.at[0])
    load.start()
    collect(drops_ref, held, two, sems.at[1], pl.ds(0, size))
    collect(drops_ref, held, three, sems.at[2], pl.ds(size, size))
    pltpu.make_async_copy(two, two, sems.at[1]).wait()
    before = pltpu.make_async_copy(two, before_ref, sems.at[1])
    before.start()
    pltpu.make_async_copy(three, three, sems.at[2]).wait()
    last = pltpu.make_async_copy(three, last_ref, sems.at[2])
    last.start()
    load.wait()
    sums[...] = sums[...] + coefs_ref[1] * two[...] + coefs_ref[2] * three[...]
    store = pltpu.make_async_copy(sums, density_ref, sems.at[0])
    store.start()
    before.wait()
    last.wait()
    store.wait()


def per_device(h_blocks, h_cols, term_prev, term_cur, t_cols, density_in, coefs):
    total = lax.axis_size("row")
    me = lax.axis_index("row")
    count, size = h_blocks.shape[1:3]
    own = jnp.stack([dropped_offset(h_cols, me, total), dropped_offset(t_cols, me, total)])
    f32, bf16 = jnp.float32, jnp.bfloat16
    dma = pltpu.SemaphoreType.DMA
    params = pltpu.CompilerParams(vmem_limit_bytes=VMEM_LIMIT)
    row = jax.ShapeDtypeStruct((count, size, size), f32)
    row_scratch = pltpu.VMEM(row.shape, f32)
    dense = jax.ShapeDtypeStruct((WINDOW, 2 * size, WINDOW * size), bf16)
    pair_shape = (WINDOW * size, 2 * size)
    terms_scratch = pltpu.VMEM((2, WINDOW, size, size), f32)
    groups = WINDOW // GROUP

    def call(kernel, smem, arrays, outs, scratch, name):
        return pl.pallas_call(
            kernel,
            out_shape=outs,
            in_specs=[SMEM] * len(smem) + [ANY] * len(arrays),
            out_specs=[ANY] * len(outs),
            scratch_shapes=scratch,
            compiler_params=params,
            name=name,
        )(*smem, *arrays)

    cycle = cycle_of(total)
    places = [cycle.index(place) for place in range(total)]
    h_all = lax.all_gather(h_blocks, "row", axis=0, tiled=True, axis_index_groups=[cycle])
    window = jnp.mod(me + jnp.arange(-REACH, REACH + 1, dtype=jnp.int32), total)
    window = jnp.array(places, jnp.int32)[window]

    message = jax.ShapeDtypeStruct((2 * size + NOTE, size), f32)
    sent = call(
        pack_kernel,
        [own],
        [term_cur[0], term_prev[0]],
        [message] * WINDOW,
        [row_scratch, row_scratch, pltpu.VMEM((size, size), f32), pltpu.VMEM((NOTE, size), f32), dma((3,))],
        "pack",
    )
    column = [shifted(sent[offset], offset - REACH) for offset in reversed(range(WINDOW))]
    drops = jnp.concatenate([part[2 * size:2 * size + 2, 0] for part in column]).astype(jnp.int32)
    dense_rows, *term1 = call(
        functools.partial(first_kernel, total),
        [drops, window],
        [h_all, *column],
        [dense] + [jax.ShapeDtypeStruct((size, size), f32)] * WINDOW,
        [
            pltpu.VMEM((WINDOW, count, size, size), f32),
            pltpu.VMEM((2, GROUP) + dense.shape[1:], bf16),
            terms_scratch,
            pltpu.VMEM(pair_shape, bf16),
            dma((WINDOW,)),
            dma,
            dma((2,)),
            dma,
        ],
        "first",
    )
    back1 = [shifted(term1[w], w - REACH) for w in range(WINDOW)]
    terms = call(
        later_kernel,
        [drops],
        [dense_rows, *column, *term1],
        [jax.ShapeDtypeStruct((2 * size, size), f32)] * WINDOW,
        [
            pltpu.VMEM(dense.shape, bf16),
            terms_scratch,
            pltpu.VMEM((2,) + pair_shape, bf16),
            dma((groups,)),
            dma,
            dma,
            dma,
        ],
        "later",
    )
    back = [shifted(terms[w], w - REACH) for w in range(WINDOW)]
    (sums,) = call(
        unpack_first_kernel,
        [own, coefs],
        [density_in[0], *back1],
        [row],
        [row_scratch, row_scratch, dma((2,))],
        "unpack_first",
    )
    density, last, before = call(
        unpack_last_kernel,
        [own, coefs],
        [sums, *back],
        [row] * 3,
        [row_scratch, row_scratch, row_scratch, dma((3,))],
        "unpack_last",
    )
    return density[None], last[None], before[None]


def solution(mesh):
    blocks = P(("groups", "row"), None, None, None)
    cols = P(("groups", "row"), None)
    return jax.shard_map(
        per_device,
        mesh=mesh,
        in_specs=(blocks, cols, blocks, blocks, cols, blocks, P()),
        out_specs=(blocks, blocks, blocks),
        check_vma=False,
    )
```

```python
import functools

import jax
import jax.numpy as jnp
from jax import lax
from jax.experimental import pallas as pl
from jax.experimental.pallas import tpu as pltpu
from jax.sharding import PartitionSpec as P

REACH = 7
NOTE = 8
SMEM = pl.BlockSpec(memory_space=pltpu.SMEM)
ANY = pl.BlockSpec(memory_space=pl.ANY)


def permute(x, target):
    devices = lax.axis_size("row")
    return lax.ppermute(x, "row", [(i, target(i)) for i in range(devices)])


def after(x, *others):
    return lax.optimization_barrier((x, *others))[0]


RING = (0, 2, 4, 6, 7, 5, 3, 1)


def along_ring(device, by):
    return 2 * RING[(RING.index(device // 2) + by) % len(RING)] + device % 2


def window_rows(me, total):
    if total != 16:
        steps = [0] + [by for hop in range(1, REACH + 1) for by in (-hop, hop)]
        return jnp.mod(me + jnp.array(steps, jnp.int32), total), (5, 4, 4, 2)
    order = (0, -1, 1, -2, 2, -3, 3, 4)
    table = [[along_ring(i, by) ^ core for by in order for core in (0, 1)] for i in range(total)]
    return jnp.array(table, jnp.int32)[me], (6, 4, 4, 2)


def gathered_rows(x, me, total, beside):
    if total != 16:
        rows = [x]
        for hop in range(1, REACH + 1):
            for by in (hop, -hop):
                rows.append(permute(x, lambda i, by=by: (i + by) % total))
        for start, end in ((0, 5), (5, 9), (9, 13), (13, 15)):
            yield rows[start:end]
        return

    def other_core(row):
        return permute(row, lambda i: i ^ 1)

    def round_of(ahead, behind):
        ahead = permute(ahead, lambda i: along_ring(i, 1))
        behind = permute(behind, lambda i: along_ring(i, -1))
        return ahead, behind, [ahead, other_core(ahead), behind, other_core(behind)]

    rows = [x, other_core(x)]
    ahead, behind, first = round_of(x, x)
    ahead, behind, second = round_of(ahead, behind)
    yield rows + first
    beside = (beside, rows[1], first[1], first[3])
    ahead, behind, third = round_of(after(ahead, *beside), after(behind, *beside))
    made = yield second
    ahead, behind = after(ahead, made), after(behind, made)
    far = permute(jnp.where(me % 2 == 0, ahead, behind), lambda i: along_ring(i, 1 if i % 2 == 0 else -1))
    made = yield third
    far = after(far, made)
    yield [far, other_core(far)]


def place_of(offset, dropped):
    named = jnp.logical_and(offset <= 2 * REACH, offset != dropped)
    slot = offset - jnp.where(offset > dropped, 1, 0)
    return jnp.clip(slot, 0, 2 * REACH - 1), named


def dropped_offset(cols, row, total):
    offsets = jnp.mod(cols - row + REACH, total)
    return REACH * (2 * REACH + 1) - jnp.sum(offsets, axis=1)


def pack_kernel(total, info_ref, cols_ref, cur_ref, prev_ref, send_ref, cur, prev, zeros, note, sems):
    row = info_ref[0]
    drop = info_ref[2]
    count, size = cur.shape[:2]
    loads = (
        pltpu.make_async_copy(cur_ref, cur, sems.at[0]),
        pltpu.make_async_copy(prev_ref, prev, sems.at[1]),
    )
    for load in loads:
        load.start()
    zeros[...] = jnp.zeros_like(zeros)
    line = lax.broadcasted_iota(jnp.int32, note.shape, 0)
    note[...] = jnp.where(line == 0, info_ref[1], drop).astype(jnp.float32)

    def fill(j, carry):
        offset = lax.rem(j - row + REACH + total, total)
        _, named = place_of(offset, drop)
        pltpu.make_async_copy(note, send_ref.at[j, pl.ds(2 * size, NOTE)], sems.at[2]).start()

        @pl.when(jnp.logical_not(named))
        def _():
            pltpu.make_async_copy(zeros, send_ref.at[j, pl.ds(0, 2 * size)], sems.at[2]).start()

        return carry

    lax.fori_loop(0, total, fill, 0)
    for which, held in enumerate((cur, prev)):
        loads[which].wait()
        for k in range(count):
            place = send_ref.at[cols_ref[k], pl.ds(which * size, size)]
            pltpu.make_async_copy(held.at[k], place, sems.at[2]).start()
    pltpu.make_async_copy(send_ref, send_ref, sems.at[2]).wait()


def split(x):
    high = x.astype(jnp.bfloat16)
    low = (x - high.astype(jnp.float32)).astype(jnp.bfloat16)
    return high, low


def kept_rows(total, rows_ref, drops_ref, w):
    row = rows_ref[w]
    offset = lax.rem(rows_ref[rows_ref.shape[0] - 1] - row + REACH + total, total)
    _, named = place_of(offset, drops_ref[2 * row + 1])
    return named


def fill_pair(pair, block, w):
    size = block.shape[-1]
    high, low = split(block)
    at = pl.ds(pl.multiple_of(w * size, size), size)
    pair[at, pl.ds(0, size)] = high
    pair[at, pl.ds(size, size)] = low


def products_of(rows, pair):
    group, double = rows.shape[:2]
    size = double // 2
    products = jnp.dot(rows.reshape(group * double, rows.shape[2]), pair, preferred_element_type=jnp.float32)
    for r in range(group):
        parts = products[r * double:r * double + size] + products[r * double + size:(r + 1) * double]
        yield parts[:, :size] + parts[:, size:]


def first_kernel(total, window, start, count, group, drops_ref, rows_ref, t_ref, *refs):
    h_refs = refs[:count]
    if start:
        pair_in, _ = refs[count:count + 2]
        dense_ref, out_ref = refs[count + 2:count + 4]
    else:
        dense_ref, out_ref, pair_out, blocks = refs[count:count + 4]
    stage, dense, prev, pair, h_sem, t_sem, prev_sem, pair_sem, dense_sem, out_sem = refs[-10:]
    size = t_ref.shape[-1]
    kept = functools.partial(kept_rows, total, rows_ref, drops_ref)

    if start:
        pltpu.make_async_copy(pair_in, pair, pair_sem).start()
    else:
        for w in range(window):
            pltpu.make_async_copy(t_ref.at[rows_ref[w], pl.ds(0, size)], blocks.at[w], t_sem).start()
    for r in range(count):
        pltpu.make_async_copy(h_refs[r], stage.at[r], h_sem.at[r]).start()
    for r in range(count):
        block = t_ref.at[rows_ref[start + r], pl.ds(size, size)]
        pltpu.make_async_copy(block, prev.at[r], prev_sem).start()
    if not start:
        pltpu.make_async_copy(blocks, blocks, t_sem).wait()
        for w in range(window):
            fill_pair(pair, jnp.where(kept(w), blocks[w], 0.0), w)
        pltpu.make_async_copy(pair, pair_out, pair_sem).start()

    def densify(r, slot, place):
        row = rows_ref[start + r]
        drop = drops_ref[2 * row]
        for p in range(window):
            offset = lax.rem(rows_ref[p] - row + REACH + total, total)
            k, named = place_of(offset, drop)
            high, low = split(jnp.where(named, stage[r, k], 0.0))
            dense[slot, place, pl.ds(0, size), pl.ds(p * size, size)] = high
            dense[slot, place, pl.ds(size, size), pl.ds(p * size, size)] = low

    def store(g, slot):
        return pltpu.make_async_copy(dense.at[slot], dense_ref.at[pl.ds(g * group, group)], dense_sem.at[slot])

    groups = count // group

    def one(g, carry):
        slot = lax.rem(g, 2)

        @pl.when(g >= 2)
        def _():
            store(g - 2, slot).wait()

        for place in range(group):
            r = g * group + place
            pltpu.make_async_copy(stage.at[r], stage.at[r], h_sem.at[r]).wait()
            densify(r, slot, place)
        store(g, slot).start()
        if start:

            @pl.when(g == 0)
            def _():
                pltpu.make_async_copy(pair, pair, pair_sem).wait()

        @pl.when(g == 0)
        def _():
            pltpu.make_async_copy(prev, prev, prev_sem).wait()

        for place, product in enumerate(products_of(dense[slot], pair[...])):
            r = g * group + place
            prev[r] = jnp.where(kept(start + r), 2.0 * product - prev[r], 0.0)
            pltpu.make_async_copy(prev.at[r], out_ref.at[rows_ref[start + r]], out_sem).start()
        return carry

    lax.fori_loop(0, groups, one, 0)
    for g in range(max(groups - 2, 0), groups):
        store(g, g % 2).wait()
    if not start:
        pltpu.make_async_copy(pair, pair, pair_sem).wait()
    pltpu.make_async_copy(prev, prev, out_sem).wait()


def later_kernel(total, window, group, parts, drops_ref, rows_ref, *refs):
    dense_refs = refs[:len(parts)]
    t_ref, first_ref, out_ref, dense, terms, pairs, dense_sem, t_sem, first_sem, out_sem = refs[len(parts):]
    size = terms.shape[-1]
    groups = window // group
    kept = functools.partial(kept_rows, total, rows_ref, drops_ref)
    for w in range(window):
        pltpu.make_async_copy(first_ref.at[rows_ref[w]], terms.at[w, 1], first_sem).start()
    start = 0
    for part, dense_ref in zip(parts, dense_refs):
        for w in range(start, start + part):
            pltpu.make_async_copy(dense_ref.at[w - start], dense.at[w], dense_sem.at[w // group]).start()
        start += part
    for w in range(window):
        pltpu.make_async_copy(t_ref.at[rows_ref[w], pl.ds(0, size)], terms.at[w, 0], t_sem).start()
    pltpu.make_async_copy(terms.at[:, 1], terms.at[:, 1], first_sem).wait()
    for w in range(window):
        fill_pair(pairs.at[0], terms[w, 1], w)
    pltpu.make_async_copy(terms.at[:, 0], terms.at[:, 0], t_sem).wait()

    def one(g, carry, step):
        rows = dense.at[pl.ds(g * group, group)]
        if step == 0:
            pltpu.make_async_copy(rows, rows, dense_sem.at[g]).wait()
        for r, product in enumerate(products_of(rows[...], pairs[step])):
            w = g * group + r
            newest = jnp.where(kept(w), 2.0 * product - terms[w, step], 0.0)
            terms[w, step] = newest
            if step == 0:
                fill_pair(pairs.at[1], newest, w)
            pltpu.make_async_copy(terms.at[w, step], out_ref.at[rows_ref[w], step], out_sem).start()
        return carry

    for step in range(2):
        lax.fori_loop(0, groups, functools.partial(one, step=step), 0)
    pltpu.make_async_copy(terms, terms, out_sem).wait()


def unpack_first_kernel(cols_ref, coefs_ref, first_ref, density_ref, out_ref, sums, one, sems):
    load = pltpu.make_async_copy(density_ref, sums, sems.at[0])
    load.start()
    for k in range(cols_ref.shape[0]):
        pltpu.make_async_copy(first_ref.at[cols_ref[k]], one.at[k], sems.at[1]).start()
    load.wait()
    pltpu.make_async_copy(one, one, sems.at[1]).wait()
    sums[...] += coefs_ref[0] * one[...]
    store = pltpu.make_async_copy(sums, out_ref, sems.at[0])
    store.start()
    store.wait()


def unpack_last_kernel(cols_ref, coefs_ref, held_ref, sum_ref, density_ref, last_ref, before_ref, sums, two, three, sems):
    load = pltpu.make_async_copy(sum_ref, sums, sems.at[0])
    load.start()
    for place, sem, which in ((two, 1, 0), (three, 2, 1)):
        for k in range(cols_ref.shape[0]):
            pltpu.make_async_copy(held_ref.at[cols_ref[k], which], place.at[k], sems.at[sem]).start()
    pltpu.make_async_copy(two, two, sems.at[1]).wait()
    before = pltpu.make_async_copy(two, before_ref, sems.at[1])
    before.start()
    pltpu.make_async_copy(three, three, sems.at[2]).wait()
    last = pltpu.make_async_copy(three, last_ref, sems.at[2])
    last.start()
    load.wait()
    sums[...] = sums[...] + coefs_ref[1] * two[...] + coefs_ref[2] * three[...]
    store = pltpu.make_async_copy(sums, density_ref, sems.at[0])
    store.start()
    before.wait()
    last.wait()
    store.wait()


def per_device(h_blocks, h_cols, term_prev, term_cur, t_cols, density_in, coefs):
    total = lax.axis_size("row")
    me = lax.axis_index("row")
    count, size = h_blocks.shape[1:3]
    drop_h = dropped_offset(h_cols, me, total)
    drop_t = dropped_offset(t_cols, me, total)
    f32, bf16 = jnp.float32, jnp.bfloat16
    dma = pltpu.SemaphoreType.DMA
    row = jax.ShapeDtypeStruct((count, size, size), f32)
    row_scratch = pltpu.VMEM(row.shape, f32)

    def call(kernel, smem, arrays, outs, scratch, name, megabytes, aliases={}):
        return pl.pallas_call(
            kernel,
            out_shape=outs,
            in_specs=[SMEM] * len(smem) + [ANY] * len(arrays),
            out_specs=[ANY] * len(outs),
            scratch_shapes=scratch,
            input_output_aliases=aliases,
            compiler_params=pltpu.CompilerParams(vmem_limit_bytes=megabytes * 1024 * 1024),
            name=name,
        )(*smem, *arrays)

    def exchange(x):
        return lax.all_to_all(x, "row", 0, 0, tiled=True)

    (send,) = call(
        functools.partial(pack_kernel, total),
        [jnp.stack([me, drop_h[0], drop_t[0]]), t_cols[0]],
        [term_cur[0], term_prev[0]],
        [jax.ShapeDtypeStruct((total, 2 * size + NOTE, size), f32)],
        [
            row_scratch,
            row_scratch,
            pltpu.VMEM((2 * size, size), f32),
            pltpu.VMEM((NOTE, size), f32),
            dma((3,)),
        ],
        "pack",
        12,
    )
    column = exchange(send)
    drops = column[:, 2 * size:2 * size + 2, 0].astype(jnp.int32).reshape(-1)
    indices, parts = window_rows(me, total)
    gathered = gathered_rows(h_blocks[0], me, total, column)
    rows = jnp.concatenate([indices, me[None]])
    window = sum(parts)
    dense_shape = (window, 2 * size, window * size)
    pair_shape = (window * size, 2 * size)
    dense = []
    start = 0
    for part in parts:
        h_rows = gathered.send(dense[-1] if start else None)
        group = max(g for g in (2, 3, 4, 5) if part % g == 0)
        scratch = [
            pltpu.VMEM((part, count, size, size), f32),
            pltpu.VMEM((2, group) + dense_shape[1:], bf16),
            pltpu.VMEM((part, size, size), f32),
            pltpu.VMEM(pair_shape, bf16),
            dma((part,)),
            dma,
            dma,
            dma,
            dma((2,)),
            dma,
        ]
        if not start:
            scratch = [pltpu.VMEM((window, size, size), f32)] + scratch
        result = call(
            functools.partial(first_kernel, total, window, start, part, group),
            [drops, rows],
            [column, *h_rows] + ([pair, term1] if start else []),
            [
                jax.ShapeDtypeStruct((part,) + dense_shape[1:], bf16),
                jax.ShapeDtypeStruct((total, size, size), f32),
            ] + ([] if start else [jax.ShapeDtypeStruct(pair_shape, bf16)]),
            scratch,
            "first",
            29,
            {part + 4: 1} if start else {},
        )
        dense.append(result[0])
        term1 = result[1]
        if not start:
            pair = result[2]
        start += part
    back1 = exchange(term1)
    group = max(g for g in (3, 4) if window % g == 0)
    (terms,) = call(
        functools.partial(later_kernel, total, window, group, parts),
        [drops, rows],
        [*dense, column, term1],
        [jax.ShapeDtypeStruct((total, 2, size, size), f32)],
        [
            pltpu.VMEM(dense_shape, bf16),
            pltpu.VMEM((window, 2, size, size), f32),
            pltpu.VMEM((2,) + pair_shape, bf16),
            dma((window // group,)),
            dma,
            dma,
            dma,
        ],
        "later",
        28,
    )
    back = exchange(after(terms, back1))
    (sums,) = call(
        unpack_first_kernel,
        [t_cols[0], coefs],
        [back1, density_in[0]],
        [row],
        [row_scratch, row_scratch, dma((2,))],
        "unpack_first",
        12,
    )
    density, last, before = call(
        unpack_last_kernel,
        [t_cols[0], coefs],
        [back, sums],
        [row] * 3,
        [row_scratch, row_scratch, row_scratch, dma((3,))],
        "unpack_last",
        12,
    )
    return density[None], last[None], before[None]


def solution(mesh):
    blocks = P(("groups", "row"), None, None, None)
    cols = P(("groups", "row"), None)
    return jax.shard_map(
        per_device,
        mesh=mesh,
        in_specs=(blocks, cols, blocks, blocks, cols, blocks, P()),
        out_specs=(blocks, blocks, blocks),
        check_vma=False,
    )
```

```python
import functools

import jax
import jax.numpy as jnp
from jax import lax
from jax.experimental import pallas as pl
from jax.experimental.pallas import tpu as pltpu
from jax.sharding import PartitionSpec as P

REACH = 7
NOTE = 8
VMEM_LIMIT = 60 * 1024 * 1024
SMEM = pl.BlockSpec(memory_space=pltpu.SMEM)
ANY = pl.BlockSpec(memory_space=pl.ANY)


def permute(x, target):
    devices = lax.axis_size("row")
    return lax.ppermute(x, "row", [(i, target(i)) for i in range(devices)])


def after(x, *others):
    return lax.optimization_barrier((x, *others))[0]


RING = (0, 2, 4, 6, 7, 5, 3, 1)


def along_ring(device, by):
    return 2 * RING[(RING.index(device // 2) + by) % len(RING)] + device % 2


def window_rows(me, total):
    if total != 16:
        steps = [0] + [by for hop in range(1, REACH + 1) for by in (-hop, hop)]
        return jnp.mod(me + jnp.array(steps, jnp.int32), total), (5, 4, 4, 2)
    order = (0, -1, 1, -2, 2, -3, 3, 4)
    table = [[along_ring(i, by) ^ core for by in order for core in (0, 1)] for i in range(total)]
    return jnp.array(table, jnp.int32)[me], (6, 4, 4, 2)


def gathered_rows(x, me, total):
    if total != 16:
        rows = [x]
        for hop in range(1, REACH + 1):
            for by in (hop, -hop):
                rows.append(permute(x, lambda i, by=by: (i + by) % total))
        for start, end in ((0, 5), (5, 9), (9, 13), (13, 15)):
            yield rows[start:end]
        return

    def other_core(row):
        return permute(row, lambda i: i ^ 1)

    def round_of(ahead, behind):
        ahead = permute(ahead, lambda i: along_ring(i, 1))
        behind = permute(behind, lambda i: along_ring(i, -1))
        return ahead, behind, [ahead, other_core(ahead), behind, other_core(behind)]

    rows = [x, other_core(x)]
    ahead, behind, first = round_of(x, x)
    ahead, behind, second = round_of(ahead, behind)
    yield rows + first
    there = (rows[1], first[1], first[3])
    ahead, behind, third = round_of(after(ahead, *there), after(behind, *there))
    made = yield second
    ahead, behind = after(ahead, made), after(behind, made)
    far = permute(jnp.where(me % 2 == 0, ahead, behind), lambda i: along_ring(i, 1 if i % 2 == 0 else -1))
    made = yield third
    far = after(far, made)
    yield [far, other_core(far)]


def place_of(offset, dropped):
    named = jnp.logical_and(offset <= 2 * REACH, offset != dropped)
    slot = offset - jnp.where(offset > dropped, 1, 0)
    return jnp.clip(slot, 0, 2 * REACH - 1), named


def dropped_offset(cols, row, total):
    offsets = jnp.mod(cols - row + REACH, total)
    return REACH * (2 * REACH + 1) - jnp.sum(offsets, axis=1)


def pack_kernel(total, info_ref, cols_ref, cur_ref, prev_ref, send_ref, cur, prev, zeros, note, sems):
    row = info_ref[0]
    drop = info_ref[2]
    count, size = cur.shape[:2]
    loads = (
        pltpu.make_async_copy(cur_ref, cur, sems.at[0]),
        pltpu.make_async_copy(prev_ref, prev, sems.at[1]),
    )
    for load in loads:
        load.start()
    zeros[...] = jnp.zeros_like(zeros)
    line = lax.broadcasted_iota(jnp.int32, note.shape, 0)
    note[...] = jnp.where(line == 0, info_ref[1], drop).astype(jnp.float32)

    def fill(j, carry):
        offset = lax.rem(j - row + REACH + total, total)
        _, named = place_of(offset, drop)
        pltpu.make_async_copy(note, send_ref.at[j, pl.ds(2 * size, NOTE)], sems.at[2]).start()

        @pl.when(jnp.logical_not(named))
        def _():
            pltpu.make_async_copy(zeros, send_ref.at[j, pl.ds(0, 2 * size)], sems.at[2]).start()

        return carry

    lax.fori_loop(0, total, fill, 0)
    for which, held in enumerate((cur, prev)):
        loads[which].wait()
        for k in range(count):
            place = send_ref.at[cols_ref[k], pl.ds(which * size, size)]
            pltpu.make_async_copy(held.at[k], place, sems.at[2]).start()
    pltpu.make_async_copy(send_ref, send_ref, sems.at[2]).wait()


def split(x):
    high = x.astype(jnp.bfloat16)
    low = (x - high.astype(jnp.float32)).astype(jnp.bfloat16)
    return high, low


def kept_rows(total, rows_ref, drops_ref, w):
    row = rows_ref[w]
    offset = lax.rem(rows_ref[rows_ref.shape[0] - 1] - row + REACH + total, total)
    _, named = place_of(offset, drops_ref[2 * row + 1])
    return named


def fill_pair(pair, block, w):
    size = block.shape[-1]
    high, low = split(block)
    at = pl.ds(pl.multiple_of(w * size, size), size)
    pair[at, pl.ds(0, size)] = high
    pair[at, pl.ds(size, size)] = low


def products_of(rows, pair):
    group, double = rows.shape[:2]
    size = double // 2
    products = jnp.dot(rows.reshape(group * double, rows.shape[2]), pair, preferred_element_type=jnp.float32)
    for r in range(group):
        parts = products[r * double:r * double + size] + products[r * double + size:(r + 1) * double]
        yield parts[:, :size] + parts[:, size:]


def first_kernel(total, window, start, count, group, drops_ref, rows_ref, t_ref, *refs):
    h_refs = refs[:count]
    if start:
        pair_in, _ = refs[count:count + 2]
        dense_ref, out_ref = refs[count + 2:count + 4]
    else:
        dense_ref, out_ref, pair_out, blocks = refs[count:count + 4]
    stage, dense, prev, pair, h_sem, t_sem, prev_sem, pair_sem, dense_sem, out_sem = refs[-10:]
    size = t_ref.shape[-1]
    kept = functools.partial(kept_rows, total, rows_ref, drops_ref)

    if start:
        pltpu.make_async_copy(pair_in, pair, pair_sem).start()
    else:
        for w in range(window):
            pltpu.make_async_copy(t_ref.at[rows_ref[w], pl.ds(0, size)], blocks.at[w], t_sem).start()
    for r in range(count):
        pltpu.make_async_copy(h_refs[r], stage.at[r], h_sem.at[r]).start()
    for r in range(count):
        block = t_ref.at[rows_ref[start + r], pl.ds(size, size)]
        pltpu.make_async_copy(block, prev.at[r], prev_sem).start()
    if not start:
        pltpu.make_async_copy(blocks, blocks, t_sem).wait()
        for w in range(window):
            fill_pair(pair, jnp.where(kept(w), blocks[w], 0.0), w)
        pltpu.make_async_copy(pair, pair_out, pair_sem).start()

    def densify(r, slot, place):
        row = rows_ref[start + r]
        drop = drops_ref[2 * row]
        for p in range(window):
            offset = lax.rem(rows_ref[p] - row + REACH + total, total)
            k, named = place_of(offset, drop)
            high, low = split(jnp.where(named, stage[r, k], 0.0))
            dense[slot, place, pl.ds(0, size), pl.ds(p * size, size)] = high
            dense[slot, place, pl.ds(size, size), pl.ds(p * size, size)] = low

    def store(g, slot):
        return pltpu.make_async_copy(dense.at[slot], dense_ref.at[pl.ds(g * group, group)], dense_sem.at[slot])

    groups = count // group

    def one(g, carry):
        slot = lax.rem(g, 2)

        @pl.when(g >= 2)
        def _():
            store(g - 2, slot).wait()

        for place in range(group):
            r = g * group + place
            pltpu.make_async_copy(stage.at[r], stage.at[r], h_sem.at[r]).wait()
            densify(r, slot, place)
        store(g, slot).start()
        if start:

            @pl.when(g == 0)
            def _():
                pltpu.make_async_copy(pair, pair, pair_sem).wait()

        @pl.when(g == 0)
        def _():
            pltpu.make_async_copy(prev, prev, prev_sem).wait()

        for place, product in enumerate(products_of(dense[slot], pair[...])):
            r = g * group + place
            prev[r] = jnp.where(kept(start + r), 2.0 * product - prev[r], 0.0)
            pltpu.make_async_copy(prev.at[r], out_ref.at[rows_ref[start + r]], out_sem).start()
        return carry

    lax.fori_loop(0, groups, one, 0)
    for g in range(max(groups - 2, 0), groups):
        store(g, g % 2).wait()
    if not start:
        pltpu.make_async_copy(pair, pair, pair_sem).wait()
    pltpu.make_async_copy(prev, prev, out_sem).wait()


def later_kernel(total, window, group, parts, drops_ref, rows_ref, *refs):
    dense_refs = refs[:len(parts)]
    t_ref, first_ref, out_ref, dense, terms, pairs, dense_sem, t_sem, first_sem, out_sem = refs[len(parts):]
    size = terms.shape[-1]
    groups = window // group
    kept = functools.partial(kept_rows, total, rows_ref, drops_ref)
    for w in range(window):
        pltpu.make_async_copy(first_ref.at[rows_ref[w]], terms.at[w, 1], first_sem).start()
    start = 0
    for part, dense_ref in zip(parts, dense_refs):
        for w in range(start, start + part):
            pltpu.make_async_copy(dense_ref.at[w - start], dense.at[w], dense_sem.at[w // group]).start()
        start += part
    for w in range(window):
        pltpu.make_async_copy(t_ref.at[rows_ref[w], pl.ds(0, size)], terms.at[w, 0], t_sem).start()
    pltpu.make_async_copy(terms.at[:, 1], terms.at[:, 1], first_sem).wait()
    for w in range(window):
        fill_pair(pairs.at[0], terms[w, 1], w)
    pltpu.make_async_copy(terms.at[:, 0], terms.at[:, 0], t_sem).wait()

    def one(g, carry, step):
        rows = dense.at[pl.ds(g * group, group)]
        if step == 0:
            pltpu.make_async_copy(rows, rows, dense_sem.at[g]).wait()
        for r, product in enumerate(products_of(rows[...], pairs[step])):
            w = g * group + r
            newest = jnp.where(kept(w), 2.0 * product - terms[w, step], 0.0)
            terms[w, step] = newest
            if step == 0:
                fill_pair(pairs.at[1], newest, w)
            pltpu.make_async_copy(terms.at[w, step], out_ref.at[rows_ref[w], step], out_sem).start()
        return carry

    for step in range(2):
        lax.fori_loop(0, groups, functools.partial(one, step=step), 0)
    pltpu.make_async_copy(terms, terms, out_sem).wait()


def unpack_first_kernel(cols_ref, coefs_ref, first_ref, density_ref, out_ref, sums, one, sems):
    load = pltpu.make_async_copy(density_ref, sums, sems.at[0])
    load.start()
    for k in range(cols_ref.shape[0]):
        pltpu.make_async_copy(first_ref.at[cols_ref[k]], one.at[k], sems.at[1]).start()
    load.wait()
    pltpu.make_async_copy(one, one, sems.at[1]).wait()
    sums[...] += coefs_ref[0] * one[...]
    store = pltpu.make_async_copy(sums, out_ref, sems.at[0])
    store.start()
    store.wait()


def unpack_last_kernel(cols_ref, coefs_ref, held_ref, sum_ref, density_ref, last_ref, before_ref, sums, two, three, sems):
    load = pltpu.make_async_copy(sum_ref, sums, sems.at[0])
    load.start()
    for place, sem, which in ((two, 1, 0), (three, 2, 1)):
        for k in range(cols_ref.shape[0]):
            pltpu.make_async_copy(held_ref.at[cols_ref[k], which], place.at[k], sems.at[sem]).start()
    pltpu.make_async_copy(two, two, sems.at[1]).wait()
    before = pltpu.make_async_copy(two, before_ref, sems.at[1])
    before.start()
    pltpu.make_async_copy(three, three, sems.at[2]).wait()
    last = pltpu.make_async_copy(three, last_ref, sems.at[2])
    last.start()
    load.wait()
    sums[...] = sums[...] + coefs_ref[1] * two[...] + coefs_ref[2] * three[...]
    store = pltpu.make_async_copy(sums, density_ref, sems.at[0])
    store.start()
    before.wait()
    last.wait()
    store.wait()


def per_device(h_blocks, h_cols, term_prev, term_cur, t_cols, density_in, coefs):
    total = lax.axis_size("row")
    me = lax.axis_index("row")
    count, size = h_blocks.shape[1:3]
    drop_h = dropped_offset(h_cols, me, total)
    drop_t = dropped_offset(t_cols, me, total)
    f32, bf16 = jnp.float32, jnp.bfloat16
    dma = pltpu.SemaphoreType.DMA
    row = jax.ShapeDtypeStruct((count, size, size), f32)
    row_scratch = pltpu.VMEM(row.shape, f32)

    def call(kernel, smem, arrays, outs, scratch, name, aliases={}):
        return pl.pallas_call(
            kernel,
            out_shape=outs,
            in_specs=[SMEM] * len(smem) + [ANY] * len(arrays),
            out_specs=[ANY] * len(outs),
            scratch_shapes=scratch,
            input_output_aliases=aliases,
            compiler_params=pltpu.CompilerParams(vmem_limit_bytes=VMEM_LIMIT),
            name=name,
        )(*smem, *arrays)

    def exchange(x):
        return lax.all_to_all(x, "row", 0, 0, tiled=True)

    (send,) = call(
        functools.partial(pack_kernel, total),
        [jnp.stack([me, drop_h[0], drop_t[0]]), t_cols[0]],
        [term_cur[0], term_prev[0]],
        [jax.ShapeDtypeStruct((total, 2 * size + NOTE, size), f32)],
        [
            row_scratch,
            row_scratch,
            pltpu.VMEM((2 * size, size), f32),
            pltpu.VMEM((NOTE, size), f32),
            dma((3,)),
        ],
        "pack",
    )
    column = exchange(send)
    drops = column[:, 2 * size:2 * size + 2, 0].astype(jnp.int32).reshape(-1)
    indices, parts = window_rows(me, total)
    gathered = gathered_rows(h_blocks[0], me, total)
    rows = jnp.concatenate([indices, me[None]])
    window = sum(parts)
    dense_shape = (window, 2 * size, window * size)
    pair_shape = (window * size, 2 * size)
    dense = []
    start = 0
    for part in parts:
        h_rows = gathered.send(dense[-1] if start else None)
        group = max(g for g in (2, 3, 4, 5) if part % g == 0)
        scratch = [
            pltpu.VMEM((part, count, size, size), f32),
            pltpu.VMEM((2, group) + dense_shape[1:], bf16),
            pltpu.VMEM((part, size, size), f32),
            pltpu.VMEM(pair_shape, bf16),
            dma((part,)),
            dma,
            dma,
            dma,
            dma((2,)),
            dma,
        ]
        if not start:
            scratch = [pltpu.VMEM((window, size, size), f32)] + scratch
        result = call(
            functools.partial(first_kernel, total, window, start, part, group),
            [drops, rows],
            [column, *h_rows] + ([pair, term1] if start else []),
            [
                jax.ShapeDtypeStruct((part,) + dense_shape[1:], bf16),
                jax.ShapeDtypeStruct((total, size, size), f32),
            ] + ([] if start else [jax.ShapeDtypeStruct(pair_shape, bf16)]),
            scratch,
            "first",
            {part + 4: 1} if start else {},
        )
        dense.append(result[0])
        term1 = result[1]
        if not start:
            pair = result[2]
        start += part
    back1 = exchange(term1)
    group = max(g for g in (3, 4) if window % g == 0)
    (terms,) = call(
        functools.partial(later_kernel, total, window, group, parts),
        [drops, rows],
        [*dense, column, term1],
        [jax.ShapeDtypeStruct((total, 2, size, size), f32)],
        [
            pltpu.VMEM(dense_shape, bf16),
            pltpu.VMEM((window, 2, size, size), f32),
            pltpu.VMEM((2,) + pair_shape, bf16),
            dma((window // group,)),
            dma,
            dma,
            dma,
        ],
        "later",
    )
    back = exchange(after(terms, back1))
    (sums,) = call(
        unpack_first_kernel,
        [t_cols[0], coefs],
        [back1, density_in[0]],
        [row],
        [row_scratch, row_scratch, dma((2,))],
        "unpack_first",
    )
    density, last, before = call(
        unpack_last_kernel,
        [t_cols[0], coefs],
        [back, sums],
        [row] * 3,
        [row_scratch, row_scratch, row_scratch, dma((3,))],
        "unpack_last",
    )
    return density[None], last[None], before[None]


def solution(mesh):
    blocks = P(("groups", "row"), None, None, None)
    cols = P(("groups", "row"), None)
    return jax.shard_map(
        per_device,
        mesh=mesh,
        in_specs=(blocks, cols, blocks, blocks, cols, blocks, P()),
        out_specs=(blocks, blocks, blocks),
        check_vma=False,
    )
```

```python
import functools

import jax
import jax.numpy as jnp
from jax import lax
from jax.experimental import pallas as pl
from jax.experimental.pallas import tpu as pltpu
from jax.sharding import PartitionSpec as P

REACH = 7
NOTE = 8
VMEM_LIMIT = 60 * 1024 * 1024
SMEM = pl.BlockSpec(memory_space=pltpu.SMEM)
ANY = pl.BlockSpec(memory_space=pl.ANY)


def permute(x, target):
    devices = lax.axis_size("row")
    return lax.ppermute(x, "row", [(i, target(i)) for i in range(devices)])


def after(x, *others):
    return lax.optimization_barrier((x, *others))[0]


RING = (0, 2, 4, 6, 7, 5, 3, 1)


def along_ring(device, by):
    return 2 * RING[(RING.index(device // 2) + by) % len(RING)] + device % 2


def window_rows(me, total):
    if total != 16:
        steps = [0] + [by for hop in range(1, REACH + 1) for by in (-hop, hop)]
        return jnp.mod(me + jnp.array(steps, jnp.int32), total), (5, 4, 4, 2)
    order = (0, -1, 1, -2, 2, -3, 3, 4)
    table = [[along_ring(i, by) ^ core for by in order for core in (0, 1)] for i in range(total)]
    return jnp.array(table, jnp.int32)[me], (6, 4, 4, 2)


def gathered_rows(x, me, total, exchange):
    if total != 16:
        rows = [x]
        for hop in range(1, REACH + 1):
            for by in (hop, -hop):
                rows.append(permute(x, lambda i, by=by: (i + by) % total))
        yield exchange()
        for start, end in ((0, 5), (5, 9), (9, 13), (13, 15)):
            yield rows[start:end]
        return

    def other_core(row):
        return permute(row, lambda i: i ^ 1)

    def round_of(ahead, behind):
        ahead = permute(ahead, lambda i: along_ring(i, 1))
        behind = permute(behind, lambda i: along_ring(i, -1))
        return ahead, behind, [ahead, other_core(ahead), behind, other_core(behind)]

    rows = [x, other_core(x)]
    ahead, behind, first = round_of(x, x)
    column = exchange(ahead, behind)
    ahead, behind, second = round_of(ahead, behind)
    yield column
    yield rows + first
    there = (column, rows[1], first[1], first[3])
    ahead, behind, third = round_of(after(ahead, *there), after(behind, *there))
    made = yield second
    ahead, behind = after(ahead, made), after(behind, made)
    far = permute(jnp.where(me % 2 == 0, ahead, behind), lambda i: along_ring(i, 1 if i % 2 == 0 else -1))
    made = yield third
    far = after(far, made)
    yield [far, other_core(far)]


def place_of(offset, dropped):
    named = jnp.logical_and(offset <= 2 * REACH, offset != dropped)
    slot = offset - jnp.where(offset > dropped, 1, 0)
    return jnp.clip(slot, 0, 2 * REACH - 1), named


def dropped_offset(cols, row, total):
    offsets = jnp.mod(cols - row + REACH, total)
    return REACH * (2 * REACH + 1) - jnp.sum(offsets, axis=1)


def pack_kernel(total, info_ref, cols_ref, cur_ref, prev_ref, send_ref, cur, prev, zeros, note, sems):
    row = info_ref[0]
    drop = info_ref[2]
    count, size = cur.shape[:2]
    loads = (
        pltpu.make_async_copy(cur_ref, cur, sems.at[0]),
        pltpu.make_async_copy(prev_ref, prev, sems.at[1]),
    )
    for load in loads:
        load.start()
    zeros[...] = jnp.zeros_like(zeros)
    line = lax.broadcasted_iota(jnp.int32, note.shape, 0)
    note[...] = jnp.where(line == 0, info_ref[1], drop).astype(jnp.float32)

    def fill(j, carry):
        offset = lax.rem(j - row + REACH + total, total)
        _, named = place_of(offset, drop)
        pltpu.make_async_copy(note, send_ref.at[j, pl.ds(2 * size, NOTE)], sems.at[2]).start()

        @pl.when(jnp.logical_not(named))
        def _():
            pltpu.make_async_copy(zeros, send_ref.at[j, pl.ds(0, 2 * size)], sems.at[2]).start()

        return carry

    lax.fori_loop(0, total, fill, 0)
    for which, held in enumerate((cur, prev)):
        loads[which].wait()
        for k in range(count):
            place = send_ref.at[cols_ref[k], pl.ds(which * size, size)]
            pltpu.make_async_copy(held.at[k], place, sems.at[2]).start()
    pltpu.make_async_copy(send_ref, send_ref, sems.at[2]).wait()


def split(x):
    high = x.astype(jnp.bfloat16)
    low = (x - high.astype(jnp.float32)).astype(jnp.bfloat16)
    return high, low


def kept_rows(total, rows_ref, drops_ref, w):
    row = rows_ref[w]
    offset = lax.rem(rows_ref[rows_ref.shape[0] - 1] - row + REACH + total, total)
    _, named = place_of(offset, drops_ref[2 * row + 1])
    return named


def fill_pair(pair, block, w):
    size = block.shape[-1]
    high, low = split(block)
    at = pl.ds(pl.multiple_of(w * size, size), size)
    pair[at, pl.ds(0, size)] = high
    pair[at, pl.ds(size, size)] = low


def products_of(rows, pair):
    group, double = rows.shape[:2]
    size = double // 2
    products = jnp.dot(rows.reshape(group * double, rows.shape[2]), pair, preferred_element_type=jnp.float32)
    for r in range(group):
        parts = products[r * double:r * double + size] + products[r * double + size:(r + 1) * double]
        yield parts[:, :size] + parts[:, size:]


def first_kernel(total, window, start, count, group, drops_ref, rows_ref, t_ref, *refs):
    h_refs = refs[:count]
    if start:
        pair_in, _ = refs[count:count + 2]
        dense_ref, out_ref = refs[count + 2:count + 4]
    else:
        dense_ref, out_ref, pair_out, blocks = refs[count:count + 4]
    stage, dense, prev, pair, h_sem, t_sem, prev_sem, pair_sem, dense_sem, out_sem = refs[-10:]
    size = t_ref.shape[-1]
    kept = functools.partial(kept_rows, total, rows_ref, drops_ref)

    if start:
        pltpu.make_async_copy(pair_in, pair, pair_sem).start()
    else:
        for w in range(window):
            pltpu.make_async_copy(t_ref.at[rows_ref[w], pl.ds(0, size)], blocks.at[w], t_sem).start()
    for r in range(count):
        pltpu.make_async_copy(h_refs[r], stage.at[r], h_sem.at[r]).start()
    for r in range(count):
        block = t_ref.at[rows_ref[start + r], pl.ds(size, size)]
        pltpu.make_async_copy(block, prev.at[r], prev_sem).start()
    if not start:
        pltpu.make_async_copy(blocks, blocks, t_sem).wait()
        for w in range(window):
            fill_pair(pair, jnp.where(kept(w), blocks[w], 0.0), w)
        pltpu.make_async_copy(pair, pair_out, pair_sem).start()

    def densify(r, slot, place):
        row = rows_ref[start + r]
        drop = drops_ref[2 * row]
        for p in range(window):
            offset = lax.rem(rows_ref[p] - row + REACH + total, total)
            k, named = place_of(offset, drop)
            high, low = split(jnp.where(named, stage[r, k], 0.0))
            dense[slot, place, pl.ds(0, size), pl.ds(p * size, size)] = high
            dense[slot, place, pl.ds(size, size), pl.ds(p * size, size)] = low

    def store(g, slot):
        return pltpu.make_async_copy(dense.at[slot], dense_ref.at[pl.ds(g * group, group)], dense_sem.at[slot])

    groups = count // group

    def one(g, carry):
        slot = lax.rem(g, 2)

        @pl.when(g >= 2)
        def _():
            store(g - 2, slot).wait()

        for place in range(group):
            r = g * group + place
            pltpu.make_async_copy(stage.at[r], stage.at[r], h_sem.at[r]).wait()
            densify(r, slot, place)
        store(g, slot).start()
        if start:

            @pl.when(g == 0)
            def _():
                pltpu.make_async_copy(pair, pair, pair_sem).wait()

        @pl.when(g == 0)
        def _():
            pltpu.make_async_copy(prev, prev, prev_sem).wait()

        for place, product in enumerate(products_of(dense[slot], pair[...])):
            r = g * group + place
            prev[r] = jnp.where(kept(start + r), 2.0 * product - prev[r], 0.0)
            pltpu.make_async_copy(prev.at[r], out_ref.at[rows_ref[start + r]], out_sem).start()
        return carry

    lax.fori_loop(0, groups, one, 0)
    for g in range(max(groups - 2, 0), groups):
        store(g, g % 2).wait()
    if not start:
        pltpu.make_async_copy(pair, pair, pair_sem).wait()
    pltpu.make_async_copy(prev, prev, out_sem).wait()


def later_kernel(total, window, group, parts, drops_ref, rows_ref, *refs):
    dense_refs = refs[:len(parts)]
    t_ref, first_ref, out_ref, dense, terms, pairs, dense_sem, t_sem, first_sem, out_sem = refs[len(parts):]
    size = terms.shape[-1]
    groups = window // group
    kept = functools.partial(kept_rows, total, rows_ref, drops_ref)
    for w in range(window):
        pltpu.make_async_copy(first_ref.at[rows_ref[w]], terms.at[w, 1], first_sem).start()
    start = 0
    for part, dense_ref in zip(parts, dense_refs):
        for w in range(start, start + part):
            pltpu.make_async_copy(dense_ref.at[w - start], dense.at[w], dense_sem.at[w // group]).start()
        start += part
    for w in range(window):
        pltpu.make_async_copy(t_ref.at[rows_ref[w], pl.ds(0, size)], terms.at[w, 0], t_sem).start()
    pltpu.make_async_copy(terms.at[:, 1], terms.at[:, 1], first_sem).wait()
    for w in range(window):
        fill_pair(pairs.at[0], terms[w, 1], w)
    pltpu.make_async_copy(terms.at[:, 0], terms.at[:, 0], t_sem).wait()

    def one(g, carry, step):
        rows = dense.at[pl.ds(g * group, group)]
        if step == 0:
            pltpu.make_async_copy(rows, rows, dense_sem.at[g]).wait()
        for r, product in enumerate(products_of(rows[...], pairs[step])):
            w = g * group + r
            newest = jnp.where(kept(w), 2.0 * product - terms[w, step], 0.0)
            terms[w, step] = newest
            if step == 0:
                fill_pair(pairs.at[1], newest, w)
            pltpu.make_async_copy(terms.at[w, step], out_ref.at[rows_ref[w], step], out_sem).start()
        return carry

    for step in range(2):
        lax.fori_loop(0, groups, functools.partial(one, step=step), 0)
    pltpu.make_async_copy(terms, terms, out_sem).wait()


def unpack_first_kernel(cols_ref, coefs_ref, first_ref, density_ref, out_ref, sums, one, sems):
    load = pltpu.make_async_copy(density_ref, sums, sems.at[0])
    load.start()
    for k in range(cols_ref.shape[0]):
        pltpu.make_async_copy(first_ref.at[cols_ref[k]], one.at[k], sems.at[1]).start()
    load.wait()
    pltpu.make_async_copy(one, one, sems.at[1]).wait()
    sums[...] += coefs_ref[0] * one[...]
    store = pltpu.make_async_copy(sums, out_ref, sems.at[0])
    store.start()
    store.wait()


def unpack_last_kernel(cols_ref, coefs_ref, held_ref, sum_ref, density_ref, last_ref, before_ref, sums, two, three, sems):
    load = pltpu.make_async_copy(sum_ref, sums, sems.at[0])
    load.start()
    for place, sem, which in ((two, 1, 0), (three, 2, 1)):
        for k in range(cols_ref.shape[0]):
            pltpu.make_async_copy(held_ref.at[cols_ref[k], which], place.at[k], sems.at[sem]).start()
    pltpu.make_async_copy(two, two, sems.at[1]).wait()
    before = pltpu.make_async_copy(two, before_ref, sems.at[1])
    before.start()
    pltpu.make_async_copy(three, three, sems.at[2]).wait()
    last = pltpu.make_async_copy(three, last_ref, sems.at[2])
    last.start()
    load.wait()
    sums[...] = sums[...] + coefs_ref[1] * two[...] + coefs_ref[2] * three[...]
    store = pltpu.make_async_copy(sums, density_ref, sems.at[0])
    store.start()
    before.wait()
    last.wait()
    store.wait()


def per_device(h_blocks, h_cols, term_prev, term_cur, t_cols, density_in, coefs):
    total = lax.axis_size("row")
    me = lax.axis_index("row")
    count, size = h_blocks.shape[1:3]
    drop_h = dropped_offset(h_cols, me, total)
    drop_t = dropped_offset(t_cols, me, total)
    f32, bf16 = jnp.float32, jnp.bfloat16
    dma = pltpu.SemaphoreType.DMA
    row = jax.ShapeDtypeStruct((count, size, size), f32)
    row_scratch = pltpu.VMEM(row.shape, f32)

    def call(kernel, smem, arrays, outs, scratch, name, aliases={}):
        return pl.pallas_call(
            kernel,
            out_shape=outs,
            in_specs=[SMEM] * len(smem) + [ANY] * len(arrays),
            out_specs=[ANY] * len(outs),
            scratch_shapes=scratch,
            input_output_aliases=aliases,
            compiler_params=pltpu.CompilerParams(vmem_limit_bytes=VMEM_LIMIT),
            name=name,
        )(*smem, *arrays)

    def exchange(x):
        return lax.all_to_all(x, "row", 0, 0, tiled=True)

    (send,) = call(
        functools.partial(pack_kernel, total),
        [jnp.stack([me, drop_h[0], drop_t[0]]), t_cols[0]],
        [term_cur[0], term_prev[0]],
        [jax.ShapeDtypeStruct((total, 2 * size + NOTE, size), f32)],
        [
            row_scratch,
            row_scratch,
            pltpu.VMEM((2 * size, size), f32),
            pltpu.VMEM((NOTE, size), f32),
            dma((3,)),
        ],
        "pack",
    )
    indices, parts = window_rows(me, total)
    gathered = gathered_rows(h_blocks[0], me, total, lambda *others: exchange(after(send, *others)))
    column = next(gathered)
    drops = column[:, 2 * size:2 * size + 2, 0].astype(jnp.int32).reshape(-1)
    rows = jnp.concatenate([indices, me[None]])
    window = sum(parts)
    dense_shape = (window, 2 * size, window * size)
    pair_shape = (window * size, 2 * size)
    dense = []
    start = 0
    for part in parts:
        h_rows = gathered.send(dense[-1] if start else None)
        group = max(g for g in (2, 3, 4, 5) if part % g == 0)
        scratch = [
            pltpu.VMEM((part, count, size, size), f32),
            pltpu.VMEM((2, group) + dense_shape[1:], bf16),
            pltpu.VMEM((part, size, size), f32),
            pltpu.VMEM(pair_shape, bf16),
            dma((part,)),
            dma,
            dma,
            dma,
            dma((2,)),
            dma,
        ]
        if not start:
            scratch = [pltpu.VMEM((window, size, size), f32)] + scratch
        result = call(
            functools.partial(first_kernel, total, window, start, part, group),
            [drops, rows],
            [column, *h_rows] + ([pair, term1] if start else []),
            [
                jax.ShapeDtypeStruct((part,) + dense_shape[1:], bf16),
                jax.ShapeDtypeStruct((total, size, size), f32),
            ] + ([] if start else [jax.ShapeDtypeStruct(pair_shape, bf16)]),
            scratch,
            "first",
            {part + 4: 1} if start else {},
        )
        dense.append(result[0])
        term1 = result[1]
        if not start:
            pair = result[2]
        start += part
    back1 = exchange(term1)
    group = max(g for g in (3, 4) if window % g == 0)
    (terms,) = call(
        functools.partial(later_kernel, total, window, group, parts),
        [drops, rows],
        [*dense, column, term1],
        [jax.ShapeDtypeStruct((total, 2, size, size), f32)],
        [
            pltpu.VMEM(dense_shape, bf16),
            pltpu.VMEM((window, 2, size, size), f32),
            pltpu.VMEM((2,) + pair_shape, bf16),
            dma((window // group,)),
            dma,
            dma,
            dma,
        ],
        "later",
    )
    back = exchange(after(terms, back1))
    (sums,) = call(
        unpack_first_kernel,
        [t_cols[0], coefs],
        [back1, density_in[0]],
        [row],
        [row_scratch, row_scratch, dma((2,))],
        "unpack_first",
    )
    density, last, before = call(
        unpack_last_kernel,
        [t_cols[0], coefs],
        [back, sums],
        [row] * 3,
        [row_scratch, row_scratch, row_scratch, dma((3,))],
        "unpack_last",
    )
    return density[None], last[None], before[None]


def solution(mesh):
    blocks = P(("groups", "row"), None, None, None)
    cols = P(("groups", "row"), None)
    return jax.shard_map(
        per_device,
        mesh=mesh,
        in_specs=(blocks, cols, blocks, blocks, cols, blocks, P()),
        out_specs=(blocks, blocks, blocks),
        check_vma=False,
    )
```

```python
import functools

import jax
import jax.numpy as jnp
from jax import lax
from jax.experimental import pallas as pl
from jax.experimental.pallas import tpu as pltpu
from jax.sharding import PartitionSpec as P

REACH = 7
NOTE = 8
VMEM_LIMIT = 60 * 1024 * 1024
WINDOW = 2 * REACH + 1
GROUP = 5
PIECES = (96, 32)
SMEM = pl.BlockSpec(memory_space=pltpu.SMEM)
ANY = pl.BlockSpec(memory_space=pl.ANY)


def cycle_of(total):
    if total != 16:
        return list(range(total))
    chips = (0, 2, 4, 6, 7, 5, 3, 1)
    return [2 * chip + core for chip in chips for core in (0, 1)]


def after(x, *others):
    return lax.optimization_barrier((x, *others))[0]


def place_of(offset, dropped):
    named = jnp.logical_and(offset <= 2 * REACH, offset != dropped)
    slot = offset - jnp.where(offset > dropped, 1, 0)
    return jnp.clip(slot, 0, 2 * REACH - 1), named


def dropped_offset(cols, row, total):
    offsets = jnp.mod(cols - row + REACH, total)
    return REACH * (2 * REACH + 1) - jnp.sum(offsets, axis=1)


def pack_kernel(total, info_ref, cols_ref, cur_ref, prev_ref, send_ref, cur, prev, zeros, note, sems):
    row = info_ref[0]
    drop = info_ref[2]
    count, size = cur.shape[:2]
    loads = (
        pltpu.make_async_copy(cur_ref, cur, sems.at[0]),
        pltpu.make_async_copy(prev_ref, prev, sems.at[1]),
    )
    for load in loads:
        load.start()
    zeros[...] = jnp.zeros_like(zeros)
    line = lax.broadcasted_iota(jnp.int32, note.shape, 0)
    note[...] = jnp.where(line == 0, info_ref[1], drop).astype(jnp.float32)

    def fill(j, carry):
        offset = lax.rem(j - row + REACH + total, total)
        _, named = place_of(offset, drop)
        pltpu.make_async_copy(note, send_ref.at[j, pl.ds(2 * size, NOTE)], sems.at[2]).start()

        @pl.when(jnp.logical_not(named))
        def _():
            pltpu.make_async_copy(zeros, send_ref.at[j, pl.ds(0, 2 * size)], sems.at[2]).start()

        return carry

    lax.fori_loop(0, total, fill, 0)
    for which, held in enumerate((cur, prev)):
        loads[which].wait()
        for k in range(count):
            place = send_ref.at[cols_ref[k], pl.ds(which * size, size)]
            pltpu.make_async_copy(held.at[k], place, sems.at[2]).start()
    pltpu.make_async_copy(send_ref, send_ref, sems.at[2]).wait()


def split(x):
    high = x.astype(jnp.bfloat16)
    low = (x - high.astype(jnp.float32)).astype(jnp.bfloat16)
    return high, low


def kept_rows(total, rows_ref, drops_ref, w):
    row = rows_ref[w]
    offset = lax.rem(rows_ref[rows_ref.shape[0] - 1] - row + REACH + total, total)
    _, named = place_of(offset, drops_ref[2 * row + 1])
    return named


def fill_pair(pair, block, w):
    size = block.shape[-1]
    high, low = split(block)
    at = pl.ds(pl.multiple_of(w * size, size), size)
    pair[at, pl.ds(0, size)] = high
    pair[at, pl.ds(size, size)] = low


def products_of(rows, pair, pieces):
    group, double = rows.shape[:2]
    size = pair.shape[1] // 2
    products = jnp.dot(rows.reshape(group * double, rows.shape[2]), pair, preferred_element_type=jnp.float32)
    for r in range(group):
        start = r * double
        for piece in pieces:
            parts = products[start:start + piece] + products[start + piece:start + 2 * piece]
            yield r, parts[:, :size] + parts[:, size:]
            start += 2 * piece


def first_kernel(total, begin, piece, drops_ref, rows_ref, places_ref, t_ref, h_ref, *refs):
    if begin:
        pair_in, _, dense_ref, out_ref = refs[:4]
    else:
        dense_ref, out_ref, pair_out, blocks = refs[:4]
    stage, dense, prev, pair, h_sem, t_sem, prev_sem, pair_sem, dense_sem, out_sem = refs[-10:]
    size = t_ref.shape[-1]
    kept = functools.partial(kept_rows, total, rows_ref, drops_ref)

    if begin:
        pltpu.make_async_copy(pair_in, pair, pair_sem).start()
    else:
        for w in range(WINDOW):
            pltpu.make_async_copy(t_ref.at[rows_ref[w], pl.ds(0, size)], blocks.at[w], t_sem).start()
    for w in range(WINDOW):
        pltpu.make_async_copy(h_ref.at[places_ref[w]], stage.at[w], h_sem.at[w]).start()
    for w in range(WINDOW):
        lines = t_ref.at[rows_ref[w], pl.ds(size + begin, piece)]
        pltpu.make_async_copy(lines, prev.at[w], prev_sem).start()
    if not begin:
        pltpu.make_async_copy(blocks, blocks, t_sem).wait()
        for w in range(WINDOW):
            fill_pair(pair, jnp.where(kept(w), blocks[w], 0.0), w)
        pltpu.make_async_copy(pair, pair_out, pair_sem).start()

    def densify(w, slot, place):
        row = rows_ref[w]
        drop = drops_ref[2 * row]
        for p in range(WINDOW):
            offset = lax.rem(p - w + REACH + total, total)
            k, named = place_of(offset, drop)
            high, low = split(jnp.where(named, stage[w, k], 0.0))
            dense[slot, place, pl.ds(0, piece), pl.ds(p * size, size)] = high
            dense[slot, place, pl.ds(piece, piece), pl.ds(p * size, size)] = low

    def store(g, slot):
        return pltpu.make_async_copy(dense.at[slot], dense_ref.at[pl.ds(g * GROUP, GROUP)], dense_sem.at[slot])

    groups = WINDOW // GROUP

    def one(g, carry):
        slot = lax.rem(g, 2)

        @pl.when(g >= 2)
        def _():
            store(g - 2, slot).wait()

        for place in range(GROUP):
            w = g * GROUP + place
            pltpu.make_async_copy(stage.at[w], stage.at[w], h_sem.at[w]).wait()
            densify(w, slot, place)
        store(g, slot).start()

        @pl.when(g == 0)
        def _():
            if begin:
                pltpu.make_async_copy(pair, pair, pair_sem).wait()
            pltpu.make_async_copy(prev, prev, prev_sem).wait()

        for place, product in products_of(dense[slot], pair[...], (piece,)):
            w = g * GROUP + place
            prev[w] = jnp.where(kept(w), 2.0 * product - prev[w], 0.0)
            pltpu.make_async_copy(prev.at[w], out_ref.at[rows_ref[w], pl.ds(begin, piece)], out_sem).start()
        return carry

    lax.fori_loop(0, groups, one, 0)
    for g in range(groups - 2, groups):
        store(g, g % 2).wait()
    if not begin:
        pltpu.make_async_copy(pair, pair, pair_sem).wait()
    pltpu.make_async_copy(prev, prev, out_sem).wait()


def later_kernel(total, drops_ref, rows_ref, *refs):
    dense_refs = refs[:len(PIECES)]
    t_ref, first_ref, out_ref, dense, terms, pairs, dense_sem, t_sem, first_sem, out_sem = refs[len(PIECES):]
    size = terms.shape[-1]
    groups = WINDOW // GROUP
    kept = functools.partial(kept_rows, total, rows_ref, drops_ref)
    for w in range(WINDOW):
        pltpu.make_async_copy(first_ref.at[rows_ref[w]], terms.at[w, 1], first_sem).start()
    for g in range(groups):
        begin = 0
        at = pl.ds(g * GROUP, GROUP)
        for piece, dense_ref in zip(PIECES, dense_refs):
            place = dense.at[at, pl.ds(2 * begin, 2 * piece)]
            pltpu.make_async_copy(dense_ref.at[at], place, dense_sem.at[g]).start()
            begin += piece
    for w in range(WINDOW):
        pltpu.make_async_copy(t_ref.at[rows_ref[w], pl.ds(0, size)], terms.at[w, 0], t_sem).start()
    pltpu.make_async_copy(terms.at[:, 1], terms.at[:, 1], first_sem).wait()
    for w in range(WINDOW):
        fill_pair(pairs.at[0], terms[w, 1], w)
    pltpu.make_async_copy(terms.at[:, 0], terms.at[:, 0], t_sem).wait()

    def one(g, carry, step):
        rows = dense.at[pl.ds(g * GROUP, GROUP)]
        if step == 0:
            pltpu.make_async_copy(rows, rows, dense_sem.at[g]).wait()
        begin = 0
        for r, product in products_of(rows[...], pairs[step], PIECES):
            w = g * GROUP + r
            lines = pl.ds(begin, product.shape[0])
            terms[w, step, lines] = jnp.where(kept(w), 2.0 * product - terms[w, step, lines], 0.0)
            begin += product.shape[0]
            if begin == size:
                begin = 0
                if step == 0:
                    fill_pair(pairs.at[1], terms[w, step], w)
                pltpu.make_async_copy(terms.at[w, step], out_ref.at[rows_ref[w], step], out_sem).start()
        return carry

    for step in range(2):
        lax.fori_loop(0, groups, functools.partial(one, step=step), 0)
    pltpu.make_async_copy(terms, terms, out_sem).wait()


def unpack_first_kernel(cols_ref, coefs_ref, first_ref, density_ref, out_ref, sums, one, sems):
    load = pltpu.make_async_copy(density_ref, sums, sems.at[0])
    load.start()
    for k in range(cols_ref.shape[0]):
        pltpu.make_async_copy(first_ref.at[cols_ref[k]], one.at[k], sems.at[1]).start()
    load.wait()
    pltpu.make_async_copy(one, one, sems.at[1]).wait()
    sums[...] += coefs_ref[0] * one[...]
    store = pltpu.make_async_copy(sums, out_ref, sems.at[0])
    store.start()
    store.wait()


def unpack_last_kernel(cols_ref, coefs_ref, held_ref, sum_ref, density_ref, last_ref, before_ref, sums, two, three, sems):
    load = pltpu.make_async_copy(sum_ref, sums, sems.at[0])
    load.start()
    for place, sem, which in ((two, 1, 0), (three, 2, 1)):
        for k in range(cols_ref.shape[0]):
            pltpu.make_async_copy(held_ref.at[cols_ref[k], which], place.at[k], sems.at[sem]).start()
    pltpu.make_async_copy(two, two, sems.at[1]).wait()
    before = pltpu.make_async_copy(two, before_ref, sems.at[1])
    before.start()
    pltpu.make_async_copy(three, three, sems.at[2]).wait()
    last = pltpu.make_async_copy(three, last_ref, sems.at[2])
    last.start()
    load.wait()
    sums[...] = sums[...] + coefs_ref[1] * two[...] + coefs_ref[2] * three[...]
    store = pltpu.make_async_copy(sums, density_ref, sems.at[0])
    store.start()
    before.wait()
    last.wait()
    store.wait()


def per_device(h_blocks, h_cols, term_prev, term_cur, t_cols, density_in, coefs):
    total = lax.axis_size("row")
    me = lax.axis_index("row")
    count, size = h_blocks.shape[1:3]
    drop_h = dropped_offset(h_cols, me, total)
    drop_t = dropped_offset(t_cols, me, total)
    f32, bf16 = jnp.float32, jnp.bfloat16
    dma = pltpu.SemaphoreType.DMA
    row = jax.ShapeDtypeStruct((count, size, size), f32)
    row_scratch = pltpu.VMEM(row.shape, f32)

    def call(kernel, smem, arrays, outs, scratch, name, aliases={}):
        return pl.pallas_call(
            kernel,
            out_shape=outs,
            in_specs=[SMEM] * len(smem) + [ANY] * len(arrays),
            out_specs=[ANY] * len(outs),
            scratch_shapes=scratch,
            input_output_aliases=aliases,
            compiler_params=pltpu.CompilerParams(vmem_limit_bytes=VMEM_LIMIT),
            name=name,
        )(*smem, *arrays)

    def exchange(x):
        return lax.all_to_all(x, "row", 0, 0, tiled=True)

    (send,) = call(
        functools.partial(pack_kernel, total),
        [jnp.stack([me, drop_h[0], drop_t[0]]), t_cols[0]],
        [term_cur[0], term_prev[0]],
        [jax.ShapeDtypeStruct((total, 2 * size + NOTE, size), f32)],
        [
            row_scratch,
            row_scratch,
            pltpu.VMEM((2 * size, size), f32),
            pltpu.VMEM((NOTE, size), f32),
            dma((3,)),
        ],
        "pack",
    )
    cycle = cycle_of(total)
    indices = jnp.mod(me + jnp.arange(-REACH, REACH + 1, dtype=jnp.int32), total)
    places = jnp.array([cycle.index(i) for i in range(total)], jnp.int32)[indices]
    column = exchange(send)
    drops = column[:, 2 * size:2 * size + 2, 0].astype(jnp.int32).reshape(-1)
    rows = jnp.concatenate([indices, me[None]])
    pair_shape = (WINDOW * size, 2 * size)
    dense = []
    begin = 0
    for piece in PIECES:
        h_piece = h_blocks[:, :, begin:begin + piece]
        if begin:
            h_piece = after(h_piece, h_all)
        h_all = lax.all_gather(h_piece, "row", axis=0, tiled=True, axis_index_groups=[cycle])
        scratch = [
            pltpu.VMEM((WINDOW, count, piece, size), f32),
            pltpu.VMEM((2, GROUP, 2 * piece, WINDOW * size), bf16),
            pltpu.VMEM((WINDOW, piece, size), f32),
            pltpu.VMEM(pair_shape, bf16),
            dma((WINDOW,)),
            dma,
            dma,
            dma,
            dma((2,)),
            dma,
        ]
        if not begin:
            scratch = [pltpu.VMEM((WINDOW, size, size), f32)] + scratch
        result = call(
            functools.partial(first_kernel, total, begin, piece),
            [drops, rows, places],
            [column, h_all] + ([pair, term1] if begin else []),
            [
                jax.ShapeDtypeStruct((WINDOW, 2 * piece, WINDOW * size), bf16),
                jax.ShapeDtypeStruct((total, size, size), f32),
            ] + ([] if begin else [jax.ShapeDtypeStruct(pair_shape, bf16)]),
            scratch,
            "first",
            {6: 1} if begin else {},
        )
        dense.append(result[0])
        term1 = result[1]
        if not begin:
            pair = result[2]
        begin += piece
    back1 = exchange(term1)
    (terms,) = call(
        functools.partial(later_kernel, total),
        [drops, rows],
        [*dense, column, term1],
        [jax.ShapeDtypeStruct((total, 2, size, size), f32)],
        [
            pltpu.VMEM((WINDOW, 2 * size, WINDOW * size), bf16),
            pltpu.VMEM((WINDOW, 2, size, size), f32),
            pltpu.VMEM((2,) + pair_shape, bf16),
            dma((WINDOW // GROUP,)),
            dma,
            dma,
            dma,
        ],
        "later",
    )
    back = exchange(after(terms, back1))
    (sums,) = call(
        unpack_first_kernel,
        [t_cols[0], coefs],
        [back1, density_in[0]],
        [row],
        [row_scratch, row_scratch, dma((2,))],
        "unpack_first",
    )
    density, last, before = call(
        unpack_last_kernel,
        [t_cols[0], coefs],
        [back, sums],
        [row] * 3,
        [row_scratch, row_scratch, row_scratch, dma((3,))],
        "unpack_last",
    )
    return density[None], last[None], before[None]


def solution(mesh):
    blocks = P(("groups", "row"), None, None, None)
    cols = P(("groups", "row"), None)
    return jax.shard_map(
        per_device,
        mesh=mesh,
        in_specs=(blocks, cols, blocks, blocks, cols, blocks, P()),
        out_specs=(blocks, blocks, blocks),
        check_vma=False,
    )
```

```python
import functools

import jax
import jax.numpy as jnp
from jax import lax
from jax.experimental import pallas as pl
from jax.experimental.pallas import tpu as pltpu
from jax.sharding import PartitionSpec as P

REACH = 7
NOTE = 8
SMEM = pl.BlockSpec(memory_space=pltpu.SMEM)
ANY = pl.BlockSpec(memory_space=pl.ANY)


def permute(x, target):
    devices = lax.axis_size("row")
    return lax.ppermute(x, "row", [(i, target(i)) for i in range(devices)])


def after(x, *others):
    return lax.optimization_barrier((x, *others))[0]


RING = (0, 2, 4, 6, 7, 5, 3, 1)


def along_ring(device, by):
    return 2 * RING[(RING.index(device // 2) + by) % len(RING)] + device % 2


LAST = 2


def window_table(total):
    if total != 16:
        steps = [0] + [by for hop in range(1, REACH + 1) for by in (-hop, hop)]
        return [[(i + by) % total for by in steps] for i in range(total)], (5, 4, 4, LAST)
    order = (0, -1, 1, -2, 2, -3, 3, 4)
    return [[along_ring(i, by) ^ core for by in order for core in (0, 1)] for i in range(total)], (6, 4, 4, LAST)


def gathered_rows(x, me, total, exchange):
    if total != 16:
        rows = [x]
        for hop in range(1, REACH + 1):
            for by in (hop, -hop):
                rows.append(permute(x, lambda i, by=by: (i + by) % total))
        yield exchange()
        for start, end in ((0, 5), (5, 9), (9, 13), (13, 15)):
            yield rows[start:end]
        return

    def other_core(row):
        return permute(row, lambda i: i ^ 1)

    def round_of(ahead, behind):
        ahead = permute(ahead, lambda i: along_ring(i, 1))
        behind = permute(behind, lambda i: along_ring(i, -1))
        return ahead, behind, [ahead, other_core(ahead), behind, other_core(behind)]

    rows = [x, other_core(x)]
    ahead, behind, first = round_of(x, x)
    column = exchange(ahead, behind)
    ahead, behind, second = round_of(ahead, behind)
    yield column
    yield rows + first
    there = (column, rows[1], first[1], first[3])
    ahead, behind, third = round_of(after(ahead, *there), after(behind, *there))
    made = yield second
    ahead, behind = after(ahead, made), after(behind, made)
    far = permute(jnp.where(me % 2 == 0, ahead, behind), lambda i: along_ring(i, 1 if i % 2 == 0 else -1))
    made = yield third
    far = after(far, made)
    yield [far, other_core(far)]


def place_of(offset, dropped):
    named = jnp.logical_and(offset <= 2 * REACH, offset != dropped)
    slot = offset - jnp.where(offset > dropped, 1, 0)
    return jnp.clip(slot, 0, 2 * REACH - 1), named


def dropped_offset(cols, row, total):
    offsets = jnp.mod(cols - row + REACH, total)
    return REACH * (2 * REACH + 1) - jnp.sum(offsets, axis=1)


def pack_kernel(total, info_ref, cols_ref, cur_ref, prev_ref, send_ref, cur, prev, zeros, note, sems):
    row = info_ref[0]
    drop = info_ref[2]
    count, size = cur.shape[:2]
    loads = (
        pltpu.make_async_copy(cur_ref, cur, sems.at[0]),
        pltpu.make_async_copy(prev_ref, prev, sems.at[1]),
    )
    for load in loads:
        load.start()
    zeros[...] = jnp.zeros_like(zeros)
    line = lax.broadcasted_iota(jnp.int32, note.shape, 0)
    note[...] = jnp.where(line == 0, info_ref[1], drop).astype(jnp.float32)

    def fill(j, carry):
        offset = lax.rem(j - row + REACH + total, total)
        _, named = place_of(offset, drop)
        pltpu.make_async_copy(note, send_ref.at[j, pl.ds(2 * size, NOTE)], sems.at[2]).start()

        @pl.when(jnp.logical_not(named))
        def _():
            pltpu.make_async_copy(zeros, send_ref.at[j, pl.ds(0, 2 * size)], sems.at[2]).start()

        return carry

    lax.fori_loop(0, total, fill, 0)
    for which, held in enumerate((cur, prev)):
        loads[which].wait()
        for k in range(count):
            place = send_ref.at[cols_ref[k], pl.ds(which * size, size)]
            pltpu.make_async_copy(held.at[k], place, sems.at[2]).start()
    pltpu.make_async_copy(send_ref, send_ref, sems.at[2]).wait()


def split(x):
    high = x.astype(jnp.bfloat16)
    low = (x - high.astype(jnp.float32)).astype(jnp.bfloat16)
    return high, low


def kept_rows(total, rows_ref, drops_ref, w):
    row = rows_ref[w]
    offset = lax.rem(rows_ref[rows_ref.shape[0] - 1] - row + REACH + total, total)
    _, named = place_of(offset, drops_ref[2 * row + 1])
    return named


def fill_pair(pair, block, w):
    size = block.shape[-1]
    high, low = split(block)
    at = pl.ds(pl.multiple_of(w * size, size), size)
    pair[at, pl.ds(0, size)] = high
    pair[at, pl.ds(size, size)] = low


def products_of(rows, pair):
    group, double = rows.shape[:2]
    size = double // 2
    products = jnp.dot(rows.reshape(group * double, rows.shape[2]), pair, preferred_element_type=jnp.float32)
    for r in range(group):
        parts = products[r * double:r * double + size] + products[r * double + size:(r + 1) * double]
        yield parts[:, :size] + parts[:, size:]


def first_kernel(total, window, start, count, group, drops_ref, rows_ref, t_ref, *refs):
    h_refs = refs[:count]
    last = start + count == window
    if last:
        pair_in, dense_ref, out_ref = refs[count:count + 3]
    elif start:
        pair_in, _, dense_ref, out_ref = refs[count:count + 4]
    else:
        dense_ref, out_ref, pair_out, blocks = refs[count:count + 4]
    stage, dense, prev, pair, h_sem, t_sem, prev_sem, pair_sem, dense_sem, out_sem = refs[-10:]
    size = t_ref.shape[-1]
    kept = functools.partial(kept_rows, total, rows_ref, drops_ref)

    if start:
        pltpu.make_async_copy(pair_in, pair, pair_sem).start()
    else:
        for w in range(window):
            pltpu.make_async_copy(t_ref.at[rows_ref[w], pl.ds(0, size)], blocks.at[w], t_sem).start()
    for r in range(count):
        pltpu.make_async_copy(h_refs[r], stage.at[r], h_sem.at[r]).start()
    for r in range(count):
        block = t_ref.at[rows_ref[start + r], pl.ds(size, size)]
        pltpu.make_async_copy(block, prev.at[r], prev_sem).start()
    if not start:
        pltpu.make_async_copy(blocks, blocks, t_sem).wait()
        for w in range(window):
            fill_pair(pair, jnp.where(kept(w), blocks[w], 0.0), w)
        pltpu.make_async_copy(pair, pair_out, pair_sem).start()

    def densify(r, slot, place):
        row = rows_ref[start + r]
        drop = drops_ref[2 * row]
        for p in range(window):
            offset = lax.rem(rows_ref[p] - row + REACH + total, total)
            k, named = place_of(offset, drop)
            high, low = split(jnp.where(named, stage[r, k], 0.0))
            dense[slot, place, pl.ds(0, size), pl.ds(p * size, size)] = high
            dense[slot, place, pl.ds(size, size), pl.ds(p * size, size)] = low

    def store(g, slot):
        return pltpu.make_async_copy(dense.at[slot], dense_ref.at[pl.ds(g * group, group)], dense_sem.at[slot])

    groups = count // group

    def one(g, carry):
        slot = lax.rem(g, 2)

        @pl.when(g >= 2)
        def _():
            store(g - 2, slot).wait()

        for place in range(group):
            r = g * group + place
            pltpu.make_async_copy(stage.at[r], stage.at[r], h_sem.at[r]).wait()
            densify(r, slot, place)
        store(g, slot).start()
        if start:

            @pl.when(g == 0)
            def _():
                pltpu.make_async_copy(pair, pair, pair_sem).wait()

        @pl.when(g == 0)
        def _():
            pltpu.make_async_copy(prev, prev, prev_sem).wait()

        for at, product in enumerate(products_of(dense[slot], pair[...])):
            r = g * group + at
            prev[r] = jnp.where(kept(start + r), 2.0 * product - prev[r], 0.0)
            place = out_ref.at[r if last else rows_ref[start + r]]
            pltpu.make_async_copy(prev.at[r], place, out_sem).start()
        return carry

    lax.fori_loop(0, groups, one, 0)
    for g in range(max(groups - 2, 0), groups):
        store(g, g % 2).wait()
    if not start:
        pltpu.make_async_copy(pair, pair, pair_sem).wait()
    pltpu.make_async_copy(prev, prev, out_sem).wait()


def later_kernel(total, window, group, parts, drops_ref, rows_ref, *refs):
    dense_refs = refs[:len(parts)]
    t_ref, first_ref, far_ref, out_ref, dense, terms, pairs, dense_sem, t_sem, first_sem, out_sem = refs[len(parts):]
    size = terms.shape[-1]
    groups = window // group
    kept = functools.partial(kept_rows, total, rows_ref, drops_ref)
    for w in range(window):
        r = w - (window - LAST)
        source = first_ref.at[rows_ref[w]] if r < 0 else far_ref.at[r]
        pltpu.make_async_copy(source, terms.at[w, 1], first_sem).start()
    start = 0
    for part, dense_ref in zip(parts, dense_refs):
        for w in range(start, start + part):
            pltpu.make_async_copy(dense_ref.at[w - start], dense.at[w], dense_sem.at[w // group]).start()
        start += part
    for w in range(window):
        pltpu.make_async_copy(t_ref.at[rows_ref[w], pl.ds(0, size)], terms.at[w, 0], t_sem).start()
    pltpu.make_async_copy(terms.at[:, 1], terms.at[:, 1], first_sem).wait()
    for w in range(window):
        fill_pair(pairs.at[0], terms[w, 1], w)
    pltpu.make_async_copy(terms.at[:, 0], terms.at[:, 0], t_sem).wait()

    def one(g, carry, step):
        rows = dense.at[pl.ds(g * group, group)]
        if step == 0:
            pltpu.make_async_copy(rows, rows, dense_sem.at[g]).wait()
        for r, product in enumerate(products_of(rows[...], pairs[step])):
            w = g * group + r
            newest = jnp.where(kept(w), 2.0 * product - terms[w, step], 0.0)
            terms[w, step] = newest
            if step == 0:
                fill_pair(pairs.at[1], newest, w)
            pltpu.make_async_copy(terms.at[w, step], out_ref.at[rows_ref[w], step], out_sem).start()
        return carry

    for step in range(2):
        lax.fori_loop(0, groups, functools.partial(one, step=step), 0)
    pltpu.make_async_copy(terms, terms, out_sem).wait()


def unpack_first_kernel(cols_ref, far_cols_ref, coefs_ref, first_ref, density_ref, far0_ref, far1_ref, out_ref, sums, one, sems):
    load = pltpu.make_async_copy(density_ref, sums, sems.at[0])
    load.start()
    for k in range(cols_ref.shape[0]):
        col = cols_ref[k]
        far = [col == far_cols_ref[r] for r in range(LAST)]
        choices = ((jnp.logical_not(jnp.logical_or(*far)), first_ref.at[col]), (far[0], far0_ref), (far[1], far1_ref))
        for chosen, source in choices:

            @pl.when(chosen)
            def _(source=source, k=k):
                pltpu.make_async_copy(source, one.at[k], sems.at[1]).start()

    load.wait()
    pltpu.make_async_copy(one, one, sems.at[1]).wait()
    sums[...] += coefs_ref[0] * one[...]
    store = pltpu.make_async_copy(sums, out_ref, sems.at[0])
    store.start()
    store.wait()


def unpack_last_kernel(cols_ref, coefs_ref, held_ref, sum_ref, density_ref, last_ref, before_ref, sums, two, three, sems):
    load = pltpu.make_async_copy(sum_ref, sums, sems.at[0])
    load.start()
    for place, sem, which in ((two, 1, 0), (three, 2, 1)):
        for k in range(cols_ref.shape[0]):
            pltpu.make_async_copy(held_ref.at[cols_ref[k], which], place.at[k], sems.at[sem]).start()
    pltpu.make_async_copy(two, two, sems.at[1]).wait()
    before = pltpu.make_async_copy(two, before_ref, sems.at[1])
    before.start()
    pltpu.make_async_copy(three, three, sems.at[2]).wait()
    last = pltpu.make_async_copy(three, last_ref, sems.at[2])
    last.start()
    load.wait()
    sums[...] = sums[...] + coefs_ref[1] * two[...] + coefs_ref[2] * three[...]
    store = pltpu.make_async_copy(sums, density_ref, sems.at[0])
    store.start()
    before.wait()
    last.wait()
    store.wait()


def per_device(h_blocks, h_cols, term_prev, term_cur, t_cols, density_in, coefs):
    total = lax.axis_size("row")
    me = lax.axis_index("row")
    count, size = h_blocks.shape[1:3]
    drop_h = dropped_offset(h_cols, me, total)
    drop_t = dropped_offset(t_cols, me, total)
    f32, bf16 = jnp.float32, jnp.bfloat16
    dma = pltpu.SemaphoreType.DMA
    row = jax.ShapeDtypeStruct((count, size, size), f32)
    row_scratch = pltpu.VMEM(row.shape, f32)

    def call(kernel, smem, arrays, outs, scratch, name, megabytes=60, aliases={}):
        return pl.pallas_call(
            kernel,
            out_shape=[pltpu.HBM(out.shape, out.dtype) for out in outs],
            in_specs=[SMEM] * len(smem) + [ANY] * len(arrays),
            out_specs=[ANY] * len(outs),
            scratch_shapes=scratch,
            input_output_aliases=aliases,
            compiler_params=pltpu.CompilerParams(vmem_limit_bytes=megabytes * 1024 * 1024),
            name=name,
        )(*smem, *arrays)

    def exchange(x):
        return lax.all_to_all(x, "row", 0, 0, tiled=True)

    (send,) = call(
        functools.partial(pack_kernel, total),
        [jnp.stack([me, drop_h[0], drop_t[0]]), t_cols[0]],
        [term_cur[0], term_prev[0]],
        [jax.ShapeDtypeStruct((total, 2 * size + NOTE, size), f32)],
        [
            row_scratch,
            row_scratch,
            pltpu.VMEM((2 * size, size), f32),
            pltpu.VMEM((NOTE, size), f32),
            dma((3,)),
        ],
        "pack",
    )
    table, parts = window_table(total)
    window = sum(parts)
    far_targets = [[row[window - LAST + r] for row in table] for r in range(LAST)]
    sources = [[targets.index(i) for targets in far_targets] for i in range(total)]
    places = jnp.array([row + from_ for row, from_ in zip(table, sources)], jnp.int32)[me]
    gathered = gathered_rows(h_blocks[0], me, total, lambda *others: exchange(after(send, *others)))
    column = next(gathered)
    drops = column[:, 2 * size:2 * size + 2, 0].astype(jnp.int32).reshape(-1)
    rows = jnp.concatenate([places[:window], me[None]])
    dense_shape = (window, 2 * size, window * size)
    pair_shape = (window * size, 2 * size)
    dense = []
    start = 0
    for part in parts:
        h_rows = gathered.send(dense[-1] if start else None)
        group = max(g for g in (2, 3, 4, 5) if part % g == 0)
        scratch = [
            pltpu.VMEM((part, count, size, size), f32),
            pltpu.VMEM((min(2, part // group), group) + dense_shape[1:], bf16),
            pltpu.VMEM((part, size, size), f32),
            pltpu.VMEM(pair_shape, bf16),
            dma((part,)),
            dma,
            dma,
            dma,
            dma((2,)),
            dma,
        ]
        if not start:
            scratch = [pltpu.VMEM((window, size, size), f32)] + scratch
        last = start + part == window
        term = jax.ShapeDtypeStruct((LAST if last else total, size, size), f32)
        result = call(
            functools.partial(first_kernel, total, window, start, part, group),
            [drops, rows],
            [column, *h_rows] + ([pair] if start else []) + ([term1] if start and not last else []),
            [jax.ShapeDtypeStruct((part,) + dense_shape[1:], bf16), term]
            + ([] if start else [jax.ShapeDtypeStruct(pair_shape, bf16)]),
            scratch,
            "first",
            24 if start + part + LAST >= window else 60,
            {part + 4: 1} if start and not last else {},
        )
        dense.append(result[0])
        if last:
            far = result[1]
        else:
            term1 = result[1]
        if not start:
            pair = result[2]
        start += part
    back1 = exchange(term1)
    far_back = [permute(far[r], lambda i, r=r: far_targets[r][i]) for r in range(LAST)]
    group = max(g for g in (3, 4) if window % g == 0)
    (terms,) = call(
        functools.partial(later_kernel, total, window, group, parts),
        [drops, rows],
        [*dense, column, term1, far],
        [jax.ShapeDtypeStruct((total, 2, size, size), f32)],
        [
            pltpu.VMEM(dense_shape, bf16),
            pltpu.VMEM((window, 2, size, size), f32),
            pltpu.VMEM((2,) + pair_shape, bf16),
            dma((window // group,)),
            dma,
            dma,
            dma,
        ],
        "later",
    )
    back = exchange(after(terms, back1))
    (sums,) = call(
        unpack_first_kernel,
        [t_cols[0], places[window:], coefs],
        [back1, density_in[0], *far_back],
        [row],
        [row_scratch, row_scratch, dma((2,))],
        "unpack_first",
    )
    density, last, before = call(
        unpack_last_kernel,
        [t_cols[0], coefs],
        [back, sums],
        [row] * 3,
        [row_scratch, row_scratch, row_scratch, dma((3,))],
        "unpack_last",
        14,
    )
    return density[None], last[None], before[None]


def solution(mesh):
    blocks = P(("groups", "row"), None, None, None)
    cols = P(("groups", "row"), None)
    return jax.shard_map(
        per_device,
        mesh=mesh,
        in_specs=(blocks, cols, blocks, blocks, cols, blocks, P()),
        out_specs=(blocks, blocks, blocks),
        check_vma=False,
    )
```

```python
import functools

import jax
import jax.numpy as jnp
from jax import lax
from jax.experimental import pallas as pl
from jax.experimental.pallas import tpu as pltpu
from jax.sharding import PartitionSpec as P

REACH = 7
NOTE = 8
SMEM = pl.BlockSpec(memory_space=pltpu.SMEM)
ANY = pl.BlockSpec(memory_space=pl.ANY)


def permute(x, target):
    devices = lax.axis_size("row")
    return lax.ppermute(x, "row", [(i, target(i)) for i in range(devices)])


def after(x, *others):
    return lax.optimization_barrier((x, *others))[0]


RING = (0, 2, 4, 6, 7, 5, 3, 1)


def along_ring(device, by):
    if device % 2:
        by = -by
    return 2 * RING[(RING.index(device // 2) + by) % len(RING)] + device % 2


def window_rows(me, total):
    if total != 16:
        steps = [0] + [by for hop in range(1, REACH + 1) for by in (-hop, hop)]
        return jnp.mod(me + jnp.array(steps, jnp.int32), total), (5, 4, 4, 2)
    order = (0, -1, 1, -2, 2, -3, 3, -4)
    table = [[along_ring(source, by) for by in order for source in (i, i ^ 1)] for i in range(total)]
    return jnp.array(table, jnp.int32)[me], (6, 4, 4, 2)


def gathered_rows(x, total, exchange):
    if total != 16:
        rows = [x]
        for hop in range(1, REACH + 1):
            for by in (hop, -hop):
                rows.append(permute(x, lambda i, by=by: (i + by) % total))
        yield exchange()
        for start, end in ((0, 5), (5, 9), (9, 13), (13, 15)):
            yield rows[start:end]
        return

    def other_core(row):
        return permute(row, lambda i: i ^ 1)

    def round_of(ahead, behind):
        ahead = permute(ahead, lambda i: along_ring(i, 1))
        behind = permute(behind, lambda i: along_ring(i, -1))
        return ahead, behind, [ahead, other_core(ahead), behind, other_core(behind)]

    rows = [x, other_core(x)]
    ahead, behind, first = round_of(x, x)
    ahead, behind, second = round_of(ahead, behind)
    column = exchange(ahead, behind, rows[1], first[1], first[3])
    yield column
    ahead, behind, third = round_of(ahead, behind)
    far = permute(after(ahead, column), lambda i: along_ring(i, 1))
    yield rows + first
    yield second
    yield third
    yield [far, other_core(far)]


def place_of(offset, dropped):
    named = jnp.logical_and(offset <= 2 * REACH, offset != dropped)
    slot = offset - jnp.where(offset > dropped, 1, 0)
    return jnp.clip(slot, 0, 2 * REACH - 1), named


def dropped_offset(cols, row, total):
    offsets = jnp.mod(cols - row + REACH, total)
    return REACH * (2 * REACH + 1) - jnp.sum(offsets, axis=1)


def pack_kernel(total, info_ref, cols_ref, cur_ref, prev_ref, send_ref, cur, prev, zeros, note, sems):
    row = info_ref[0]
    drop = info_ref[2]
    count, size = cur.shape[:2]
    loads = (
        pltpu.make_async_copy(cur_ref, cur, sems.at[0]),
        pltpu.make_async_copy(prev_ref, prev, sems.at[1]),
    )
    for load in loads:
        load.start()
    zeros[...] = jnp.zeros_like(zeros)
    line = lax.broadcasted_iota(jnp.int32, note.shape, 0)
    note[...] = jnp.where(line == 0, info_ref[1], drop).astype(jnp.float32)

    def fill(j, carry):
        offset = lax.rem(j - row + REACH + total, total)
        _, named = place_of(offset, drop)
        pltpu.make_async_copy(note, send_ref.at[j, pl.ds(2 * size, NOTE)], sems.at[2]).start()

        @pl.when(jnp.logical_not(named))
        def _():
            pltpu.make_async_copy(zeros, send_ref.at[j, pl.ds(0, 2 * size)], sems.at[2]).start()

        return carry

    lax.fori_loop(0, total, fill, 0)
    for which, held in enumerate((cur, prev)):
        loads[which].wait()
        for k in range(count):
            place = send_ref.at[cols_ref[k], pl.ds(which * size, size)]
            pltpu.make_async_copy(held.at[k], place, sems.at[2]).start()
    pltpu.make_async_copy(send_ref, send_ref, sems.at[2]).wait()


def split(x):
    high = x.astype(jnp.bfloat16)
    low = (x - high.astype(jnp.float32)).astype(jnp.bfloat16)
    return high, low


def kept_rows(total, rows_ref, drops_ref, w):
    row = rows_ref[w]
    offset = lax.rem(rows_ref[rows_ref.shape[0] - 1] - row + REACH + total, total)
    _, named = place_of(offset, drops_ref[2 * row + 1])
    return named


def fill_pair(pair, block, w):
    size = block.shape[-1]
    high, low = split(block)
    at = pl.ds(pl.multiple_of(w * size, size), size)
    pair[at, pl.ds(0, size)] = high
    pair[at, pl.ds(size, size)] = low


def products_of(rows, pair):
    group, double = rows.shape[:2]
    size = double // 2
    products = jnp.dot(rows.reshape(group * double, rows.shape[2]), pair, preferred_element_type=jnp.float32)
    for r in range(group):
        parts = products[r * double:r * double + size] + products[r * double + size:(r + 1) * double]
        yield parts[:, :size] + parts[:, size:]


def first_kernel(total, window, start, count, group, drops_ref, rows_ref, t_ref, *refs):
    h_refs = refs[:count]
    if start:
        pair_in, _ = refs[count:count + 2]
        dense_ref, out_ref = refs[count + 2:count + 4]
    else:
        dense_ref, out_ref, pair_out, blocks = refs[count:count + 4]
    stage, dense, prev, pair, h_sem, t_sem, prev_sem, pair_sem, dense_sem, out_sem = refs[-10:]
    size = t_ref.shape[-1]
    kept = functools.partial(kept_rows, total, rows_ref, drops_ref)

    if start:
        pltpu.make_async_copy(pair_in, pair, pair_sem).start()
    else:
        for w in range(window):
            pltpu.make_async_copy(t_ref.at[rows_ref[w], pl.ds(0, size)], blocks.at[w], t_sem).start()
    for r in range(count):
        pltpu.make_async_copy(h_refs[r], stage.at[r], h_sem.at[r]).start()
    for r in range(count):
        block = t_ref.at[rows_ref[start + r], pl.ds(size, size)]
        pltpu.make_async_copy(block, prev.at[r], prev_sem).start()
    if not start:
        pltpu.make_async_copy(blocks, blocks, t_sem).wait()
        for w in range(window):
            fill_pair(pair, jnp.where(kept(w), blocks[w], 0.0), w)
        pltpu.make_async_copy(pair, pair_out, pair_sem).start()

    def densify(r, slot, place):
        row = rows_ref[start + r]
        drop = drops_ref[2 * row]
        for p in range(window):
            offset = lax.rem(rows_ref[p] - row + REACH + total, total)
            k, named = place_of(offset, drop)
            high, low = split(jnp.where(named, stage[r, k], 0.0))
            dense[slot, place, pl.ds(0, size), pl.ds(p * size, size)] = high
            dense[slot, place, pl.ds(size, size), pl.ds(p * size, size)] = low

    def store(g, slot):
        return pltpu.make_async_copy(dense.at[slot], dense_ref.at[pl.ds(g * group, group)], dense_sem.at[slot])

    groups = count // group

    def one(g, carry):
        slot = lax.rem(g, 2)

        @pl.when(g >= 2)
        def _():
            store(g - 2, slot).wait()

        for place in range(group):
            r = g * group + place
            pltpu.make_async_copy(stage.at[r], stage.at[r], h_sem.at[r]).wait()
            densify(r, slot, place)
        store(g, slot).start()
        if start:

            @pl.when(g == 0)
            def _():
                pltpu.make_async_copy(pair, pair, pair_sem).wait()

        @pl.when(g == 0)
        def _():
            pltpu.make_async_copy(prev, prev, prev_sem).wait()

        for place, product in enumerate(products_of(dense[slot], pair[...])):
            r = g * group + place
            prev[r] = jnp.where(kept(start + r), 2.0 * product - prev[r], 0.0)
            pltpu.make_async_copy(prev.at[r], out_ref.at[rows_ref[start + r]], out_sem).start()
        return carry

    lax.fori_loop(0, groups, one, 0)
    for g in range(max(groups - 2, 0), groups):
        store(g, g % 2).wait()
    if not start:
        pltpu.make_async_copy(pair, pair, pair_sem).wait()
    pltpu.make_async_copy(prev, prev, out_sem).wait()


def later_kernel(total, window, group, parts, drops_ref, rows_ref, *refs):
    dense_refs = refs[:len(parts)]
    t_ref, first_ref, out_ref, dense, terms, pairs, dense_sem, t_sem, first_sem, out_sem = refs[len(parts):]
    size = terms.shape[-1]
    groups = window // group
    kept = functools.partial(kept_rows, total, rows_ref, drops_ref)
    for w in range(window):
        pltpu.make_async_copy(first_ref.at[rows_ref[w]], terms.at[w, 1], first_sem).start()
    start = 0
    for part, dense_ref in zip(parts, dense_refs):
        for w in range(start, start + part):
            pltpu.make_async_copy(dense_ref.at[w - start], dense.at[w], dense_sem.at[w // group]).start()
        start += part
    for w in range(window):
        pltpu.make_async_copy(t_ref.at[rows_ref[w], pl.ds(0, size)], terms.at[w, 0], t_sem).start()
    pltpu.make_async_copy(terms.at[:, 1], terms.at[:, 1], first_sem).wait()
    for w in range(window):
        fill_pair(pairs.at[0], terms[w, 1], w)
    pltpu.make_async_copy(terms.at[:, 0], terms.at[:, 0], t_sem).wait()

    def one(g, carry, step):
        rows = dense.at[pl.ds(g * group, group)]
        if step == 0:
            pltpu.make_async_copy(rows, rows, dense_sem.at[g]).wait()
        for r, product in enumerate(products_of(rows[...], pairs[step])):
            w = g * group + r
            newest = jnp.where(kept(w), 2.0 * product - terms[w, step], 0.0)
            terms[w, step] = newest
            if step == 0:
                fill_pair(pairs.at[1], newest, w)
            pltpu.make_async_copy(terms.at[w, step], out_ref.at[rows_ref[w], step], out_sem).start()
        return carry

    for step in range(2):
        lax.fori_loop(0, groups, functools.partial(one, step=step), 0)
    pltpu.make_async_copy(terms, terms, out_sem).wait()


def unpack_first_kernel(cols_ref, coefs_ref, first_ref, density_ref, out_ref, sums, one, sems):
    load = pltpu.make_async_copy(density_ref, sums, sems.at[0])
    load.start()
    for k in range(cols_ref.shape[0]):
        pltpu.make_async_copy(first_ref.at[cols_ref[k]], one.at[k], sems.at[1]).start()
    load.wait()
    pltpu.make_async_copy(one, one, sems.at[1]).wait()
    sums[...] += coefs_ref[0] * one[...]
    store = pltpu.make_async_copy(sums, out_ref, sems.at[0])
    store.start()
    store.wait()


def unpack_last_kernel(cols_ref, coefs_ref, held_ref, sum_ref, density_ref, last_ref, before_ref, sums, two, three, sems):
    load = pltpu.make_async_copy(sum_ref, sums, sems.at[0])
    load.start()
    for place, sem, which in ((two, 1, 0), (three, 2, 1)):
        for k in range(cols_ref.shape[0]):
            pltpu.make_async_copy(held_ref.at[cols_ref[k], which], place.at[k], sems.at[sem]).start()
    pltpu.make_async_copy(two, two, sems.at[1]).wait()
    before = pltpu.make_async_copy(two, before_ref, sems.at[1])
    before.start()
    pltpu.make_async_copy(three, three, sems.at[2]).wait()
    last = pltpu.make_async_copy(three, last_ref, sems.at[2])
    last.start()
    load.wait()
    sums[...] = sums[...] + coefs_ref[1] * two[...] + coefs_ref[2] * three[...]
    store = pltpu.make_async_copy(sums, density_ref, sems.at[0])
    store.start()
    before.wait()
    last.wait()
    store.wait()


def per_device(h_blocks, h_cols, term_prev, term_cur, t_cols, density_in, coefs):
    total = lax.axis_size("row")
    me = lax.axis_index("row")
    count, size = h_blocks.shape[1:3]
    drop_h = dropped_offset(h_cols, me, total)
    drop_t = dropped_offset(t_cols, me, total)
    f32, bf16 = jnp.float32, jnp.bfloat16
    dma = pltpu.SemaphoreType.DMA
    row = jax.ShapeDtypeStruct((count, size, size), f32)
    row_scratch = pltpu.VMEM(row.shape, f32)

    def call(kernel, smem, arrays, outs, scratch, name, megabytes, aliases={}):
        return pl.pallas_call(
            kernel,
            out_shape=[pltpu.HBM(out.shape, out.dtype) for out in outs],
            in_specs=[SMEM] * len(smem) + [ANY] * len(arrays),
            out_specs=[ANY] * len(outs),
            scratch_shapes=scratch,
            input_output_aliases=aliases,
            compiler_params=pltpu.CompilerParams(vmem_limit_bytes=megabytes * 1024 * 1024),
            name=name,
        )(*smem, *arrays)

    def exchange(x):
        return lax.all_to_all(x, "row", 0, 0, tiled=True)

    (send,) = call(
        functools.partial(pack_kernel, total),
        [jnp.stack([me, drop_h[0], drop_t[0]]), t_cols[0]],
        [term_cur[0], term_prev[0]],
        [jax.ShapeDtypeStruct((total, 2 * size + NOTE, size), f32)],
        [
            row_scratch,
            row_scratch,
            pltpu.VMEM((2 * size, size), f32),
            pltpu.VMEM((NOTE, size), f32),
            dma((3,)),
        ],
        "pack",
        12,
    )
    indices, parts = window_rows(me, total)
    gathered = gathered_rows(h_blocks[0], total, lambda *others: exchange(after(send, *others)))
    column = next(gathered)
    drops = column[:, 2 * size:2 * size + 2, 0].astype(jnp.int32).reshape(-1)
    rows = jnp.concatenate([indices, me[None]])
    window = sum(parts)
    dense_shape = (window, 2 * size, window * size)
    pair_shape = (window * size, 2 * size)
    dense = []
    start = 0
    for part in parts:
        h_rows = next(gathered)
        group = max(g for g in (2, 3, 4, 5) if part % g == 0)
        scratch = [
            pltpu.VMEM((part, count, size, size), f32),
            pltpu.VMEM((min(2, part // group), group) + dense_shape[1:], bf16),
            pltpu.VMEM((part, size, size), f32),
            pltpu.VMEM(pair_shape, bf16),
            dma((part,)),
            dma,
            dma,
            dma,
            dma((2,)),
            dma,
        ]
        if not start:
            scratch = [pltpu.VMEM((window, size, size), f32)] + scratch
        result = call(
            functools.partial(first_kernel, total, window, start, part, group),
            [drops, rows],
            [column, *h_rows] + ([pair, term1] if start else []),
            [
                jax.ShapeDtypeStruct((part,) + dense_shape[1:], bf16),
                jax.ShapeDtypeStruct((total, size, size), f32),
            ] + ([] if start else [jax.ShapeDtypeStruct(pair_shape, bf16)]),
            scratch,
            "first",
            24,
            {part + 4: 1} if start else {},
        )
        dense.append(result[0])
        term1 = result[1]
        if not start:
            pair = result[2]
        start += part
    back1 = exchange(term1)
    group = max(g for g in (3, 4) if window % g == 0)
    (terms,) = call(
        functools.partial(later_kernel, total, window, group, parts),
        [drops, rows],
        [*dense, column, term1],
        [jax.ShapeDtypeStruct((total, 2, size, size), f32)],
        [
            pltpu.VMEM(dense_shape, bf16),
            pltpu.VMEM((window, 2, size, size), f32),
            pltpu.VMEM((2,) + pair_shape, bf16),
            dma((window // group,)),
            dma,
            dma,
            dma,
        ],
        "later",
        60,
    )
    back = exchange(after(terms, back1))
    (sums,) = call(
        unpack_first_kernel,
        [t_cols[0], coefs],
        [back1, density_in[0]],
        [row],
        [row_scratch, row_scratch, dma((2,))],
        "unpack_first",
        60,
    )
    density, last, before = call(
        unpack_last_kernel,
        [t_cols[0], coefs],
        [back, sums],
        [row] * 3,
        [row_scratch, row_scratch, row_scratch, dma((3,))],
        "unpack_last",
        60,
    )
    return density[None], last[None], before[None]


def solution(mesh):
    blocks = P(("groups", "row"), None, None, None)
    cols = P(("groups", "row"), None)
    return jax.shard_map(
        per_device,
        mesh=mesh,
        in_specs=(blocks, cols, blocks, blocks, cols, blocks, P()),
        out_specs=(blocks, blocks, blocks),
        check_vma=False,
    )
```

```python
import functools

import jax
import jax.numpy as jnp
from jax import lax
from jax.experimental import pallas as pl
from jax.experimental.pallas import tpu as pltpu
from jax.sharding import PartitionSpec as P

REACH = 7
NOTE = 8
SMEM = pl.BlockSpec(memory_space=pltpu.SMEM)
ANY = pl.BlockSpec(memory_space=pl.ANY)


def permute(x, target):
    devices = lax.axis_size("row")
    return lax.ppermute(x, "row", [(i, target(i)) for i in range(devices)])


def after(x, *others):
    return lax.optimization_barrier((x, *others))[0]


RING = (0, 2, 4, 6, 7, 5, 3, 1)


def along_ring(device, by):
    if device % 2:
        by = -by
    return 2 * RING[(RING.index(device // 2) + by) % len(RING)] + device % 2


def window_rows(me, total):
    if total != 16:
        steps = [0] + [by for hop in range(1, REACH + 1) for by in (-hop, hop)]
        return jnp.mod(me + jnp.array(steps, jnp.int32), total), (5, 4, 4, 2)
    order = (0, -1, 1, -2, 2, -3, 3, -4)
    table = [[along_ring(source, by) for by in order for source in (i, i ^ 1)] for i in range(total)]
    return jnp.array(table, jnp.int32)[me], (6, 4, 4, 2)


def gathered_rows(x, total, exchange):
    if total != 16:
        rows = [x]
        for hop in range(1, REACH + 1):
            for by in (hop, -hop):
                rows.append(permute(x, lambda i, by=by: (i + by) % total))
        yield exchange()
        for start, end in ((0, 5), (5, 9), (9, 13), (13, 15)):
            yield rows[start:end]
        return

    def other_core(row):
        return permute(row, lambda i: i ^ 1)

    def round_of(ahead, behind):
        ahead = permute(ahead, lambda i: along_ring(i, 1))
        behind = permute(behind, lambda i: along_ring(i, -1))
        return ahead, behind, [ahead, other_core(ahead), behind, other_core(behind)]

    rows = [x, other_core(x)]
    ahead, behind, first = round_of(x, x)
    ahead, behind, second = round_of(ahead, behind)
    column = exchange(ahead, behind, rows[1], first[1], first[3])
    yield column
    ahead, behind, third = round_of(ahead, behind)
    far = permute(after(ahead, column), lambda i: along_ring(i, 1))
    yield rows + first
    made = yield second
    yield third
    far = after(far, made)
    yield [far, other_core(far)]


def place_of(offset, dropped):
    named = jnp.logical_and(offset <= 2 * REACH, offset != dropped)
    slot = offset - jnp.where(offset > dropped, 1, 0)
    return jnp.clip(slot, 0, 2 * REACH - 1), named


def dropped_offset(cols, row, total):
    offsets = jnp.mod(cols - row + REACH, total)
    return REACH * (2 * REACH + 1) - jnp.sum(offsets, axis=1)


def pack_kernel(total, info_ref, cols_ref, cur_ref, prev_ref, send_ref, cur, prev, zeros, note, sems):
    row = info_ref[0]
    drop = info_ref[2]
    count, size = cur.shape[:2]
    loads = (
        pltpu.make_async_copy(cur_ref, cur, sems.at[0]),
        pltpu.make_async_copy(prev_ref, prev, sems.at[1]),
    )
    for load in loads:
        load.start()
    zeros[...] = jnp.zeros_like(zeros)
    line = lax.broadcasted_iota(jnp.int32, note.shape, 0)
    note[...] = jnp.where(line == 0, info_ref[1], drop).astype(jnp.float32)

    def fill(j, carry):
        offset = lax.rem(j - row + REACH + total, total)
        _, named = place_of(offset, drop)
        pltpu.make_async_copy(note, send_ref.at[j, pl.ds(2 * size, NOTE)], sems.at[2]).start()

        @pl.when(jnp.logical_not(named))
        def _():
            pltpu.make_async_copy(zeros, send_ref.at[j, pl.ds(0, 2 * size)], sems.at[2]).start()

        return carry

    lax.fori_loop(0, total, fill, 0)
    for which, held in enumerate((cur, prev)):
        loads[which].wait()
        for k in range(count):
            place = send_ref.at[cols_ref[k], pl.ds(which * size, size)]
            pltpu.make_async_copy(held.at[k], place, sems.at[2]).start()
    pltpu.make_async_copy(send_ref, send_ref, sems.at[2]).wait()


def split(x):
    high = x.astype(jnp.bfloat16)
    low = (x - high.astype(jnp.float32)).astype(jnp.bfloat16)
    return high, low


def kept_rows(total, rows_ref, drops_ref, w):
    row = rows_ref[w]
    offset = lax.rem(rows_ref[rows_ref.shape[0] - 1] - row + REACH + total, total)
    _, named = place_of(offset, drops_ref[2 * row + 1])
    return named


def fill_pair(pair, block, w):
    size = block.shape[-1]
    high, low = split(block)
    at = pl.ds(pl.multiple_of(w * size, size), size)
    pair[at, pl.ds(0, size)] = high
    pair[at, pl.ds(size, size)] = low


def products_of(rows, pair):
    group, double = rows.shape[:2]
    size = double // 2
    products = jnp.dot(rows.reshape(group * double, rows.shape[2]), pair, preferred_element_type=jnp.float32)
    for r in range(group):
        parts = products[r * double:r * double + size] + products[r * double + size:(r + 1) * double]
        yield parts[:, :size] + parts[:, size:]


def first_kernel(total, window, start, count, group, drops_ref, rows_ref, t_ref, *refs):
    h_refs = refs[:count]
    if start:
        pair_in, _ = refs[count:count + 2]
        dense_ref, out_ref = refs[count + 2:count + 4]
    else:
        dense_ref, out_ref, pair_out, blocks = refs[count:count + 4]
    stage, dense, prev, pair, h_sem, t_sem, prev_sem, pair_sem, dense_sem, out_sem = refs[-10:]
    size = t_ref.shape[-1]
    kept = functools.partial(kept_rows, total, rows_ref, drops_ref)

    if start:
        pltpu.make_async_copy(pair_in, pair, pair_sem).start()
    else:
        for w in range(window):
            pltpu.make_async_copy(t_ref.at[rows_ref[w], pl.ds(0, size)], blocks.at[w], t_sem).start()
    for r in range(count):
        pltpu.make_async_copy(h_refs[r], stage.at[r], h_sem.at[r]).start()
    for r in range(count):
        block = t_ref.at[rows_ref[start + r], pl.ds(size, size)]
        pltpu.make_async_copy(block, prev.at[r], prev_sem).start()
    if not start:
        pltpu.make_async_copy(blocks, blocks, t_sem).wait()
        for w in range(window):
            fill_pair(pair, jnp.where(kept(w), blocks[w], 0.0), w)
        pltpu.make_async_copy(pair, pair_out, pair_sem).start()

    def densify(r, slot, place):
        row = rows_ref[start + r]
        drop = drops_ref[2 * row]
        for p in range(window):
            offset = lax.rem(rows_ref[p] - row + REACH + total, total)
            k, named = place_of(offset, drop)
            high, low = split(jnp.where(named, stage[r, k], 0.0))
            dense[slot, place, pl.ds(0, size), pl.ds(p * size, size)] = high
            dense[slot, place, pl.ds(size, size), pl.ds(p * size, size)] = low

    def store(g, slot):
        return pltpu.make_async_copy(dense.at[slot], dense_ref.at[pl.ds(g * group, group)], dense_sem.at[slot])

    groups = count // group

    def one(g, carry):
        slot = lax.rem(g, 2)

        @pl.when(g >= 2)
        def _():
            store(g - 2, slot).wait()

        for place in range(group):
            r = g * group + place
            pltpu.make_async_copy(stage.at[r], stage.at[r], h_sem.at[r]).wait()
            densify(r, slot, place)
        store(g, slot).start()
        if start:

            @pl.when(g == 0)
            def _():
                pltpu.make_async_copy(pair, pair, pair_sem).wait()

        @pl.when(g == 0)
        def _():
            pltpu.make_async_copy(prev, prev, prev_sem).wait()

        for place, product in enumerate(products_of(dense[slot], pair[...])):
            r = g * group + place
            prev[r] = jnp.where(kept(start + r), 2.0 * product - prev[r], 0.0)
            pltpu.make_async_copy(prev.at[r], out_ref.at[rows_ref[start + r]], out_sem).start()
        return carry

    lax.fori_loop(0, groups, one, 0)
    for g in range(max(groups - 2, 0), groups):
        store(g, g % 2).wait()
    if not start:
        pltpu.make_async_copy(pair, pair, pair_sem).wait()
    pltpu.make_async_copy(prev, prev, out_sem).wait()


def later_kernel(total, window, group, parts, drops_ref, rows_ref, *refs):
    dense_refs = refs[:len(parts)]
    t_ref, first_ref, out_ref, dense, terms, pairs, dense_sem, t_sem, first_sem, out_sem = refs[len(parts):]
    size = terms.shape[-1]
    groups = window // group
    kept = functools.partial(kept_rows, total, rows_ref, drops_ref)
    for w in range(window):
        pltpu.make_async_copy(first_ref.at[rows_ref[w]], terms.at[w, 1], first_sem).start()
    start = 0
    for part, dense_ref in zip(parts, dense_refs):
        for w in range(start, start + part):
            pltpu.make_async_copy(dense_ref.at[w - start], dense.at[w], dense_sem.at[w // group]).start()
        start += part
    for w in range(window):
        pltpu.make_async_copy(t_ref.at[rows_ref[w], pl.ds(0, size)], terms.at[w, 0], t_sem).start()
    pltpu.make_async_copy(terms.at[:, 1], terms.at[:, 1], first_sem).wait()
    for w in range(window):
        fill_pair(pairs.at[0], terms[w, 1], w)
    pltpu.make_async_copy(terms.at[:, 0], terms.at[:, 0], t_sem).wait()

    def one(g, carry, step):
        rows = dense.at[pl.ds(g * group, group)]
        if step == 0:
            pltpu.make_async_copy(rows, rows, dense_sem.at[g]).wait()
        for r, product in enumerate(products_of(rows[...], pairs[step])):
            w = g * group + r
            newest = jnp.where(kept(w), 2.0 * product - terms[w, step], 0.0)
            terms[w, step] = newest
            if step == 0:
                fill_pair(pairs.at[1], newest, w)
            pltpu.make_async_copy(terms.at[w, step], out_ref.at[rows_ref[w], step], out_sem).start()
        return carry

    for step in range(2):
        lax.fori_loop(0, groups, functools.partial(one, step=step), 0)
    pltpu.make_async_copy(terms, terms, out_sem).wait()


def unpack_first_kernel(cols_ref, coefs_ref, first_ref, density_ref, out_ref, sums, one, sems):
    load = pltpu.make_async_copy(density_ref, sums, sems.at[0])
    load.start()
    for k in range(cols_ref.shape[0]):
        pltpu.make_async_copy(first_ref.at[cols_ref[k]], one.at[k], sems.at[1]).start()
    load.wait()
    pltpu.make_async_copy(one, one, sems.at[1]).wait()
    sums[...] += coefs_ref[0] * one[...]
    store = pltpu.make_async_copy(sums, out_ref, sems.at[0])
    store.start()
    store.wait()


def unpack_last_kernel(cols_ref, coefs_ref, held_ref, sum_ref, density_ref, last_ref, before_ref, sums, two, three, sems):
    load = pltpu.make_async_copy(sum_ref, sums, sems.at[0])
    load.start()
    for place, sem, which in ((two, 1, 0), (three, 2, 1)):
        for k in range(cols_ref.shape[0]):
            pltpu.make_async_copy(held_ref.at[cols_ref[k], which], place.at[k], sems.at[sem]).start()
    pltpu.make_async_copy(two, two, sems.at[1]).wait()
    before = pltpu.make_async_copy(two, before_ref, sems.at[1])
    before.start()
    pltpu.make_async_copy(three, three, sems.at[2]).wait()
    last = pltpu.make_async_copy(three, last_ref, sems.at[2])
    last.start()
    load.wait()
    sums[...] = sums[...] + coefs_ref[1] * two[...] + coefs_ref[2] * three[...]
    store = pltpu.make_async_copy(sums, density_ref, sems.at[0])
    store.start()
    before.wait()
    last.wait()
    store.wait()


def per_device(h_blocks, h_cols, term_prev, term_cur, t_cols, density_in, coefs):
    total = lax.axis_size("row")
    me = lax.axis_index("row")
    count, size = h_blocks.shape[1:3]
    drop_h = dropped_offset(h_cols, me, total)
    drop_t = dropped_offset(t_cols, me, total)
    f32, bf16 = jnp.float32, jnp.bfloat16
    dma = pltpu.SemaphoreType.DMA
    row = jax.ShapeDtypeStruct((count, size, size), f32)
    row_scratch = pltpu.VMEM(row.shape, f32)

    def call(kernel, smem, arrays, outs, scratch, name, megabytes, aliases={}):
        return pl.pallas_call(
            kernel,
            out_shape=[pltpu.HBM(out.shape, out.dtype) for out in outs],
            in_specs=[SMEM] * len(smem) + [ANY] * len(arrays),
            out_specs=[ANY] * len(outs),
            scratch_shapes=scratch,
            input_output_aliases=aliases,
            compiler_params=pltpu.CompilerParams(vmem_limit_bytes=megabytes * 1024 * 1024),
            name=name,
        )(*smem, *arrays)

    def exchange(x):
        return lax.all_to_all(x, "row", 0, 0, tiled=True)

    (send,) = call(
        functools.partial(pack_kernel, total),
        [jnp.stack([me, drop_h[0], drop_t[0]]), t_cols[0]],
        [term_cur[0], term_prev[0]],
        [jax.ShapeDtypeStruct((total, 2 * size + NOTE, size), f32)],
        [
            row_scratch,
            row_scratch,
            pltpu.VMEM((2 * size, size), f32),
            pltpu.VMEM((NOTE, size), f32),
            dma((3,)),
        ],
        "pack",
        60,
    )
    indices, parts = window_rows(me, total)
    gathered = gathered_rows(h_blocks[0], total, lambda *others: exchange(after(send, *others)))
    column = next(gathered)
    drops = column[:, 2 * size:2 * size + 2, 0].astype(jnp.int32).reshape(-1)
    rows = jnp.concatenate([indices, me[None]])
    window = sum(parts)
    dense_shape = (window, 2 * size, window * size)
    pair_shape = (window * size, 2 * size)
    dense = []
    start = 0
    for part in parts:
        h_rows = gathered.send(dense[-1] if start else None)
        group = max(g for g in (2, 3, 4, 5) if part % g == 0)
        scratch = [
            pltpu.VMEM((part, count, size, size), f32),
            pltpu.VMEM((min(2, part // group), group) + dense_shape[1:], bf16),
            pltpu.VMEM((part, size, size), f32),
            pltpu.VMEM(pair_shape, bf16),
            dma((part,)),
            dma,
            dma,
            dma,
            dma((2,)),
            dma,
        ]
        if not start:
            scratch = [pltpu.VMEM((window, size, size), f32)] + scratch
        result = call(
            functools.partial(first_kernel, total, window, start, part, group),
            [drops, rows],
            [column, *h_rows] + ([pair, term1] if start else []),
            [
                jax.ShapeDtypeStruct((part,) + dense_shape[1:], bf16),
                jax.ShapeDtypeStruct((total, size, size), f32),
            ] + ([] if start else [jax.ShapeDtypeStruct(pair_shape, bf16)]),
            scratch,
            "first",
            60 if start < 10 else 24,
            {part + 4: 1} if start else {},
        )
        dense.append(result[0])
        term1 = result[1]
        if not start:
            pair = result[2]
        start += part
    back1 = exchange(term1)
    group = max(g for g in (3, 4) if window % g == 0)
    (terms,) = call(
        functools.partial(later_kernel, total, window, group, parts),
        [drops, rows],
        [*dense, column, term1],
        [jax.ShapeDtypeStruct((total, 2, size, size), f32)],
        [
            pltpu.VMEM(dense_shape, bf16),
            pltpu.VMEM((window, 2, size, size), f32),
            pltpu.VMEM((2,) + pair_shape, bf16),
            dma((window // group,)),
            dma,
            dma,
            dma,
        ],
        "later",
        60,
    )
    back = exchange(after(terms, back1))
    (sums,) = call(
        unpack_first_kernel,
        [t_cols[0], coefs],
        [back1, density_in[0]],
        [row],
        [row_scratch, row_scratch, dma((2,))],
        "unpack_first",
        60,
    )
    density, last, before = call(
        unpack_last_kernel,
        [t_cols[0], coefs],
        [back, sums],
        [row] * 3,
        [row_scratch, row_scratch, row_scratch, dma((3,))],
        "unpack_last",
        60,
    )
    return density[None], last[None], before[None]


def solution(mesh):
    blocks = P(("groups", "row"), None, None, None)
    cols = P(("groups", "row"), None)
    return jax.shard_map(
        per_device,
        mesh=mesh,
        in_specs=(blocks, cols, blocks, blocks, cols, blocks, P()),
        out_specs=(blocks, blocks, blocks),
        check_vma=False,
    )
```

```python
import functools

import jax
import jax.numpy as jnp
from jax import lax
from jax.experimental import pallas as pl
from jax.experimental.pallas import tpu as pltpu
from jax.sharding import PartitionSpec as P

REACH = 7
NOTE = 8
SMEM = pl.BlockSpec(memory_space=pltpu.SMEM)
ANY = pl.BlockSpec(memory_space=pl.ANY)


def permute(x, target):
    devices = lax.axis_size("row")
    return lax.ppermute(x, "row", [(i, target(i)) for i in range(devices)])


def after(x, *others):
    return lax.optimization_barrier((x, *others))[0]


RING = (0, 2, 4, 6, 7, 5, 3, 1)


def along_ring(device, by):
    if device % 2:
        by = -by
    return 2 * RING[(RING.index(device // 2) + by) % len(RING)] + device % 2


def window_table(total):
    if total != 16:
        steps = [0] + [by for hop in range(1, REACH + 1) for by in (-hop, hop)]
        return [[(i + by) % total for by in steps] for i in range(total)], (13, 2)
    order = (0, -1, 1, -2, 2, -3, 3, -4)
    table = [[along_ring(source, by) for by in order for source in (i, i ^ 1)] for i in range(total)]
    return table, (14, 2)


def gathered_rows(x, total, exchange):
    if total != 16:
        rows = [x]
        for hop in range(1, REACH + 1):
            for by in (hop, -hop):
                rows.append(permute(x, lambda i, by=by: (i + by) % total))
        yield exchange()
        yield rows[:13]
        yield rows[13:]
        return

    def other_core(row):
        return permute(row, lambda i: i ^ 1)

    def round_of(ahead, behind):
        ahead = permute(ahead, lambda i: along_ring(i, 1))
        behind = permute(behind, lambda i: along_ring(i, -1))
        return ahead, behind, [ahead, other_core(ahead), behind, other_core(behind)]

    rows = [x, other_core(x)]
    ahead, behind, first = round_of(x, x)
    ahead, behind, second = round_of(ahead, behind)
    column = exchange(ahead, behind, rows[1], first[1], first[3])
    yield column
    ahead, behind, third = round_of(ahead, behind)
    far = permute(after(ahead, column), lambda i: along_ring(i, 1))
    made = yield rows + first + second + third
    far = after(far, made)
    yield [far, other_core(far)]


def place_of(offset, dropped):
    named = jnp.logical_and(offset <= 2 * REACH, offset != dropped)
    slot = offset - jnp.where(offset > dropped, 1, 0)
    return jnp.clip(slot, 0, 2 * REACH - 1), named


def dropped_offset(cols, row, total):
    offsets = jnp.mod(cols - row + REACH, total)
    return REACH * (2 * REACH + 1) - jnp.sum(offsets, axis=1)


def pack_kernel(total, info_ref, cols_ref, cur_ref, prev_ref, send_ref, cur, prev, zeros, note, sems):
    row = info_ref[0]
    drop = info_ref[2]
    count, size = cur.shape[:2]
    loads = (
        pltpu.make_async_copy(cur_ref, cur, sems.at[0]),
        pltpu.make_async_copy(prev_ref, prev, sems.at[1]),
    )
    for load in loads:
        load.start()
    zeros[...] = jnp.zeros_like(zeros)
    line = lax.broadcasted_iota(jnp.int32, note.shape, 0)
    note[...] = jnp.where(line == 0, info_ref[1], drop).astype(jnp.float32)

    def fill(j, carry):
        offset = lax.rem(j - row + REACH + total, total)
        _, named = place_of(offset, drop)
        pltpu.make_async_copy(note, send_ref.at[j, pl.ds(2 * size, NOTE)], sems.at[2]).start()

        @pl.when(jnp.logical_not(named))
        def _():
            pltpu.make_async_copy(zeros, send_ref.at[j, pl.ds(0, 2 * size)], sems.at[2]).start()

        return carry

    lax.fori_loop(0, total, fill, 0)
    for which, held in enumerate((cur, prev)):
        loads[which].wait()
        for k in range(count):
            place = send_ref.at[cols_ref[k], pl.ds(which * size, size)]
            pltpu.make_async_copy(held.at[k], place, sems.at[2]).start()
    pltpu.make_async_copy(send_ref, send_ref, sems.at[2]).wait()


def split(x):
    high = x.astype(jnp.bfloat16)
    low = (x - high.astype(jnp.float32)).astype(jnp.bfloat16)
    return high, low


class Rows:
    def __init__(self, total, me_ref, table_ref):
        self.me = me_ref[0]
        self.table_ref = table_ref
        self.window = table_ref.shape[0] // total

    def __getitem__(self, w):
        return self.table_ref[self.me * self.window + w]


def kept_rows(total, rows, drops_ref, w):
    row = rows[w]
    offset = lax.rem(rows.me - row + REACH + total, total)
    _, named = place_of(offset, drops_ref[2 * row + 1])
    return named


def fill_pair(pair, block, w):
    size = block.shape[-1]
    high, low = split(block)
    at = pl.ds(pl.multiple_of(w * size, size), size)
    pair[at, pl.ds(0, size)] = high
    pair[at, pl.ds(size, size)] = low


def products_of(rows, pair):
    group, double = rows.shape[:2]
    size = double // 2
    products = jnp.dot(rows.reshape(group * double, rows.shape[2]), pair, preferred_element_type=jnp.float32)
    for r in range(group):
        parts = products[r * double:r * double + size] + products[r * double + size:(r + 1) * double]
        yield parts[:, :size] + parts[:, size:]


def first_kernel(total, window, start, count, group, drops_ref, me_ref, table_ref, t_ref, *refs):
    rows = Rows(total, me_ref, table_ref)
    h_refs = refs[:count]
    if start:
        pair_in, _ = refs[count:count + 2]
        dense_ref, out_ref = refs[count + 2:count + 4]
    else:
        dense_ref, out_ref, pair_out, blocks = refs[count:count + 4]
    stage, dense, prev, pair, h_sem, t_sem, prev_sem, pair_sem, dense_sem, out_sem = refs[-10:]
    size = t_ref.shape[-1]
    kept = functools.partial(kept_rows, total, rows, drops_ref)

    if start:
        pltpu.make_async_copy(pair_in, pair, pair_sem).start()
    else:
        for w in range(window):
            pltpu.make_async_copy(t_ref.at[rows[w], pl.ds(0, size)], blocks.at[w], t_sem).start()
    for r in range(count):
        pltpu.make_async_copy(h_refs[r], stage.at[r], h_sem.at[r]).start()
    for r in range(count):
        block = t_ref.at[rows[start + r], pl.ds(size, size)]
        pltpu.make_async_copy(block, prev.at[r], prev_sem).start()
    if not start:
        pltpu.make_async_copy(blocks, blocks, t_sem).wait()
        for w in range(window):
            fill_pair(pair, jnp.where(kept(w), blocks[w], 0.0), w)
        pltpu.make_async_copy(pair, pair_out, pair_sem).start()

    def densify(r, slot, place):
        row = rows[start + r]
        drop = drops_ref[2 * row]
        for p in range(window):
            offset = lax.rem(rows[p] - row + REACH + total, total)
            k, named = place_of(offset, drop)
            high, low = split(jnp.where(named, stage[r, k], 0.0))
            dense[slot, place, pl.ds(0, size), pl.ds(p * size, size)] = high
            dense[slot, place, pl.ds(size, size), pl.ds(p * size, size)] = low

    def store(g, slot):
        return pltpu.make_async_copy(dense.at[slot], dense_ref.at[pl.ds(g * group, group)], dense_sem.at[slot])

    groups = count // group

    def one(g, carry):
        slot = lax.rem(g, 2)

        @pl.when(g >= 2)
        def _():
            store(g - 2, slot).wait()

        for place in range(group):
            r = g * group + place
            pltpu.make_async_copy(stage.at[r], stage.at[r], h_sem.at[r]).wait()
            densify(r, slot, place)
        store(g, slot).start()
        if start:

            @pl.when(g == 0)
            def _():
                pltpu.make_async_copy(pair, pair, pair_sem).wait()

        @pl.when(g == 0)
        def _():
            pltpu.make_async_copy(prev, prev, prev_sem).wait()

        for place, product in enumerate(products_of(dense[slot], pair[...])):
            r = g * group + place
            prev[r] = jnp.where(kept(start + r), 2.0 * product - prev[r], 0.0)
            pltpu.make_async_copy(prev.at[r], out_ref.at[rows[start + r]], out_sem).start()
        return carry

    lax.fori_loop(0, groups, one, 0)
    for g in range(max(groups - 2, 0), groups):
        store(g, g % 2).wait()
    if not start:
        pltpu.make_async_copy(pair, pair, pair_sem).wait()
    pltpu.make_async_copy(prev, prev, out_sem).wait()


def later_kernel(total, window, group, parts, drops_ref, me_ref, table_ref, *refs):
    rows = Rows(total, me_ref, table_ref)
    dense_refs = refs[:len(parts)]
    t_ref, first_ref, out_ref, dense, terms, pairs, dense_sem, t_sem, first_sem, out_sem = refs[len(parts):]
    size = terms.shape[-1]
    groups = window // group
    kept = functools.partial(kept_rows, total, rows, drops_ref)
    for w in range(window):
        pltpu.make_async_copy(first_ref.at[rows[w]], terms.at[w, 1], first_sem).start()
    start = 0
    for part, dense_ref in zip(parts, dense_refs):
        for w in range(start, start + part):
            pltpu.make_async_copy(dense_ref.at[w - start], dense.at[w], dense_sem.at[w // group]).start()
        start += part
    for w in range(window):
        pltpu.make_async_copy(t_ref.at[rows[w], pl.ds(0, size)], terms.at[w, 0], t_sem).start()
    pltpu.make_async_copy(terms.at[:, 1], terms.at[:, 1], first_sem).wait()
    for w in range(window):
        fill_pair(pairs.at[0], terms[w, 1], w)
    pltpu.make_async_copy(terms.at[:, 0], terms.at[:, 0], t_sem).wait()

    def one(g, carry, step):
        held = dense.at[pl.ds(g * group, group)]
        if step == 0:
            pltpu.make_async_copy(held, held, dense_sem.at[g]).wait()
        for r, product in enumerate(products_of(held[...], pairs[step])):
            w = g * group + r
            newest = jnp.where(kept(w), 2.0 * product - terms[w, step], 0.0)
            terms[w, step] = newest
            if step == 0:
                fill_pair(pairs.at[1], newest, w)
            pltpu.make_async_copy(terms.at[w, step], out_ref.at[rows[w], step], out_sem).start()
        return carry

    for step in range(2):
        lax.fori_loop(0, groups, functools.partial(one, step=step), 0)
    pltpu.make_async_copy(terms, terms, out_sem).wait()


def unpack_first_kernel(cols_ref, coefs_ref, first_ref, density_ref, out_ref, sums, one, sems):
    load = pltpu.make_async_copy(density_ref, sums, sems.at[0])
    load.start()
    for k in range(cols_ref.shape[0]):
        pltpu.make_async_copy(first_ref.at[cols_ref[k]], one.at[k], sems.at[1]).start()
    load.wait()
    pltpu.make_async_copy(one, one, sems.at[1]).wait()
    sums[...] += coefs_ref[0] * one[...]
    store = pltpu.make_async_copy(sums, out_ref, sems.at[0])
    store.start()
    store.wait()


def unpack_last_kernel(cols_ref, coefs_ref, held_ref, sum_ref, density_ref, last_ref, before_ref, sums, two, three, sems):
    load = pltpu.make_async_copy(sum_ref, sums, sems.at[0])
    load.start()
    for place, sem, which in ((two, 1, 0), (three, 2, 1)):
        for k in range(cols_ref.shape[0]):
            pltpu.make_async_copy(held_ref.at[cols_ref[k], which], place.at[k], sems.at[sem]).start()
    pltpu.make_async_copy(two, two, sems.at[1]).wait()
    before = pltpu.make_async_copy(two, before_ref, sems.at[1])
    before.start()
    pltpu.make_async_copy(three, three, sems.at[2]).wait()
    last = pltpu.make_async_copy(three, last_ref, sems.at[2])
    last.start()
    load.wait()
    sums[...] = sums[...] + coefs_ref[1] * two[...] + coefs_ref[2] * three[...]
    store = pltpu.make_async_copy(sums, density_ref, sems.at[0])
    store.start()
    before.wait()
    last.wait()
    store.wait()


def per_device(h_blocks, h_cols, term_prev, term_cur, t_cols, density_in, coefs):
    total = lax.axis_size("row")
    me = lax.axis_index("row")
    count, size = h_blocks.shape[1:3]
    drop_h = dropped_offset(h_cols, me, total)
    drop_t = dropped_offset(t_cols, me, total)
    f32, bf16 = jnp.float32, jnp.bfloat16
    dma = pltpu.SemaphoreType.DMA
    row = jax.ShapeDtypeStruct((count, size, size), f32)
    row_scratch = pltpu.VMEM(row.shape, f32)

    def call(kernel, smem, arrays, outs, scratch, name, megabytes, aliases={}):
        return pl.pallas_call(
            kernel,
            out_shape=[pltpu.HBM(out.shape, out.dtype) for out in outs],
            in_specs=[SMEM] * len(smem) + [ANY] * len(arrays),
            out_specs=[ANY] * len(outs),
            scratch_shapes=scratch,
            input_output_aliases=aliases,
            compiler_params=pltpu.CompilerParams(vmem_limit_bytes=megabytes * 1024 * 1024),
            name=name,
        )(*smem, *arrays)

    def exchange(x):
        return lax.all_to_all(x, "row", 0, 0, tiled=True)

    (send,) = call(
        functools.partial(pack_kernel, total),
        [jnp.stack([me, drop_h[0], drop_t[0]]), t_cols[0]],
        [term_cur[0], term_prev[0]],
        [jax.ShapeDtypeStruct((total, 2 * size + NOTE, size), f32)],
        [
            row_scratch,
            row_scratch,
            pltpu.VMEM((2 * size, size), f32),
            pltpu.VMEM((NOTE, size), f32),
            dma((3,)),
        ],
        "pack",
        60,
    )
    table, parts = window_table(total)
    gathered = gathered_rows(h_blocks[0], total, lambda *others: exchange(after(send, *others)))
    column = next(gathered)
    drops = column[:, 2 * size:2 * size + 2, 0].astype(jnp.int32).reshape(-1)
    rows = jnp.array(table, jnp.int32).reshape(-1)
    window = sum(parts)
    dense_shape = (window, 2 * size, window * size)
    pair_shape = (window * size, 2 * size)
    dense = []
    start = 0
    for part in parts:
        h_rows = gathered.send(dense[-1] if start else None)
        group = max(g for g in (2, 7, 13) if part % g == 0)
        scratch = [
            pltpu.VMEM((part, count, size, size), f32),
            pltpu.VMEM((min(2, part // group), group) + dense_shape[1:], bf16),
            pltpu.VMEM((part, size, size), f32),
            pltpu.VMEM(pair_shape, bf16),
            dma((part,)),
            dma,
            dma,
            dma,
            dma((2,)),
            dma,
        ]
        if not start:
            scratch = [pltpu.VMEM((window, size, size), f32)] + scratch
        result = call(
            functools.partial(first_kernel, total, window, start, part, group),
            [drops, me[None], rows],
            [column, *h_rows] + ([pair, term1] if start else []),
            [
                jax.ShapeDtypeStruct((part,) + dense_shape[1:], bf16),
                jax.ShapeDtypeStruct((total, size, size), f32),
            ] + ([] if start else [jax.ShapeDtypeStruct(pair_shape, bf16)]),
            scratch,
            "first",
            60,
            {part + 5: 1} if start else {},
        )
        dense.append(result[0])
        term1 = result[1]
        if not start:
            pair = result[2]
        start += part
    back1 = exchange(term1)
    group = max(g for g in (3, 4) if window % g == 0)
    (terms,) = call(
        functools.partial(later_kernel, total, window, group, parts),
        [drops, me[None], rows],
        [*dense, column, term1],
        [jax.ShapeDtypeStruct((total, 2, size, size), f32)],
        [
            pltpu.VMEM(dense_shape, bf16),
            pltpu.VMEM((window, 2, size, size), f32),
            pltpu.VMEM((2,) + pair_shape, bf16),
            dma((window // group,)),
            dma,
            dma,
            dma,
        ],
        "later",
        60,
    )
    back = exchange(after(terms, back1))
    (sums,) = call(
        unpack_first_kernel,
        [t_cols[0], coefs],
        [back1, density_in[0]],
        [row],
        [row_scratch, row_scratch, dma((2,))],
        "unpack_first",
        60,
    )
    density, last, before = call(
        unpack_last_kernel,
        [t_cols[0], coefs],
        [back, sums],
        [row] * 3,
        [row_scratch, row_scratch, row_scratch, dma((3,))],
        "unpack_last",
        60,
    )
    return density[None], last[None], before[None]


def solution(mesh):
    blocks = P(("groups", "row"), None, None, None)
    cols = P(("groups", "row"), None)
    return jax.shard_map(
        per_device,
        mesh=mesh,
        in_specs=(blocks, cols, blocks, blocks, cols, blocks, P()),
        out_specs=(blocks, blocks, blocks),
        check_vma=False,
    )
```

```python
import functools

import jax
import jax.numpy as jnp
from jax import lax
from jax.experimental import pallas as pl
from jax.experimental.pallas import tpu as pltpu
from jax.sharding import PartitionSpec as P

REACH = 7
NOTE = 8
LAST = 2
SMEM = pl.BlockSpec(memory_space=pltpu.SMEM)
ANY = pl.BlockSpec(memory_space=pl.ANY)


def permute(x, target):
    devices = lax.axis_size("row")
    return lax.ppermute(x, "row", [(i, target(i)) for i in range(devices)])


def after(x, *others):
    return lax.optimization_barrier((x, *others))[0]


RING = (0, 2, 4, 6, 7, 5, 3, 1)


def along_ring(device, by):
    if device % 2:
        by = -by
    return 2 * RING[(RING.index(device // 2) + by) % len(RING)] + device % 2


def window_table(total):
    if total != 16:
        steps = [0] + [by for hop in range(1, REACH + 1) for by in (-hop, hop)]
        return [[(i + by) % total for by in steps] for i in range(total)], (13, LAST)
    order = (0, -1, 1, -2, 2, -3, 3, -4)
    table = [[along_ring(source, by) for by in order for source in (i, i ^ 1)] for i in range(total)]
    return table, (14, LAST)


def gathered_rows(x, total, exchange):
    if total != 16:
        rows = [x]
        for hop in range(1, REACH + 1):
            for by in (hop, -hop):
                rows.append(permute(x, lambda i, by=by: (i + by) % total))
        yield exchange()
        yield rows[:13]
        yield rows[13:]
        return

    def other_core(row):
        return permute(row, lambda i: i ^ 1)

    def round_of(ahead, behind):
        ahead = permute(ahead, lambda i: along_ring(i, 1))
        behind = permute(behind, lambda i: along_ring(i, -1))
        return ahead, behind, [ahead, other_core(ahead), behind, other_core(behind)]

    rows = [x, other_core(x)]
    ahead, behind, first = round_of(x, x)
    ahead, behind, second = round_of(ahead, behind)
    column = exchange(ahead, behind, rows[1], first[1], first[3])
    yield column
    ahead, behind, third = round_of(ahead, behind)
    far = permute(after(ahead, column), lambda i: along_ring(i, 1))
    made = yield rows + first + second + third
    far = after(far, made)
    yield [far, other_core(far)]


def place_of(offset, dropped):
    named = jnp.logical_and(offset <= 2 * REACH, offset != dropped)
    slot = offset - jnp.where(offset > dropped, 1, 0)
    return jnp.clip(slot, 0, 2 * REACH - 1), named


def dropped_offset(cols, row, total):
    offsets = jnp.mod(cols - row + REACH, total)
    return REACH * (2 * REACH + 1) - jnp.sum(offsets, axis=1)


def pack_kernel(total, info_ref, cols_ref, cur_ref, prev_ref, send_ref, cur, prev, zeros, note, sems):
    row = info_ref[0]
    drop = info_ref[2]
    count, size = cur.shape[:2]
    loads = (
        pltpu.make_async_copy(cur_ref, cur, sems.at[0]),
        pltpu.make_async_copy(prev_ref, prev, sems.at[1]),
    )
    for load in loads:
        load.start()
    zeros[...] = jnp.zeros_like(zeros)
    line = lax.broadcasted_iota(jnp.int32, note.shape, 0)
    note[...] = jnp.where(line == 0, info_ref[1], drop).astype(jnp.float32)

    def fill(j, carry):
        offset = lax.rem(j - row + REACH + total, total)
        _, named = place_of(offset, drop)
        pltpu.make_async_copy(note, send_ref.at[j, pl.ds(2 * size, NOTE)], sems.at[2]).start()

        @pl.when(jnp.logical_not(named))
        def _():
            pltpu.make_async_copy(zeros, send_ref.at[j, pl.ds(0, 2 * size)], sems.at[2]).start()

        return carry

    lax.fori_loop(0, total, fill, 0)
    for which, held in enumerate((cur, prev)):
        loads[which].wait()
        for k in range(count):
            place = send_ref.at[cols_ref[k], pl.ds(which * size, size)]
            pltpu.make_async_copy(held.at[k], place, sems.at[2]).start()
    pltpu.make_async_copy(send_ref, send_ref, sems.at[2]).wait()


def split(x):
    high = x.astype(jnp.bfloat16)
    low = (x - high.astype(jnp.float32)).astype(jnp.bfloat16)
    return high, low


class Rows:
    def __init__(self, total, me_ref, table_ref):
        self.me = me_ref[0]
        self.table_ref = table_ref
        self.window = table_ref.shape[0] // total

    def __getitem__(self, w):
        return self.table_ref[self.me * self.window + w]


def kept_rows(total, rows, drops_ref, w):
    row = rows[w]
    offset = lax.rem(rows.me - row + REACH + total, total)
    _, named = place_of(offset, drops_ref[2 * row + 1])
    return named


def fill_pair(pair, block, w):
    size = block.shape[-1]
    high, low = split(block)
    at = pl.ds(pl.multiple_of(w * size, size), size)
    pair[at, pl.ds(0, size)] = high
    pair[at, pl.ds(size, size)] = low


def products_of(rows, pair):
    group, double = rows.shape[:2]
    size = double // 2
    products = jnp.dot(rows.reshape(group * double, rows.shape[2]), pair, preferred_element_type=jnp.float32)
    for r in range(group):
        parts = products[r * double:r * double + size] + products[r * double + size:(r + 1) * double]
        yield parts[:, :size] + parts[:, size:]


def first_kernel(total, window, start, count, group, drops_ref, me_ref, table_ref, t_ref, *refs):
    rows = Rows(total, me_ref, table_ref)
    h_refs = refs[:count]
    if start:
        pair_in, dense_ref, out_ref = refs[count:count + 3]
    else:
        dense_ref, out_ref, pair_out, blocks = refs[count:count + 4]
    stage, dense, prev, pair, h_sem, t_sem, prev_sem, pair_sem, dense_sem, out_sem = refs[-10:]
    size = t_ref.shape[-1]
    kept = functools.partial(kept_rows, total, rows, drops_ref)

    if start:
        pltpu.make_async_copy(pair_in, pair, pair_sem).start()
    else:
        for w in range(window):
            pltpu.make_async_copy(t_ref.at[rows[w], pl.ds(0, size)], blocks.at[w], t_sem).start()
    for r in range(count):
        pltpu.make_async_copy(h_refs[r], stage.at[r], h_sem.at[r]).start()
    for r in range(count):
        block = t_ref.at[rows[start + r], pl.ds(size, size)]
        pltpu.make_async_copy(block, prev.at[r], prev_sem).start()
    if not start:
        pltpu.make_async_copy(blocks, blocks, t_sem).wait()
        for w in range(window):
            fill_pair(pair, jnp.where(kept(w), blocks[w], 0.0), w)
        pltpu.make_async_copy(pair, pair_out, pair_sem).start()

    def densify(r, slot, place):
        row = rows[start + r]
        drop = drops_ref[2 * row]
        for p in range(window):
            offset = lax.rem(rows[p] - row + REACH + total, total)
            k, named = place_of(offset, drop)
            high, low = split(jnp.where(named, stage[r, k], 0.0))
            dense[slot, place, pl.ds(0, size), pl.ds(p * size, size)] = high
            dense[slot, place, pl.ds(size, size), pl.ds(p * size, size)] = low

    def store(g, slot):
        return pltpu.make_async_copy(dense.at[slot], dense_ref.at[pl.ds(g * group, group)], dense_sem.at[slot])

    groups = count // group

    def one(g, carry):
        slot = lax.rem(g, 2)

        @pl.when(g >= 2)
        def _():
            store(g - 2, slot).wait()

        for place in range(group):
            r = g * group + place
            pltpu.make_async_copy(stage.at[r], stage.at[r], h_sem.at[r]).wait()
            densify(r, slot, place)
        store(g, slot).start()
        if start:

            @pl.when(g == 0)
            def _():
                pltpu.make_async_copy(pair, pair, pair_sem).wait()

        @pl.when(g == 0)
        def _():
            pltpu.make_async_copy(prev, prev, prev_sem).wait()

        for place, product in enumerate(products_of(dense[slot], pair[...])):
            r = g * group + place
            prev[r] = jnp.where(kept(start + r), 2.0 * product - prev[r], 0.0)
            block = out_ref.at[r if start else rows[start + r]]
            pltpu.make_async_copy(prev.at[r], block, out_sem).start()
        return carry

    lax.fori_loop(0, groups, one, 0)
    for g in range(max(groups - 2, 0), groups):
        store(g, g % 2).wait()
    if not start:
        pltpu.make_async_copy(pair, pair, pair_sem).wait()
    pltpu.make_async_copy(prev, prev, out_sem).wait()


def later_kernel(total, window, group, parts, drops_ref, me_ref, table_ref, *refs):
    rows = Rows(total, me_ref, table_ref)
    dense_refs = refs[:len(parts)]
    t_ref, first_ref, last_ref, out_ref, dense, terms, pairs, dense_sem, t_sem, first_sem, out_sem = refs[len(parts):]
    size = terms.shape[-1]
    groups = window // group
    kept = functools.partial(kept_rows, total, rows, drops_ref)
    for w in range(window):
        late = w - (window - LAST)
        source = first_ref.at[rows[w]] if late < 0 else last_ref.at[late]
        pltpu.make_async_copy(source, terms.at[w, 1], first_sem).start()
    start = 0
    for part, dense_ref in zip(parts, dense_refs):
        for w in range(start, start + part):
            pltpu.make_async_copy(dense_ref.at[w - start], dense.at[w], dense_sem.at[w // group]).start()
        start += part
    for w in range(window):
        pltpu.make_async_copy(t_ref.at[rows[w], pl.ds(0, size)], terms.at[w, 0], t_sem).start()
    pltpu.make_async_copy(terms.at[:, 1], terms.at[:, 1], first_sem).wait()
    for w in range(window):
        fill_pair(pairs.at[0], terms[w, 1], w)
    pltpu.make_async_copy(terms.at[:, 0], terms.at[:, 0], t_sem).wait()

    def one(g, carry, step):
        held = dense.at[pl.ds(g * group, group)]
        if step == 0:
            pltpu.make_async_copy(held, held, dense_sem.at[g]).wait()
        for r, product in enumerate(products_of(held[...], pairs[step])):
            w = g * group + r
            newest = jnp.where(kept(w), 2.0 * product - terms[w, step], 0.0)
            terms[w, step] = newest
            if step == 0:
                fill_pair(pairs.at[1], newest, w)
            pltpu.make_async_copy(terms.at[w, step], out_ref.at[rows[w], step], out_sem).start()
        return carry

    for step in range(2):
        lax.fori_loop(0, groups, functools.partial(one, step=step), 0)
    pltpu.make_async_copy(terms, terms, out_sem).wait()


def unpack_first_kernel(
    cols_ref, me_ref, sources_ref, coefs_ref, first_ref, density_ref, *refs
):
    late_refs = refs[:LAST]
    out_ref, sums, one, sems = refs[LAST:]
    load = pltpu.make_async_copy(density_ref, sums, sems.at[0])
    load.start()
    late = [sources_ref[me_ref[0] * LAST + r] for r in range(LAST)]
    for k in range(cols_ref.shape[0]):
        col = cols_ref[k]
        early = jnp.logical_and(col != late[0], col != late[1])
        choices = [(early, first_ref.at[col])] + [(col == late[r], late_refs[r]) for r in range(LAST)]
        for chosen, source in choices:

            @pl.when(chosen)
            def _(source=source, k=k):
                pltpu.make_async_copy(source, one.at[k], sems.at[1]).start()

    load.wait()
    pltpu.make_async_copy(one, one, sems.at[1]).wait()
    sums[...] += coefs_ref[0] * one[...]
    store = pltpu.make_async_copy(sums, out_ref, sems.at[0])
    store.start()
    store.wait()


def unpack_last_kernel(cols_ref, coefs_ref, held_ref, sum_ref, density_ref, last_ref, before_ref, sums, two, three, sems):
    load = pltpu.make_async_copy(sum_ref, sums, sems.at[0])
    load.start()
    for place, sem, which in ((two, 1, 0), (three, 2, 1)):
        for k in range(cols_ref.shape[0]):
            pltpu.make_async_copy(held_ref.at[cols_ref[k], which], place.at[k], sems.at[sem]).start()
    pltpu.make_async_copy(two, two, sems.at[1]).wait()
    before = pltpu.make_async_copy(two, before_ref, sems.at[1])
    before.start()
    pltpu.make_async_copy(three, three, sems.at[2]).wait()
    last = pltpu.make_async_copy(three, last_ref, sems.at[2])
    last.start()
    load.wait()
    sums[...] = sums[...] + coefs_ref[1] * two[...] + coefs_ref[2] * three[...]
    store = pltpu.make_async_copy(sums, density_ref, sems.at[0])
    store.start()
    before.wait()
    last.wait()
    store.wait()


def per_device(h_blocks, h_cols, term_prev, term_cur, t_cols, density_in, coefs):
    total = lax.axis_size("row")
    me = lax.axis_index("row")
    count, size = h_blocks.shape[1:3]
    drop_h = dropped_offset(h_cols, me, total)
    drop_t = dropped_offset(t_cols, me, total)
    f32, bf16 = jnp.float32, jnp.bfloat16
    dma = pltpu.SemaphoreType.DMA
    row = jax.ShapeDtypeStruct((count, size, size), f32)
    row_scratch = pltpu.VMEM(row.shape, f32)

    def call(kernel, smem, arrays, outs, scratch, name, megabytes, aliases={}):
        return pl.pallas_call(
            kernel,
            out_shape=[pltpu.HBM(out.shape, out.dtype) for out in outs],
            in_specs=[SMEM] * len(smem) + [ANY] * len(arrays),
            out_specs=[ANY] * len(outs),
            scratch_shapes=scratch,
            input_output_aliases=aliases,
            compiler_params=pltpu.CompilerParams(vmem_limit_bytes=megabytes * 1024 * 1024),
            name=name,
        )(*smem, *arrays)

    def exchange(x):
        return lax.all_to_all(x, "row", 0, 0, tiled=True)

    (send,) = call(
        functools.partial(pack_kernel, total),
        [jnp.stack([me, drop_h[0], drop_t[0]]), t_cols[0]],
        [term_cur[0], term_prev[0]],
        [jax.ShapeDtypeStruct((total, 2 * size + NOTE, size), f32)],
        [
            row_scratch,
            row_scratch,
            pltpu.VMEM((2 * size, size), f32),
            pltpu.VMEM((NOTE, size), f32),
            dma((3,)),
        ],
        "pack",
        60,
    )
    table, parts = window_table(total)
    gathered = gathered_rows(h_blocks[0], total, lambda *others: exchange(after(send, *others)))
    column = next(gathered)
    drops = column[:, 2 * size:2 * size + 2, 0].astype(jnp.int32).reshape(-1)
    rows = jnp.array(table, jnp.int32).reshape(-1)
    window = sum(parts)
    dense_shape = (window, 2 * size, window * size)
    pair_shape = (window * size, 2 * size)
    dense = []
    start = 0
    for part in parts:
        h_rows = gathered.send(dense[-1] if start else None)
        group = max(g for g in (2, 7, 13) if part % g == 0)
        scratch = [
            pltpu.VMEM((part, count, size, size), f32),
            pltpu.VMEM((min(2, part // group), group) + dense_shape[1:], bf16),
            pltpu.VMEM((part, size, size), f32),
            pltpu.VMEM(pair_shape, bf16),
            dma((part,)),
            dma,
            dma,
            dma,
            dma((2,)),
            dma,
        ]
        if not start:
            scratch = [pltpu.VMEM((window, size, size), f32)] + scratch
        result = call(
            functools.partial(first_kernel, total, window, start, part, group),
            [drops, me[None], rows],
            [column, *h_rows] + ([pair] if start else []),
            [
                jax.ShapeDtypeStruct((part,) + dense_shape[1:], bf16),
                jax.ShapeDtypeStruct((LAST if start else total, size, size), f32),
            ]
            + ([] if start else [jax.ShapeDtypeStruct(pair_shape, bf16)]),
            scratch,
            "first",
            60,
        )
        dense.append(result[0])
        if start:
            late1 = result[1]
        else:
            term1, pair = result[1:]
        start += part
    back1 = exchange(term1)
    targets = [[row[window - LAST + r] for row in table] for r in range(LAST)]
    late_back = [permute(late1[r], lambda i, r=r: targets[r][i]) for r in range(LAST)]
    sources = jnp.array([[to.index(i) for to in targets] for i in range(total)], jnp.int32).reshape(-1)
    group = max(g for g in (3, 4) if window % g == 0)
    (terms,) = call(
        functools.partial(later_kernel, total, window, group, parts),
        [drops, me[None], rows],
        [*dense, column, term1, late1],
        [jax.ShapeDtypeStruct((total, 2, size, size), f32)],
        [
            pltpu.VMEM(dense_shape, bf16),
            pltpu.VMEM((window, 2, size, size), f32),
            pltpu.VMEM((2,) + pair_shape, bf16),
            dma((window // group,)),
            dma,
            dma,
            dma,
        ],
        "later",
        60,
    )
    back = exchange(after(terms, back1, *late_back))
    (sums,) = call(
        unpack_first_kernel,
        [t_cols[0], me[None], sources, coefs],
        [back1, density_in[0], *late_back],
        [row],
        [row_scratch, row_scratch, dma((2,))],
        "unpack_first",
        60,
    )
    density, last, before = call(
        unpack_last_kernel,
        [t_cols[0], coefs],
        [back, sums],
        [row] * 3,
        [row_scratch, row_scratch, row_scratch, dma((3,))],
        "unpack_last",
        60,
    )
    return density[None], last[None], before[None]


def solution(mesh):
    blocks = P(("groups", "row"), None, None, None)
    cols = P(("groups", "row"), None)
    return jax.shard_map(
        per_device,
        mesh=mesh,
        in_specs=(blocks, cols, blocks, blocks, cols, blocks, P()),
        out_specs=(blocks, blocks, blocks),
        check_vma=False,
    )
```

```python
import functools

import jax
import jax.numpy as jnp
from jax import lax
from jax.experimental import pallas as pl
from jax.experimental.pallas import tpu as pltpu
from jax.sharding import PartitionSpec as P

REACH = 7
NOTE = 8
LAST = 2
SMEM = pl.BlockSpec(memory_space=pltpu.SMEM)
ANY = pl.BlockSpec(memory_space=pl.ANY)


def permute(x, target):
    devices = lax.axis_size("row")
    return lax.ppermute(x, "row", [(i, target(i)) for i in range(devices)])


def after(x, *others):
    return lax.optimization_barrier((x, *others))[0]


RING = (0, 2, 4, 6, 7, 5, 3, 1)


def along_ring(device, by):
    if device % 2:
        by = -by
    return 2 * RING[(RING.index(device // 2) + by) % len(RING)] + device % 2


def window_table(total):
    if total != 16:
        steps = [0] + [by for hop in range(1, REACH + 1) for by in (-hop, hop)]
        return [[(i + by) % total for by in steps] for i in range(total)], (13, LAST)
    order = (0, -1, 1, -2, 2, -3, 3, -4)
    table = [[along_ring(source, by) for by in order for source in (i, i ^ 1)] for i in range(total)]
    return table, (14, LAST)


def gathered_rows(x, total, exchange):
    if total != 16:
        rows = [x]
        for hop in range(1, REACH + 1):
            for by in (hop, -hop):
                rows.append(permute(x, lambda i, by=by: (i + by) % total))
        yield exchange()
        yield rows[:13]
        yield rows[13:]
        return

    def other_core(row):
        return permute(row, lambda i: i ^ 1)

    def round_of(ahead, behind):
        ahead = permute(ahead, lambda i: along_ring(i, 1))
        behind = permute(behind, lambda i: along_ring(i, -1))
        return ahead, behind, [ahead, other_core(ahead), behind, other_core(behind)]

    rows = [x, other_core(x)]
    ahead, behind, first = round_of(x, x)
    ahead, behind, second = round_of(ahead, behind)
    column = exchange(ahead, behind, rows[1], first[1], first[3])
    yield column
    ahead, behind, third = round_of(ahead, behind)
    far = permute(after(ahead, column), lambda i: along_ring(i, 1))
    made = yield rows + first + second + third
    far = after(far, made)
    yield [far, other_core(far)]


def place_of(offset, dropped):
    named = jnp.logical_and(offset <= 2 * REACH, offset != dropped)
    slot = offset - jnp.where(offset > dropped, 1, 0)
    return jnp.clip(slot, 0, 2 * REACH - 1), named


def dropped_offset(cols, row, total):
    offsets = jnp.mod(cols - row + REACH, total)
    return REACH * (2 * REACH + 1) - jnp.sum(offsets, axis=1)


def pack_kernel(total, info_ref, cols_ref, cur_ref, prev_ref, send_ref, cur, prev, zeros, note, sems):
    row = info_ref[0]
    drop = info_ref[2]
    count, size = cur.shape[:2]
    loads = (
        pltpu.make_async_copy(cur_ref, cur, sems.at[0]),
        pltpu.make_async_copy(prev_ref, prev, sems.at[1]),
    )
    for load in loads:
        load.start()
    zeros[...] = jnp.zeros_like(zeros)
    line = lax.broadcasted_iota(jnp.int32, note.shape, 0)
    note[...] = jnp.where(line == 0, info_ref[1], drop).astype(jnp.float32)

    def fill(j, carry):
        offset = lax.rem(j - row + REACH + total, total)
        _, named = place_of(offset, drop)
        pltpu.make_async_copy(note, send_ref.at[j, pl.ds(2 * size, NOTE)], sems.at[2]).start()

        @pl.when(jnp.logical_not(named))
        def _():
            pltpu.make_async_copy(zeros, send_ref.at[j, pl.ds(0, 2 * size)], sems.at[2]).start()

        return carry

    lax.fori_loop(0, total, fill, 0)
    for which, held in enumerate((cur, prev)):
        loads[which].wait()
        for k in range(count):
            place = send_ref.at[cols_ref[k], pl.ds(which * size, size)]
            pltpu.make_async_copy(held.at[k], place, sems.at[2]).start()
    pltpu.make_async_copy(send_ref, send_ref, sems.at[2]).wait()


def split(x):
    high = x.astype(jnp.bfloat16)
    low = (x - high.astype(jnp.float32)).astype(jnp.bfloat16)
    return high, low


class Rows:
    def __init__(self, total, me_ref, table_ref):
        self.me = me_ref[0]
        self.table_ref = table_ref
        self.window = table_ref.shape[0] // total

    def __getitem__(self, w):
        return self.table_ref[self.me * self.window + w]


def kept_rows(total, rows, drops_ref, w):
    row = rows[w]
    offset = lax.rem(rows.me - row + REACH + total, total)
    _, named = place_of(offset, drops_ref[2 * row + 1])
    return named


def fill_pair(pair, block, w):
    size = block.shape[-1]
    high, low = split(block)
    at = pl.ds(pl.multiple_of(w * size, size), size)
    pair[at, pl.ds(0, size)] = high
    pair[at, pl.ds(size, size)] = low


def products_of(rows, pair):
    group, double = rows.shape[:2]
    size = double // 2
    products = jnp.dot(rows.reshape(group * double, rows.shape[2]), pair, preferred_element_type=jnp.float32)
    for r in range(group):
        parts = products[r * double:r * double + size] + products[r * double + size:(r + 1) * double]
        yield parts[:, :size] + parts[:, size:]


def first_kernel(total, window, start, count, group, drops_ref, me_ref, table_ref, t_ref, *refs):
    rows = Rows(total, me_ref, table_ref)
    h_refs = refs[:count]
    if start:
        pair_in, dense_ref, *outs = refs[count:count + 2 + LAST]
    else:
        dense_ref, out_ref, pair_out, blocks = refs[count:count + 4]
    stage, dense, prev, pair, h_sem, t_sem, prev_sem, pair_sem, dense_sem, out_sem = refs[-10:]
    size = t_ref.shape[-1]
    kept = functools.partial(kept_rows, total, rows, drops_ref)

    if start:
        pltpu.make_async_copy(pair_in, pair, pair_sem).start()
    else:
        for w in range(window):
            pltpu.make_async_copy(t_ref.at[rows[w], pl.ds(0, size)], blocks.at[w], t_sem).start()
    for r in range(count):
        pltpu.make_async_copy(h_refs[r], stage.at[r], h_sem.at[r]).start()
    for r in range(count):
        block = t_ref.at[rows[start + r], pl.ds(size, size)]
        pltpu.make_async_copy(block, prev.at[r], prev_sem).start()
    if not start:
        pltpu.make_async_copy(blocks, blocks, t_sem).wait()
        for w in range(window):
            fill_pair(pair, jnp.where(kept(w), blocks[w], 0.0), w)
        pltpu.make_async_copy(pair, pair_out, pair_sem).start()

    def densify(r, slot, place):
        row = rows[start + r]
        drop = drops_ref[2 * row]
        for p in range(window):
            offset = lax.rem(rows[p] - row + REACH + total, total)
            k, named = place_of(offset, drop)
            high, low = split(jnp.where(named, stage[r, k], 0.0))
            dense[slot, place, pl.ds(0, size), pl.ds(p * size, size)] = high
            dense[slot, place, pl.ds(size, size), pl.ds(p * size, size)] = low

    def store(g, slot):
        return pltpu.make_async_copy(dense.at[slot], dense_ref.at[pl.ds(g * group, group)], dense_sem.at[slot])

    groups = count // group

    def one(g, carry):
        slot = lax.rem(g, 2)

        @pl.when(g >= 2)
        def _():
            store(g - 2, slot).wait()

        for place in range(group):
            r = g * group + place
            pltpu.make_async_copy(stage.at[r], stage.at[r], h_sem.at[r]).wait()
            densify(r, slot, place)
        store(g, slot).start()
        if start:

            @pl.when(g == 0)
            def _():
                pltpu.make_async_copy(pair, pair, pair_sem).wait()

        @pl.when(g == 0)
        def _():
            pltpu.make_async_copy(prev, prev, prev_sem).wait()

        for place, product in enumerate(products_of(dense[slot], pair[...])):
            r = g * group + place
            prev[r] = jnp.where(kept(start + r), 2.0 * product - prev[r], 0.0)
            block = outs[place] if start else out_ref.at[rows[start + r]]
            pltpu.make_async_copy(prev.at[r], block, out_sem).start()
        return carry

    lax.fori_loop(0, groups, one, 0)
    for g in range(max(groups - 2, 0), groups):
        store(g, g % 2).wait()
    if not start:
        pltpu.make_async_copy(pair, pair, pair_sem).wait()
    pltpu.make_async_copy(prev, prev, out_sem).wait()


def later_kernel(total, window, group, parts, drops_ref, me_ref, table_ref, *refs):
    rows = Rows(total, me_ref, table_ref)
    dense_refs = refs[:len(parts)]
    t_ref, first_ref, *late_refs, out_ref, dense, terms, pairs, dense_sem, t_sem, first_sem, out_sem = refs[len(parts):]
    size = terms.shape[-1]
    groups = window // group
    kept = functools.partial(kept_rows, total, rows, drops_ref)
    for w in range(window):
        late = w - (window - LAST)
        source = first_ref.at[rows[w]] if late < 0 else late_refs[late]
        pltpu.make_async_copy(source, terms.at[w, 1], first_sem).start()
    start = 0
    for part, dense_ref in zip(parts, dense_refs):
        for w in range(start, start + part):
            pltpu.make_async_copy(dense_ref.at[w - start], dense.at[w], dense_sem.at[w // group]).start()
        start += part
    for w in range(window):
        pltpu.make_async_copy(t_ref.at[rows[w], pl.ds(0, size)], terms.at[w, 0], t_sem).start()
    pltpu.make_async_copy(terms.at[:, 1], terms.at[:, 1], first_sem).wait()
    for w in range(window):
        fill_pair(pairs.at[0], terms[w, 1], w)
    pltpu.make_async_copy(terms.at[:, 0], terms.at[:, 0], t_sem).wait()

    def one(g, carry, step):
        held = dense.at[pl.ds(g * group, group)]
        if step == 0:
            pltpu.make_async_copy(held, held, dense_sem.at[g]).wait()
        for r, product in enumerate(products_of(held[...], pairs[step])):
            w = g * group + r
            newest = jnp.where(kept(w), 2.0 * product - terms[w, step], 0.0)
            terms[w, step] = newest
            if step == 0:
                fill_pair(pairs.at[1], newest, w)
            pltpu.make_async_copy(terms.at[w, step], out_ref.at[rows[w], step], out_sem).start()
        return carry

    for step in range(2):
        lax.fori_loop(0, groups, functools.partial(one, step=step), 0)
    pltpu.make_async_copy(terms, terms, out_sem).wait()


def late_sources(me_ref, sources_ref):
    return [sources_ref[me_ref[0] * LAST + r] for r in range(LAST)]


def unpack_first_kernel(
    cols_ref, me_ref, sources_ref, coefs_ref, first_ref, density_ref, out_ref, sums, one, sems
):
    load = pltpu.make_async_copy(density_ref, sums, sems.at[0])
    load.start()
    late = late_sources(me_ref, sources_ref)
    for k in range(cols_ref.shape[0]):
        pltpu.make_async_copy(first_ref.at[cols_ref[k]], one.at[k], sems.at[1]).start()
    load.wait()
    pltpu.make_async_copy(one, one, sems.at[1]).wait()
    for k in range(cols_ref.shape[0]):
        col = cols_ref[k]
        early = jnp.logical_and(col != late[0], col != late[1])
        sums[k] = sums[k] + jnp.where(early, coefs_ref[0] * one[k], 0.0)
    store = pltpu.make_async_copy(sums, out_ref, sems.at[0])
    store.start()
    store.wait()


def unpack_last_kernel(cols_ref, me_ref, sources_ref, coefs_ref, held_ref, sum_ref, *refs):
    late_refs = refs[:LAST]
    density_ref, last_ref, before_ref, sums, two, three, ones, sems = refs[LAST:]
    load = pltpu.make_async_copy(sum_ref, sums, sems.at[0])
    load.start()
    for place, sem, which in ((two, 1, 0), (three, 2, 1)):
        for k in range(cols_ref.shape[0]):
            pltpu.make_async_copy(held_ref.at[cols_ref[k], which], place.at[k], sems.at[sem]).start()
    for r in range(LAST):
        pltpu.make_async_copy(late_refs[r], ones.at[r], sems.at[3]).start()
    pltpu.make_async_copy(two, two, sems.at[1]).wait()
    before = pltpu.make_async_copy(two, before_ref, sems.at[1])
    before.start()
    pltpu.make_async_copy(three, three, sems.at[2]).wait()
    last = pltpu.make_async_copy(three, last_ref, sems.at[2])
    last.start()
    load.wait()
    sums[...] = sums[...] + coefs_ref[1] * two[...] + coefs_ref[2] * three[...]
    pltpu.make_async_copy(ones, ones, sems.at[3]).wait()
    for r, source in enumerate(late_sources(me_ref, sources_ref)):
        for k in range(cols_ref.shape[0]):

            @pl.when(cols_ref[k] == source)
            def _(k=k, r=r):
                sums[k] = sums[k] + coefs_ref[0] * ones[r]

    store = pltpu.make_async_copy(sums, density_ref, sems.at[0])
    store.start()
    before.wait()
    last.wait()
    store.wait()


def per_device(h_blocks, h_cols, term_prev, term_cur, t_cols, density_in, coefs):
    total = lax.axis_size("row")
    me = lax.axis_index("row")
    count, size = h_blocks.shape[1:3]
    drop_h = dropped_offset(h_cols, me, total)
    drop_t = dropped_offset(t_cols, me, total)
    f32, bf16 = jnp.float32, jnp.bfloat16
    dma = pltpu.SemaphoreType.DMA
    row = jax.ShapeDtypeStruct((count, size, size), f32)
    row_scratch = pltpu.VMEM(row.shape, f32)

    def call(kernel, smem, arrays, outs, scratch, name, megabytes, aliases={}):
        return pl.pallas_call(
            kernel,
            out_shape=[pltpu.HBM(out.shape, out.dtype) for out in outs],
            in_specs=[SMEM] * len(smem) + [ANY] * len(arrays),
            out_specs=[ANY] * len(outs),
            scratch_shapes=scratch,
            input_output_aliases=aliases,
            compiler_params=pltpu.CompilerParams(vmem_limit_bytes=megabytes * 1024 * 1024),
            name=name,
        )(*smem, *arrays)

    def in_hbm(x):
        return pltpu.with_memory_space_constraint(x, pltpu.HBM)

    def exchange(x):
        return lax.all_to_all(x, "row", 0, 0, tiled=True)

    (send,) = call(
        functools.partial(pack_kernel, total),
        [jnp.stack([me, drop_h[0], drop_t[0]]), t_cols[0]],
        [term_cur[0], term_prev[0]],
        [jax.ShapeDtypeStruct((total, 2 * size + NOTE, size), f32)],
        [
            row_scratch,
            row_scratch,
            pltpu.VMEM((2 * size, size), f32),
            pltpu.VMEM((NOTE, size), f32),
            dma((3,)),
        ],
        "pack",
        60,
    )
    table, parts = window_table(total)
    gathered = gathered_rows(h_blocks[0], total, lambda *others: exchange(after(send, *others)))
    column = next(gathered)
    drops = column[:, 2 * size:2 * size + 2, 0].astype(jnp.int32).reshape(-1)
    rows = jnp.array(table, jnp.int32).reshape(-1)
    window = sum(parts)
    dense_shape = (window, 2 * size, window * size)
    pair_shape = (window * size, 2 * size)
    dense = []
    start = 0
    for part in parts:
        h_rows = gathered.send(dense[-1] if start else None)
        group = max(g for g in (2, 7, 13) if part % g == 0)
        scratch = [
            pltpu.VMEM((part, count, size, size), f32),
            pltpu.VMEM((min(2, part // group), group) + dense_shape[1:], bf16),
            pltpu.VMEM((part, size, size), f32),
            pltpu.VMEM(pair_shape, bf16),
            dma((part,)),
            dma,
            dma,
            dma,
            dma((2,)),
            dma,
        ]
        if not start:
            scratch = [pltpu.VMEM((window, size, size), f32)] + scratch
        result = call(
            functools.partial(first_kernel, total, window, start, part, group),
            [drops, me[None], rows],
            [in_hbm(column), *h_rows, in_hbm(pair)] if start else [column, *h_rows],
            [
                jax.ShapeDtypeStruct((part,) + dense_shape[1:], bf16),
            ]
            + (
                [jax.ShapeDtypeStruct((size, size), f32)] * LAST
                if start
                else [jax.ShapeDtypeStruct((total, size, size), f32), jax.ShapeDtypeStruct(pair_shape, bf16)]
            ),
            scratch,
            "first",
            24 if start else 60,
        )
        dense.append(result[0])
        if start:
            late1 = result[1:]
        else:
            term1, pair = result[1:]
        start += part
    back1 = exchange(term1)
    targets = [[row[window - LAST + r] for row in table] for r in range(LAST)]
    sources = jnp.array([[to.index(i) for to in targets] for i in range(total)], jnp.int32).reshape(-1)
    group = max(g for g in (3, 4) if window % g == 0)
    (terms,) = call(
        functools.partial(later_kernel, total, window, group, parts),
        [drops, me[None], rows],
        [*dense, column, term1, *late1],
        [jax.ShapeDtypeStruct((total, 2, size, size), f32)],
        [
            pltpu.VMEM(dense_shape, bf16),
            pltpu.VMEM((window, 2, size, size), f32),
            pltpu.VMEM((2,) + pair_shape, bf16),
            dma((window // group,)),
            dma,
            dma,
            dma,
        ],
        "later",
        60,
    )
    back = exchange(after(terms, back1))
    late_back = [permute(after(late1[r], terms), lambda i, r=r: targets[r][i]) for r in range(LAST)]
    own = [t_cols[0], me[None], sources, coefs]
    (sums,) = call(
        unpack_first_kernel,
        own,
        [back1, density_in[0]],
        [row],
        [row_scratch, row_scratch, dma((2,))],
        "unpack_first",
        60,
    )
    density, last, before = call(
        unpack_last_kernel,
        own,
        [back, sums, *late_back],
        [row] * 3,
        [row_scratch, row_scratch, row_scratch, pltpu.VMEM((LAST, size, size), f32), dma((4,))],
        "unpack_last",
        60,
    )
    return density[None], last[None], before[None]


def solution(mesh):
    blocks = P(("groups", "row"), None, None, None)
    cols = P(("groups", "row"), None)
    return jax.shard_map(
        per_device,
        mesh=mesh,
        in_specs=(blocks, cols, blocks, blocks, cols, blocks, P()),
        out_specs=(blocks, blocks, blocks),
        check_vma=False,
    )
```

```python
import functools

import jax
import jax.numpy as jnp
from jax import lax
from jax.experimental import pallas as pl
from jax.experimental.pallas import tpu as pltpu
from jax.sharding import PartitionSpec as P

REACH = 7
NOTE = 8
LAST = 2
SMEM = pl.BlockSpec(memory_space=pltpu.SMEM)
ANY = pl.BlockSpec(memory_space=pl.ANY)


def permute(x, target):
    devices = lax.axis_size("row")
    return lax.ppermute(x, "row", [(i, target(i)) for i in range(devices)])


def after(x, *others):
    return lax.optimization_barrier((x, *others))[0]


RING = (0, 2, 4, 6, 7, 5, 3, 1)


def along_ring(device, by):
    if device % 2:
        by = -by
    return 2 * RING[(RING.index(device // 2) + by) % len(RING)] + device % 2


def window_table(total):
    if total != 16:
        steps = [0] + [by for hop in range(1, REACH + 1) for by in (-hop, hop)]
        return [[(i + by) % total for by in steps] for i in range(total)], (13, LAST)
    order = (0, -1, 1, -2, 2, -3, 3, -4)
    table = [[along_ring(source, by) for by in order for source in (i, i ^ 1)] for i in range(total)]
    return table, (14, LAST)


def gathered_rows(x, total, exchange):
    if total != 16:
        rows = [x]
        for hop in range(1, REACH + 1):
            for by in (hop, -hop):
                rows.append(permute(x, lambda i, by=by: (i + by) % total))
        yield exchange()
        yield rows[:13]
        yield rows[13:]
        return

    def other_core(row):
        return permute(row, lambda i: i ^ 1)

    def round_of(ahead, behind):
        ahead = permute(ahead, lambda i: along_ring(i, 1))
        behind = permute(behind, lambda i: along_ring(i, -1))
        return ahead, behind, [ahead, other_core(ahead), behind, other_core(behind)]

    rows = [x, other_core(x)]
    ahead, behind, first = round_of(x, x)
    ahead, behind, second = round_of(ahead, behind)
    column = exchange(ahead, behind, rows[1], first[1], first[3])
    yield column
    ahead, behind, third = round_of(ahead, behind)
    far = permute(after(ahead, column), lambda i: along_ring(i, 1))
    made = yield rows + first + second + third
    far = after(far, made)
    yield [far, other_core(far)]


def place_of(offset, dropped):
    named = jnp.logical_and(offset <= 2 * REACH, offset != dropped)
    slot = offset - jnp.where(offset > dropped, 1, 0)
    return jnp.clip(slot, 0, 2 * REACH - 1), named


def dropped_offset(cols, row, total):
    offsets = jnp.mod(cols - row + REACH, total)
    return REACH * (2 * REACH + 1) - jnp.sum(offsets, axis=1)


def pack_kernel(total, info_ref, cols_ref, cur_ref, prev_ref, send_ref, cur, prev, zeros, note, sems):
    row = info_ref[0]
    drop = info_ref[2]
    count, size = cur.shape[:2]
    loads = (
        pltpu.make_async_copy(cur_ref, cur, sems.at[0]),
        pltpu.make_async_copy(prev_ref, prev, sems.at[1]),
    )
    for load in loads:
        load.start()
    zeros[...] = jnp.zeros_like(zeros)
    line = lax.broadcasted_iota(jnp.int32, note.shape, 0)
    note[...] = jnp.where(line == 0, info_ref[1], drop).astype(jnp.float32)

    def fill(j, carry):
        offset = lax.rem(j - row + REACH + total, total)
        _, named = place_of(offset, drop)
        pltpu.make_async_copy(note, send_ref.at[j, pl.ds(2 * size, NOTE)], sems.at[2]).start()

        @pl.when(jnp.logical_not(named))
        def _():
            pltpu.make_async_copy(zeros, send_ref.at[j, pl.ds(0, 2 * size)], sems.at[2]).start()

        return carry

    lax.fori_loop(0, total, fill, 0)
    for which, held in enumerate((cur, prev)):
        loads[which].wait()
        for k in range(count):
            place = send_ref.at[cols_ref[k], pl.ds(which * size, size)]
            pltpu.make_async_copy(held.at[k], place, sems.at[2]).start()
    pltpu.make_async_copy(send_ref, send_ref, sems.at[2]).wait()


def split(x):
    high = x.astype(jnp.bfloat16)
    low = (x - high.astype(jnp.float32)).astype(jnp.bfloat16)
    return high, low


class Rows:
    def __init__(self, total, me_ref, table_ref):
        self.me = me_ref[0]
        self.table_ref = table_ref
        self.window = table_ref.shape[0] // total

    def __getitem__(self, w):
        return self.table_ref[self.me * self.window + w]


def kept_rows(total, rows, drops_ref, w):
    row = rows[w]
    offset = lax.rem(rows.me - row + REACH + total, total)
    _, named = place_of(offset, drops_ref[2 * row + 1])
    return named


def fill_pair(pair, block, w):
    size = block.shape[-1]
    high, low = split(block)
    at = pl.ds(pl.multiple_of(w * size, size), size)
    pair[at, pl.ds(0, size)] = high
    pair[at, pl.ds(size, size)] = low


def products_of(rows, pair):
    group, double = rows.shape[:2]
    size = double // 2
    products = jnp.dot(rows.reshape(group * double, rows.shape[2]), pair, preferred_element_type=jnp.float32)
    for r in range(group):
        parts = products[r * double:r * double + size] + products[r * double + size:(r + 1) * double]
        yield parts[:, :size] + parts[:, size:]


def first_kernel(total, window, start, count, group, drops_ref, me_ref, table_ref, t_ref, *refs):
    rows = Rows(total, me_ref, table_ref)
    h_refs = refs[:count]
    if start:
        pair_in, dense_ref, *outs = refs[count:count + 2 + LAST]
    else:
        dense_ref, out_ref, pair_out, blocks = refs[count:count + 4]
    stage, dense, prev, pair, h_sem, t_sem, prev_sem, pair_sem, dense_sem, out_sem = refs[-10:]
    size = t_ref.shape[-1]
    kept = functools.partial(kept_rows, total, rows, drops_ref)

    if start:
        pltpu.make_async_copy(pair_in, pair, pair_sem).start()
    else:
        for w in range(window):
            pltpu.make_async_copy(t_ref.at[rows[w], pl.ds(0, size)], blocks.at[w], t_sem).start()
    for r in range(count):
        pltpu.make_async_copy(h_refs[r], stage.at[r], h_sem.at[r]).start()
    for r in range(count):
        block = t_ref.at[rows[start + r], pl.ds(size, size)]
        pltpu.make_async_copy(block, prev.at[r], prev_sem).start()
    if not start:
        pltpu.make_async_copy(blocks, blocks, t_sem).wait()
        for w in range(window):
            fill_pair(pair, jnp.where(kept(w), blocks[w], 0.0), w)
        pltpu.make_async_copy(pair, pair_out, pair_sem).start()

    def densify(r, slot, place):
        row = rows[start + r]
        drop = drops_ref[2 * row]
        for p in range(window):
            offset = lax.rem(rows[p] - row + REACH + total, total)
            k, named = place_of(offset, drop)
            high, low = split(jnp.where(named, stage[r, k], 0.0))
            dense[slot, place, pl.ds(0, size), pl.ds(p * size, size)] = high
            dense[slot, place, pl.ds(size, size), pl.ds(p * size, size)] = low

    def store(g, slot):
        return pltpu.make_async_copy(dense.at[slot], dense_ref.at[pl.ds(g * group, group)], dense_sem.at[slot])

    groups = count // group

    def one(g, carry):
        slot = lax.rem(g, 2)

        @pl.when(g >= 2)
        def _():
            store(g - 2, slot).wait()

        for place in range(group):
            r = g * group + place
            pltpu.make_async_copy(stage.at[r], stage.at[r], h_sem.at[r]).wait()
            densify(r, slot, place)
        store(g, slot).start()
        if start:

            @pl.when(g == 0)
            def _():
                pltpu.make_async_copy(pair, pair, pair_sem).wait()

        @pl.when(g == 0)
        def _():
            pltpu.make_async_copy(prev, prev, prev_sem).wait()

        for place, product in enumerate(products_of(dense[slot], pair[...])):
            r = g * group + place
            prev[r] = jnp.where(kept(start + r), 2.0 * product - prev[r], 0.0)
            block = outs[place] if start else out_ref.at[rows[start + r]]
            pltpu.make_async_copy(prev.at[r], block, out_sem).start()
        return carry

    lax.fori_loop(0, groups, one, 0)
    for g in range(max(groups - 2, 0), groups):
        store(g, g % 2).wait()
    if not start:
        pltpu.make_async_copy(pair, pair, pair_sem).wait()
    pltpu.make_async_copy(prev, prev, out_sem).wait()


def later_kernel(total, window, group, parts, drops_ref, me_ref, table_ref, *refs):
    rows = Rows(total, me_ref, table_ref)
    dense_refs = refs[:len(parts)]
    t_ref, first_ref, *late_refs, out_ref, dense, terms, pairs, dense_sem, t_sem, first_sem, out_sem = refs[len(parts):]
    size = terms.shape[-1]
    groups = window // group
    kept = functools.partial(kept_rows, total, rows, drops_ref)
    for w in range(window):
        late = w - (window - LAST)
        source = first_ref.at[rows[w]] if late < 0 else late_refs[late]
        pltpu.make_async_copy(source, terms.at[w, 1], first_sem).start()
    start = 0
    for part, dense_ref in zip(parts, dense_refs):
        for w in range(start, start + part):
            pltpu.make_async_copy(dense_ref.at[w - start], dense.at[w], dense_sem.at[w // group]).start()
        start += part
    for w in range(window):
        pltpu.make_async_copy(t_ref.at[rows[w], pl.ds(0, size)], terms.at[w, 0], t_sem).start()
    pltpu.make_async_copy(terms.at[:, 1], terms.at[:, 1], first_sem).wait()
    for w in range(window):
        fill_pair(pairs.at[0], terms[w, 1], w)
    pltpu.make_async_copy(terms.at[:, 0], terms.at[:, 0], t_sem).wait()

    def one(g, carry, step):
        held = dense.at[pl.ds(g * group, group)]
        if step == 0:
            pltpu.make_async_copy(held, held, dense_sem.at[g]).wait()
        for r, product in enumerate(products_of(held[...], pairs[step])):
            w = g * group + r
            newest = jnp.where(kept(w), 2.0 * product - terms[w, step], 0.0)
            terms[w, step] = newest
            if step == 0:
                fill_pair(pairs.at[1], newest, w)
            pltpu.make_async_copy(terms.at[w, step], out_ref.at[rows[w], step], out_sem).start()
        return carry

    for step in range(2):
        lax.fori_loop(0, groups, functools.partial(one, step=step), 0)
    pltpu.make_async_copy(terms, terms, out_sem).wait()


def late_sources(me_ref, sources_ref):
    return [sources_ref[me_ref[0] * LAST + r] for r in range(LAST)]


def unpack_first_kernel(
    cols_ref, me_ref, sources_ref, coefs_ref, first_ref, density_ref, out_ref, sums, one, sems
):
    load = pltpu.make_async_copy(density_ref, sums, sems.at[0])
    load.start()
    late = late_sources(me_ref, sources_ref)
    for k in range(cols_ref.shape[0]):
        pltpu.make_async_copy(first_ref.at[cols_ref[k]], one.at[k], sems.at[1]).start()
    load.wait()
    pltpu.make_async_copy(one, one, sems.at[1]).wait()
    for k in range(cols_ref.shape[0]):
        col = cols_ref[k]
        early = jnp.logical_and(col != late[0], col != late[1])
        sums[k] = sums[k] + jnp.where(early, coefs_ref[0] * one[k], 0.0)
    store = pltpu.make_async_copy(sums, out_ref, sems.at[0])
    store.start()
    store.wait()


def unpack_last_kernel(cols_ref, me_ref, sources_ref, coefs_ref, held_ref, sum_ref, *refs):
    late_refs = refs[:LAST]
    density_ref, last_ref, before_ref, sums, two, three, ones, sems = refs[LAST:]
    load = pltpu.make_async_copy(sum_ref, sums, sems.at[0])
    load.start()
    for place, sem, which in ((two, 1, 0), (three, 2, 1)):
        for k in range(cols_ref.shape[0]):
            pltpu.make_async_copy(held_ref.at[cols_ref[k], which], place.at[k], sems.at[sem]).start()
    for r in range(LAST):
        pltpu.make_async_copy(late_refs[r], ones.at[r], sems.at[3]).start()
    pltpu.make_async_copy(two, two, sems.at[1]).wait()
    before = pltpu.make_async_copy(two, before_ref, sems.at[1])
    before.start()
    pltpu.make_async_copy(three, three, sems.at[2]).wait()
    last = pltpu.make_async_copy(three, last_ref, sems.at[2])
    last.start()
    load.wait()
    sums[...] = sums[...] + coefs_ref[1] * two[...] + coefs_ref[2] * three[...]
    pltpu.make_async_copy(ones, ones, sems.at[3]).wait()
    for r, source in enumerate(late_sources(me_ref, sources_ref)):
        for k in range(cols_ref.shape[0]):

            @pl.when(cols_ref[k] == source)
            def _(k=k, r=r):
                sums[k] = sums[k] + coefs_ref[0] * ones[r]

    store = pltpu.make_async_copy(sums, density_ref, sems.at[0])
    store.start()
    before.wait()
    last.wait()
    store.wait()


def per_device(h_blocks, h_cols, term_prev, term_cur, t_cols, density_in, coefs):
    total = lax.axis_size("row")
    me = lax.axis_index("row")
    count, size = h_blocks.shape[1:3]
    drop_h = dropped_offset(h_cols, me, total)
    drop_t = dropped_offset(t_cols, me, total)
    f32, bf16 = jnp.float32, jnp.bfloat16
    dma = pltpu.SemaphoreType.DMA
    row = jax.ShapeDtypeStruct((count, size, size), f32)
    row_scratch = pltpu.VMEM(row.shape, f32)

    def call(kernel, smem, arrays, outs, scratch, name, megabytes, aliases={}):
        return pl.pallas_call(
            kernel,
            out_shape=[pltpu.HBM(out.shape, out.dtype) for out in outs],
            in_specs=[SMEM] * len(smem) + [ANY] * len(arrays),
            out_specs=[ANY] * len(outs),
            scratch_shapes=scratch,
            input_output_aliases=aliases,
            compiler_params=pltpu.CompilerParams(vmem_limit_bytes=megabytes * 1024 * 1024),
            name=name,
        )(*smem, *arrays)

    def in_hbm(x):
        return pltpu.with_memory_space_constraint(x, pltpu.HBM)

    def exchange(x):
        return lax.all_to_all(x, "row", 0, 0, tiled=True)

    (send,) = call(
        functools.partial(pack_kernel, total),
        [jnp.stack([me, drop_h[0], drop_t[0]]), t_cols[0]],
        [term_cur[0], term_prev[0]],
        [jax.ShapeDtypeStruct((total, 2 * size + NOTE, size), f32)],
        [
            row_scratch,
            row_scratch,
            pltpu.VMEM((2 * size, size), f32),
            pltpu.VMEM((NOTE, size), f32),
            dma((3,)),
        ],
        "pack",
        60,
    )
    table, parts = window_table(total)
    gathered = gathered_rows(h_blocks[0], total, lambda *others: exchange(after(send, *others)))
    column = next(gathered)
    drops = column[:, 2 * size:2 * size + 2, 0].astype(jnp.int32).reshape(-1)
    rows = jnp.array(table, jnp.int32).reshape(-1)
    window = sum(parts)
    dense_shape = (window, 2 * size, window * size)
    pair_shape = (window * size, 2 * size)
    dense = []
    start = 0
    for part in parts:
        h_rows = gathered.send(dense[-1] if start else None)
        group = max(g for g in (2, 7, 13) if part % g == 0)
        scratch = [
            pltpu.VMEM((part, count, size, size), f32),
            pltpu.VMEM((min(2, part // group), group) + dense_shape[1:], bf16),
            pltpu.VMEM((part, size, size), f32),
            pltpu.VMEM(pair_shape, bf16),
            dma((part,)),
            dma,
            dma,
            dma,
            dma((2,)),
            dma,
        ]
        if not start:
            scratch = [pltpu.VMEM((window, size, size), f32)] + scratch
        result = call(
            functools.partial(first_kernel, total, window, start, part, group),
            [drops, me[None], rows],
            [in_hbm(column), *h_rows, in_hbm(pair)] if start else [column, *h_rows],
            [
                jax.ShapeDtypeStruct((part,) + dense_shape[1:], bf16),
            ]
            + (
                [jax.ShapeDtypeStruct((size, size), f32)] * LAST
                if start
                else [jax.ShapeDtypeStruct((total, size, size), f32), jax.ShapeDtypeStruct(pair_shape, bf16)]
            ),
            scratch,
            "first",
            24 if start else 60,
        )
        dense.append(result[0])
        if start:
            late1 = result[1:]
        else:
            term1, pair = result[1:]
        start += part
    back1 = exchange(after(term1, h_rows[0]))
    targets = [[row[window - LAST + r] for row in table] for r in range(LAST)]
    sources = jnp.array([[to.index(i) for to in targets] for i in range(total)], jnp.int32).reshape(-1)
    group = max(g for g in (3, 4) if window % g == 0)
    (terms,) = call(
        functools.partial(later_kernel, total, window, group, parts),
        [drops, me[None], rows],
        [*dense, column, term1, *late1],
        [jax.ShapeDtypeStruct((total, 2, size, size), f32)],
        [
            pltpu.VMEM(dense_shape, bf16),
            pltpu.VMEM((window, 2, size, size), f32),
            pltpu.VMEM((2,) + pair_shape, bf16),
            dma((window // group,)),
            dma,
            dma,
            dma,
        ],
        "later",
        60,
    )
    back = exchange(after(terms, back1))
    late_back = [permute(after(late1[r], terms), lambda i, r=r: targets[r][i]) for r in range(LAST)]
    own = [t_cols[0], me[None], sources, coefs]
    (sums,) = call(
        unpack_first_kernel,
        own,
        [back1, density_in[0]],
        [row],
        [row_scratch, row_scratch, dma((2,))],
        "unpack_first",
        60,
    )
    density, last, before = call(
        unpack_last_kernel,
        own,
        [back, sums, *late_back],
        [row] * 3,
        [row_scratch, row_scratch, row_scratch, pltpu.VMEM((LAST, size, size), f32), dma((4,))],
        "unpack_last",
        60,
    )
    return density[None], last[None], before[None]


def solution(mesh):
    blocks = P(("groups", "row"), None, None, None)
    cols = P(("groups", "row"), None)
    return jax.shard_map(
        per_device,
        mesh=mesh,
        in_specs=(blocks, cols, blocks, blocks, cols, blocks, P()),
        out_specs=(blocks, blocks, blocks),
        check_vma=False,
    )
```

```python
import functools

import jax
import jax.numpy as jnp
from jax import lax
from jax.experimental import pallas as pl
from jax.experimental.pallas import tpu as pltpu
from jax.sharding import PartitionSpec as P

REACH = 7
NOTE = 8
SMEM = pl.BlockSpec(memory_space=pltpu.SMEM)
ANY = pl.BlockSpec(memory_space=pl.ANY)


def permute(x, target):
    devices = lax.axis_size("row")
    return lax.ppermute(x, "row", [(i, target(i)) for i in range(devices)])


def after(x, *others):
    return lax.optimization_barrier((x, *others))[0]


RING = (0, 2, 4, 6, 7, 5, 3, 1)


def along_ring(device, by):
    if device % 2:
        by = -by
    return 2 * RING[(RING.index(device // 2) + by) % len(RING)] + device % 2


def window_table(total):
    if total != 16:
        steps = [0] + [by for hop in range(1, REACH + 1) for by in (-hop, hop)]
        return [[(i + by) % total for by in steps] for i in range(total)], (13, 2)
    order = (0, -1, 1, -2, 2, -3, 3, -4)
    table = [[along_ring(source, by) for by in order for source in (i, i ^ 1)] for i in range(total)]
    return table, (14, 2)


def gathered_rows(x, total, exchange):
    if total != 16:
        rows = [x]
        for hop in range(1, REACH + 1):
            for by in (hop, -hop):
                rows.append(permute(x, lambda i, by=by: (i + by) % total))
        yield exchange()
        yield rows[:13]
        yield rows[13:]
        return

    def other_core(row):
        return permute(row, lambda i: i ^ 1)

    def round_of(ahead, behind):
        ahead = permute(ahead, lambda i: along_ring(i, 1))
        behind = permute(behind, lambda i: along_ring(i, -1))
        return ahead, behind, [ahead, other_core(ahead), behind, other_core(behind)]

    rows = [x, other_core(x)]
    ahead, behind, first = round_of(x, x)
    ahead, behind, second = round_of(ahead, behind)
    column = exchange(ahead, behind, rows[1], first[1], first[3])
    yield column
    ahead, behind, third = round_of(ahead, behind)
    far = permute(after(ahead, column), lambda i: along_ring(i, 1))
    made = yield rows + first + second + third
    far = after(far, made)
    yield [far, other_core(far)]


def place_of(offset, dropped):
    named = jnp.logical_and(offset <= 2 * REACH, offset != dropped)
    slot = offset - jnp.where(offset > dropped, 1, 0)
    return jnp.clip(slot, 0, 2 * REACH - 1), named


def dropped_offset(cols, row, total):
    offsets = jnp.mod(cols - row + REACH, total)
    return REACH * (2 * REACH + 1) - jnp.sum(offsets, axis=1)


def pack_kernel(total, info_ref, cols_ref, cur_ref, prev_ref, send_ref, cur, prev, zeros, note, sems):
    row = info_ref[0]
    drop = info_ref[2]
    count, size = cur.shape[:2]
    loads = (
        pltpu.make_async_copy(cur_ref, cur, sems.at[0]),
        pltpu.make_async_copy(prev_ref, prev, sems.at[1]),
    )
    for load in loads:
        load.start()
    zeros[...] = jnp.zeros_like(zeros)
    line = lax.broadcasted_iota(jnp.int32, note.shape, 0)
    note[...] = jnp.where(line == 0, info_ref[1], drop).astype(jnp.float32)

    def fill(j, carry):
        offset = lax.rem(j - row + REACH + total, total)
        _, named = place_of(offset, drop)
        pltpu.make_async_copy(note, send_ref.at[j, pl.ds(2 * size, NOTE)], sems.at[2]).start()

        @pl.when(jnp.logical_not(named))
        def _():
            pltpu.make_async_copy(zeros, send_ref.at[j, pl.ds(0, 2 * size)], sems.at[2]).start()

        return carry

    lax.fori_loop(0, total, fill, 0)
    for which, held in enumerate((cur, prev)):
        loads[which].wait()
        for k in range(count):
            place = send_ref.at[cols_ref[k], pl.ds(which * size, size)]
            pltpu.make_async_copy(held.at[k], place, sems.at[2]).start()
    pltpu.make_async_copy(send_ref, send_ref, sems.at[2]).wait()


def split(x):
    high = x.astype(jnp.bfloat16)
    low = (x - high.astype(jnp.float32)).astype(jnp.bfloat16)
    return high, low


class Rows:
    def __init__(self, total, me_ref, table_ref):
        self.me = me_ref[0]
        self.table_ref = table_ref
        self.window = table_ref.shape[0] // total

    def __getitem__(self, w):
        return self.table_ref[self.me * self.window + w]


def kept_rows(total, rows, drops_ref, w):
    row = rows[w]
    offset = lax.rem(rows.me - row + REACH + total, total)
    _, named = place_of(offset, drops_ref[2 * row + 1])
    return named


def fill_pair(pair, block, w):
    size = block.shape[-1]
    high, low = split(block)
    at = pl.ds(pl.multiple_of(w * size, size), size)
    pair[at, pl.ds(0, size)] = high
    pair[at, pl.ds(size, size)] = low


def products_of(rows, pair):
    group, double = rows.shape[:2]
    size = double // 2
    products = jnp.dot(rows.reshape(group * double, rows.shape[2]), pair, preferred_element_type=jnp.float32)
    for r in range(group):
        parts = products[r * double:r * double + size] + products[r * double + size:(r + 1) * double]
        yield parts[:, :size] + parts[:, size:]


def first_kernel(total, window, start, count, group, drops_ref, me_ref, table_ref, t_ref, *refs):
    rows = Rows(total, me_ref, table_ref)
    h_refs = refs[:count]
    if start:
        pair_in, _ = refs[count:count + 2]
        dense_ref, out_ref = refs[count + 2:count + 4]
    else:
        dense_ref, out_ref, pair_out, blocks = refs[count:count + 4]
    stage, dense, prev, pair, h_sem, t_sem, prev_sem, pair_sem, dense_sem, out_sem = refs[-10:]
    size = t_ref.shape[-1]
    kept = functools.partial(kept_rows, total, rows, drops_ref)

    if start:
        pltpu.make_async_copy(pair_in, pair, pair_sem).start()
    else:
        for w in range(window):
            pltpu.make_async_copy(t_ref.at[rows[w], pl.ds(0, size)], blocks.at[w], t_sem).start()
    for r in range(count):
        pltpu.make_async_copy(h_refs[r], stage.at[r], h_sem.at[r]).start()
    for r in range(count):
        block = t_ref.at[rows[start + r], pl.ds(size, size)]
        pltpu.make_async_copy(block, prev.at[r], prev_sem).start()
    if not start:
        pltpu.make_async_copy(blocks, blocks, t_sem).wait()
        for w in range(window):
            fill_pair(pair, jnp.where(kept(w), blocks[w], 0.0), w)
        pltpu.make_async_copy(pair, pair_out, pair_sem).start()

    def densify(r, slot, place):
        row = rows[start + r]
        drop = drops_ref[2 * row]
        for p in range(window):
            offset = lax.rem(rows[p] - row + REACH + total, total)
            k, named = place_of(offset, drop)
            high, low = split(jnp.where(named, stage[r, k], 0.0))
            dense[slot, place, pl.ds(0, size), pl.ds(p * size, size)] = high
            dense[slot, place, pl.ds(size, size), pl.ds(p * size, size)] = low

    def store(g, slot):
        return pltpu.make_async_copy(dense.at[slot], dense_ref.at[pl.ds(g * group, group)], dense_sem.at[slot])

    groups = count // group

    def one(g, carry):
        slot = lax.rem(g, 2)

        @pl.when(g >= 2)
        def _():
            store(g - 2, slot).wait()

        def ready(place, carry):
            r = g * group + place
            pltpu.make_async_copy(stage.at[r], stage.at[r], h_sem.at[r]).wait()
            densify(r, slot, place)
            return carry

        lax.fori_loop(0, group, ready, 0)
        store(g, slot).start()
        if start:

            @pl.when(g == 0)
            def _():
                pltpu.make_async_copy(pair, pair, pair_sem).wait()

        @pl.when(g == 0)
        def _():
            pltpu.make_async_copy(prev, prev, prev_sem).wait()

        for place, product in enumerate(products_of(dense[slot], pair[...])):
            r = g * group + place
            prev[r] = jnp.where(kept(start + r), 2.0 * product - prev[r], 0.0)
            pltpu.make_async_copy(prev.at[r], out_ref.at[rows[start + r]], out_sem).start()
        return carry

    lax.fori_loop(0, groups, one, 0)
    for g in range(max(groups - 2, 0), groups):
        store(g, g % 2).wait()
    if not start:
        pltpu.make_async_copy(pair, pair, pair_sem).wait()
    pltpu.make_async_copy(prev, prev, out_sem).wait()


def later_kernel(total, window, group, parts, drops_ref, me_ref, table_ref, *refs):
    rows = Rows(total, me_ref, table_ref)
    dense_refs = refs[:len(parts)]
    t_ref, first_ref, out_ref, dense, terms, pairs, dense_sem, t_sem, first_sem, out_sem = refs[len(parts):]
    size = terms.shape[-1]
    groups = window // group
    kept = functools.partial(kept_rows, total, rows, drops_ref)
    for w in range(window):
        pltpu.make_async_copy(first_ref.at[rows[w]], terms.at[w, 1], first_sem).start()
    start = 0
    for part, dense_ref in zip(parts, dense_refs):
        for w in range(start, start + part):
            pltpu.make_async_copy(dense_ref.at[w - start], dense.at[w], dense_sem.at[w // group]).start()
        start += part
    for w in range(window):
        pltpu.make_async_copy(t_ref.at[rows[w], pl.ds(0, size)], terms.at[w, 0], t_sem).start()
    pltpu.make_async_copy(terms.at[:, 1], terms.at[:, 1], first_sem).wait()
    for w in range(window):
        fill_pair(pairs.at[0], terms[w, 1], w)
    pltpu.make_async_copy(terms.at[:, 0], terms.at[:, 0], t_sem).wait()

    def one(g, carry, step):
        held = dense.at[pl.ds(g * group, group)]
        if step == 0:
            pltpu.make_async_copy(held, held, dense_sem.at[g]).wait()
        for r, product in enumerate(products_of(held[...], pairs[step])):
            w = g * group + r
            newest = jnp.where(kept(w), 2.0 * product - terms[w, step], 0.0)
            terms[w, step] = newest
            if step == 0:
                fill_pair(pairs.at[1], newest, w)
            pltpu.make_async_copy(terms.at[w, step], out_ref.at[rows[w], step], out_sem).start()
        return carry

    for step in range(2):
        lax.fori_loop(0, groups, functools.partial(one, step=step), 0)
    pltpu.make_async_copy(terms, terms, out_sem).wait()


def unpack_first_kernel(cols_ref, coefs_ref, first_ref, density_ref, out_ref, sums, one, sems):
    load = pltpu.make_async_copy(density_ref, sums, sems.at[0])
    load.start()
    for k in range(cols_ref.shape[0]):
        pltpu.make_async_copy(first_ref.at[cols_ref[k]], one.at[k], sems.at[1]).start()
    load.wait()
    pltpu.make_async_copy(one, one, sems.at[1]).wait()
    sums[...] += coefs_ref[0] * one[...]
    store = pltpu.make_async_copy(sums, out_ref, sems.at[0])
    store.start()
    store.wait()


def unpack_last_kernel(cols_ref, coefs_ref, held_ref, sum_ref, density_ref, last_ref, before_ref, sums, two, three, sems):
    load = pltpu.make_async_copy(sum_ref, sums, sems.at[0])
    load.start()
    for place, sem, which in ((two, 1, 0), (three, 2, 1)):
        for k in range(cols_ref.shape[0]):
            pltpu.make_async_copy(held_ref.at[cols_ref[k], which], place.at[k], sems.at[sem]).start()
    pltpu.make_async_copy(two, two, sems.at[1]).wait()
    before = pltpu.make_async_copy(two, before_ref, sems.at[1])
    before.start()
    pltpu.make_async_copy(three, three, sems.at[2]).wait()
    last = pltpu.make_async_copy(three, last_ref, sems.at[2])
    last.start()
    load.wait()
    sums[...] = sums[...] + coefs_ref[1] * two[...] + coefs_ref[2] * three[...]
    store = pltpu.make_async_copy(sums, density_ref, sems.at[0])
    store.start()
    before.wait()
    last.wait()
    store.wait()


def per_device(h_blocks, h_cols, term_prev, term_cur, t_cols, density_in, coefs):
    total = lax.axis_size("row")
    me = lax.axis_index("row")
    count, size = h_blocks.shape[1:3]
    drop_h = dropped_offset(h_cols, me, total)
    drop_t = dropped_offset(t_cols, me, total)
    f32, bf16 = jnp.float32, jnp.bfloat16
    dma = pltpu.SemaphoreType.DMA
    row = jax.ShapeDtypeStruct((count, size, size), f32)
    row_scratch = pltpu.VMEM(row.shape, f32)

    def call(kernel, smem, arrays, outs, scratch, name, megabytes, aliases={}):
        return pl.pallas_call(
            kernel,
            out_shape=[pltpu.HBM(out.shape, out.dtype) for out in outs],
            in_specs=[SMEM] * len(smem) + [ANY] * len(arrays),
            out_specs=[ANY] * len(outs),
            scratch_shapes=scratch,
            input_output_aliases=aliases,
            compiler_params=pltpu.CompilerParams(vmem_limit_bytes=megabytes * 1024 * 1024),
            name=name,
        )(*smem, *arrays)

    def in_hbm(x):
        return pltpu.with_memory_space_constraint(x, pltpu.HBM)

    def exchange(x):
        return lax.all_to_all(x, "row", 0, 0, tiled=True)

    (send,) = call(
        functools.partial(pack_kernel, total),
        [jnp.stack([me, drop_h[0], drop_t[0]]), t_cols[0]],
        [term_cur[0], term_prev[0]],
        [jax.ShapeDtypeStruct((total, 2 * size + NOTE, size), f32)],
        [
            row_scratch,
            row_scratch,
            pltpu.VMEM((2 * size, size), f32),
            pltpu.VMEM((NOTE, size), f32),
            dma((3,)),
        ],
        "pack",
        60,
    )
    table, parts = window_table(total)
    gathered = gathered_rows(h_blocks[0], total, lambda *others: exchange(after(send, *others)))
    column = next(gathered)
    drops = column[:, 2 * size:2 * size + 2, 0].astype(jnp.int32).reshape(-1)
    rows = jnp.array(table, jnp.int32).reshape(-1)
    window = sum(parts)
    dense_shape = (window, 2 * size, window * size)
    pair_shape = (window * size, 2 * size)
    dense = []
    start = 0
    for part in parts:
        h_rows = gathered.send(dense[-1] if start else None)
        group = max(g for g in (2, 7, 13) if part % g == 0)
        scratch = [
            pltpu.VMEM((part, count, size, size), f32),
            pltpu.VMEM((min(2, part // group), group) + dense_shape[1:], bf16),
            pltpu.VMEM((part, size, size), f32),
            pltpu.VMEM(pair_shape, bf16),
            dma((part,)),
            dma,
            dma,
            dma,
            dma((2,)),
            dma,
        ]
        if not start:
            scratch = [pltpu.VMEM((window, size, size), f32)] + scratch
        result = call(
            functools.partial(first_kernel, total, window, start, part, group),
            [drops, me[None], rows],
            [in_hbm(column), *h_rows, in_hbm(pair), term1] if start else [column, *h_rows],
            [
                jax.ShapeDtypeStruct((part,) + dense_shape[1:], bf16),
                jax.ShapeDtypeStruct((total, size, size), f32),
            ] + ([] if start else [jax.ShapeDtypeStruct(pair_shape, bf16)]),
            scratch,
            "first",
            24 if start else 60,
            {part + 5: 1} if start else {},
        )
        dense.append(result[0])
        term1 = result[1]
        if not start:
            pair = result[2]
        start += part
    back1 = exchange(term1)
    group = max(g for g in (3, 4) if window % g == 0)
    (terms,) = call(
        functools.partial(later_kernel, total, window, group, parts),
        [drops, me[None], rows],
        [*dense, column, term1],
        [jax.ShapeDtypeStruct((total, 2, size, size), f32)],
        [
            pltpu.VMEM(dense_shape, bf16),
            pltpu.VMEM((window, 2, size, size), f32),
            pltpu.VMEM((2,) + pair_shape, bf16),
            dma((window // group,)),
            dma,
            dma,
            dma,
        ],
        "later",
        60,
    )
    back = exchange(after(terms, back1))
    (sums,) = call(
        unpack_first_kernel,
        [t_cols[0], coefs],
        [back1, density_in[0]],
        [row],
        [row_scratch, row_scratch, dma((2,))],
        "unpack_first",
        60,
    )
    density, last, before = call(
        unpack_last_kernel,
        [t_cols[0], coefs],
        [back, sums],
        [row] * 3,
        [row_scratch, row_scratch, row_scratch, dma((3,))],
        "unpack_last",
        60,
    )
    return density[None], last[None], before[None]


def solution(mesh):
    blocks = P(("groups", "row"), None, None, None)
    cols = P(("groups", "row"), None)
    return jax.shard_map(
        per_device,
        mesh=mesh,
        in_specs=(blocks, cols, blocks, blocks, cols, blocks, P()),
        out_specs=(blocks, blocks, blocks),
        check_vma=False,
    )
```

```python
import functools

import jax
import jax.numpy as jnp
from jax import lax
from jax.experimental import pallas as pl
from jax.experimental.pallas import tpu as pltpu
from jax.sharding import PartitionSpec as P

REACH = 7
NOTE = 8
SMEM = pl.BlockSpec(memory_space=pltpu.SMEM)
ANY = pl.BlockSpec(memory_space=pl.ANY)


def permute(x, target):
    devices = lax.axis_size("row")
    return lax.ppermute(x, "row", [(i, target(i)) for i in range(devices)])


def after(x, *others):
    return lax.optimization_barrier((x, *others))[0]


RING = (0, 2, 4, 6, 7, 5, 3, 1)


def along_ring(device, by):
    if device % 2:
        by = -by
    return 2 * RING[(RING.index(device // 2) + by) % len(RING)] + device % 2


def window_table(total):
    if total != 16:
        steps = [0] + [by for hop in range(1, REACH + 1) for by in (-hop, hop)]
        return [[(i + by) % total for by in steps] for i in range(total)], (13, 2)
    order = (0, -1, 1, -2, 2, -3, 3, -4)
    table = [[along_ring(source, by) for by in order for source in (i, i ^ 1)] for i in range(total)]
    return table, (14, 2)


def gathered_rows(x, total, exchange):
    if total != 16:
        rows = [x]
        for hop in range(1, REACH + 1):
            for by in (hop, -hop):
                rows.append(permute(x, lambda i, by=by: (i + by) % total))
        yield exchange()
        yield rows[:13]
        yield rows[13:]
        return

    def other_core(row):
        return permute(row, lambda i: i ^ 1)

    def round_of(ahead, behind):
        ahead = permute(ahead, lambda i: along_ring(i, 1))
        behind = permute(behind, lambda i: along_ring(i, -1))
        return ahead, behind, [ahead, other_core(ahead), behind, other_core(behind)]

    rows = [x, other_core(x)]
    ahead, behind, first = round_of(x, x)
    ahead, behind, second = round_of(ahead, behind)
    column = exchange(ahead, behind, rows[1], first[1], first[3])
    yield column
    ahead, behind, third = round_of(ahead, behind)
    far = permute(after(ahead, column), lambda i: along_ring(i, 1))
    made = yield rows + first + second + third
    far = after(far, made)
    yield [far, other_core(far)]


def place_of(offset, dropped):
    named = jnp.logical_and(offset <= 2 * REACH, offset != dropped)
    slot = offset - jnp.where(offset > dropped, 1, 0)
    return jnp.clip(slot, 0, 2 * REACH - 1), named


def dropped_offset(cols, row, total):
    offsets = jnp.mod(cols - row + REACH, total)
    return REACH * (2 * REACH + 1) - jnp.sum(offsets, axis=1)


def pack_kernel(total, info_ref, cols_ref, cur_ref, prev_ref, send_ref, cur, prev, zeros, note, sems):
    row = info_ref[0]
    drop = info_ref[2]
    count, size = cur.shape[:2]
    loads = (
        pltpu.make_async_copy(cur_ref, cur, sems.at[0]),
        pltpu.make_async_copy(prev_ref, prev, sems.at[1]),
    )
    for load in loads:
        load.start()
    zeros[...] = jnp.zeros_like(zeros)
    line = lax.broadcasted_iota(jnp.int32, note.shape, 0)
    note[...] = jnp.where(line == 0, info_ref[1], drop).astype(jnp.float32)

    def fill(j, carry):
        offset = lax.rem(j - row + REACH + total, total)
        _, named = place_of(offset, drop)
        pltpu.make_async_copy(note, send_ref.at[j, pl.ds(2 * size, NOTE)], sems.at[2]).start()

        @pl.when(jnp.logical_not(named))
        def _():
            pltpu.make_async_copy(zeros, send_ref.at[j, pl.ds(0, 2 * size)], sems.at[2]).start()

        return carry

    lax.fori_loop(0, total, fill, 0)
    for which, held in enumerate((cur, prev)):
        loads[which].wait()
        for k in range(count):
            place = send_ref.at[cols_ref[k], pl.ds(which * size, size)]
            pltpu.make_async_copy(held.at[k], place, sems.at[2]).start()
    pltpu.make_async_copy(send_ref, send_ref, sems.at[2]).wait()


def split(x):
    high = x.astype(jnp.bfloat16)
    low = (x - high.astype(jnp.float32)).astype(jnp.bfloat16)
    return high, low


class Rows:
    def __init__(self, total, me_ref, table_ref):
        self.me = me_ref[0]
        self.table_ref = table_ref
        self.window = table_ref.shape[0] // total

    def __getitem__(self, w):
        return self.table_ref[self.me * self.window + w]


def kept_rows(total, rows, drops_ref, w):
    row = rows[w]
    offset = lax.rem(rows.me - row + REACH + total, total)
    _, named = place_of(offset, drops_ref[2 * row + 1])
    return named


def fill_pair(pair, block, w):
    size = block.shape[-1]
    high, low = split(block)
    at = pl.ds(pl.multiple_of(w * size, size), size)
    pair[at, pl.ds(0, size)] = high
    pair[at, pl.ds(size, size)] = low


def products_of(rows, pair):
    group, double = rows.shape[:2]
    size = double // 2
    products = jnp.dot(rows.reshape(group * double, rows.shape[2]), pair, preferred_element_type=jnp.float32)
    for r in range(group):
        parts = products[r * double:r * double + size] + products[r * double + size:(r + 1) * double]
        yield parts[:, :size] + parts[:, size:]


def first_kernel(total, window, start, count, group, drops_ref, me_ref, table_ref, t_ref, *refs):
    rows = Rows(total, me_ref, table_ref)
    h_refs = refs[:count]
    if start:
        pair_in, _ = refs[count:count + 2]
        dense_ref, out_ref = refs[count + 2:count + 4]
    else:
        dense_ref, out_ref, pair_out, blocks = refs[count:count + 4]
    stage, dense, prev, pair, h_sem, t_sem, prev_sem, pair_sem, dense_sem, out_sem = refs[-10:]
    size = t_ref.shape[-1]
    kept = functools.partial(kept_rows, total, rows, drops_ref)

    if start:
        pltpu.make_async_copy(pair_in, pair, pair_sem).start()
    else:
        for w in range(window):
            pltpu.make_async_copy(t_ref.at[rows[w], pl.ds(0, size)], blocks.at[w], t_sem).start()
    for r in range(count):
        pltpu.make_async_copy(h_refs[r], stage.at[r], h_sem.at[r]).start()
    for r in range(count):
        block = t_ref.at[rows[start + r], pl.ds(size, size)]
        pltpu.make_async_copy(block, prev.at[r], prev_sem).start()
    if not start:
        pltpu.make_async_copy(blocks, blocks, t_sem).wait()
        for w in range(window):
            fill_pair(pair, jnp.where(kept(w), blocks[w], 0.0), w)
        pltpu.make_async_copy(pair, pair_out, pair_sem).start()

    def densify(r, slot, place):
        row = rows[start + r]
        drop = drops_ref[2 * row]
        for p in range(window):
            offset = lax.rem(rows[p] - row + REACH + total, total)
            k, named = place_of(offset, drop)
            high, low = split(jnp.where(named, stage[r, k], 0.0))
            dense[slot, place, pl.ds(0, size), pl.ds(p * size, size)] = high
            dense[slot, place, pl.ds(size, size), pl.ds(p * size, size)] = low

    def store(g):
        return pltpu.make_async_copy(dense.at[g % 2], dense_ref.at[pl.ds(g * group, group)], dense_sem.at[g % 2])

    def arrive(g):
        if g >= 2:
            store(g - 2).wait()
        for r in range(g * group, (g + 1) * group):
            pltpu.make_async_copy(stage.at[r], stage.at[r], h_sem.at[r]).wait()

    def prepare(g):
        for place in range(group):
            densify(g * group + place, g % 2, place)
        store(g).start()

    groups = count // group
    arrive(0)
    prepare(0)
    if start:
        pltpu.make_async_copy(pair, pair, pair_sem).wait()
    pltpu.make_async_copy(prev, prev, prev_sem).wait()
    for g in range(groups):
        if g + 1 < groups:
            arrive(g + 1)
        products = list(products_of(dense[g % 2], pair[...]))
        if g + 1 < groups:
            prepare(g + 1)
        for place, product in enumerate(products):
            r = g * group + place
            prev[r] = jnp.where(kept(start + r), 2.0 * product - prev[r], 0.0)
            pltpu.make_async_copy(prev.at[r], out_ref.at[rows[start + r]], out_sem).start()
    for g in range(max(groups - 2, 0), groups):
        store(g).wait()
    if not start:
        pltpu.make_async_copy(pair, pair, pair_sem).wait()
    pltpu.make_async_copy(prev, prev, out_sem).wait()


def later_kernel(total, window, group, parts, drops_ref, me_ref, table_ref, *refs):
    rows = Rows(total, me_ref, table_ref)
    dense_refs = refs[:len(parts)]
    t_ref, first_ref, out_ref, dense, terms, pairs, dense_sem, t_sem, first_sem, out_sem = refs[len(parts):]
    size = terms.shape[-1]
    groups = window // group
    kept = functools.partial(kept_rows, total, rows, drops_ref)
    for w in range(window):
        pltpu.make_async_copy(first_ref.at[rows[w]], terms.at[w, 1], first_sem).start()
    start = 0
    for part, dense_ref in zip(parts, dense_refs):
        for w in range(start, start + part):
            pltpu.make_async_copy(dense_ref.at[w - start], dense.at[w], dense_sem.at[w // group]).start()
        start += part
    for w in range(window):
        pltpu.make_async_copy(t_ref.at[rows[w], pl.ds(0, size)], terms.at[w, 0], t_sem).start()
    pltpu.make_async_copy(terms.at[:, 1], terms.at[:, 1], first_sem).wait()
    for w in range(window):
        fill_pair(pairs.at[0], terms[w, 1], w)
    pltpu.make_async_copy(terms.at[:, 0], terms.at[:, 0], t_sem).wait()

    def one(g, carry, step):
        held = dense.at[pl.ds(g * group, group)]
        if step == 0:
            pltpu.make_async_copy(held, held, dense_sem.at[g]).wait()
        for r, product in enumerate(products_of(held[...], pairs[step])):
            w = g * group + r
            newest = jnp.where(kept(w), 2.0 * product - terms[w, step], 0.0)
            terms[w, step] = newest
            if step == 0:
                fill_pair(pairs.at[1], newest, w)
            pltpu.make_async_copy(terms.at[w, step], out_ref.at[rows[w], step], out_sem).start()
        return carry

    for step in range(2):
        lax.fori_loop(0, groups, functools.partial(one, step=step), 0)
    pltpu.make_async_copy(terms, terms, out_sem).wait()


def unpack_first_kernel(cols_ref, coefs_ref, first_ref, density_ref, out_ref, sums, one, sems):
    load = pltpu.make_async_copy(density_ref, sums, sems.at[0])
    load.start()
    for k in range(cols_ref.shape[0]):
        pltpu.make_async_copy(first_ref.at[cols_ref[k]], one.at[k], sems.at[1]).start()
    load.wait()
    pltpu.make_async_copy(one, one, sems.at[1]).wait()
    sums[...] += coefs_ref[0] * one[...]
    store = pltpu.make_async_copy(sums, out_ref, sems.at[0])
    store.start()
    store.wait()


def unpack_last_kernel(cols_ref, coefs_ref, held_ref, sum_ref, density_ref, last_ref, before_ref, sums, two, three, sems):
    load = pltpu.make_async_copy(sum_ref, sums, sems.at[0])
    load.start()
    for place, sem, which in ((two, 1, 0), (three, 2, 1)):
        for k in range(cols_ref.shape[0]):
            pltpu.make_async_copy(held_ref.at[cols_ref[k], which], place.at[k], sems.at[sem]).start()
    pltpu.make_async_copy(two, two, sems.at[1]).wait()
    before = pltpu.make_async_copy(two, before_ref, sems.at[1])
    before.start()
    pltpu.make_async_copy(three, three, sems.at[2]).wait()
    last = pltpu.make_async_copy(three, last_ref, sems.at[2])
    last.start()
    load.wait()
    sums[...] = sums[...] + coefs_ref[1] * two[...] + coefs_ref[2] * three[...]
    store = pltpu.make_async_copy(sums, density_ref, sems.at[0])
    store.start()
    before.wait()
    last.wait()
    store.wait()


def per_device(h_blocks, h_cols, term_prev, term_cur, t_cols, density_in, coefs):
    total = lax.axis_size("row")
    me = lax.axis_index("row")
    count, size = h_blocks.shape[1:3]
    drop_h = dropped_offset(h_cols, me, total)
    drop_t = dropped_offset(t_cols, me, total)
    f32, bf16 = jnp.float32, jnp.bfloat16
    dma = pltpu.SemaphoreType.DMA
    row = jax.ShapeDtypeStruct((count, size, size), f32)
    row_scratch = pltpu.VMEM(row.shape, f32)

    def call(kernel, smem, arrays, outs, scratch, name, megabytes, aliases={}):
        return pl.pallas_call(
            kernel,
            out_shape=[pltpu.HBM(out.shape, out.dtype) for out in outs],
            in_specs=[SMEM] * len(smem) + [ANY] * len(arrays),
            out_specs=[ANY] * len(outs),
            scratch_shapes=scratch,
            input_output_aliases=aliases,
            compiler_params=pltpu.CompilerParams(vmem_limit_bytes=megabytes * 1024 * 1024),
            name=name,
        )(*smem, *arrays)

    def in_hbm(x):
        return pltpu.with_memory_space_constraint(x, pltpu.HBM)

    def exchange(x):
        return lax.all_to_all(x, "row", 0, 0, tiled=True)

    (send,) = call(
        functools.partial(pack_kernel, total),
        [jnp.stack([me, drop_h[0], drop_t[0]]), t_cols[0]],
        [term_cur[0], term_prev[0]],
        [jax.ShapeDtypeStruct((total, 2 * size + NOTE, size), f32)],
        [
            row_scratch,
            row_scratch,
            pltpu.VMEM((2 * size, size), f32),
            pltpu.VMEM((NOTE, size), f32),
            dma((3,)),
        ],
        "pack",
        60,
    )
    table, parts = window_table(total)
    gathered = gathered_rows(h_blocks[0], total, lambda *others: exchange(after(send, *others)))
    column = next(gathered)
    drops = column[:, 2 * size:2 * size + 2, 0].astype(jnp.int32).reshape(-1)
    rows = jnp.array(table, jnp.int32).reshape(-1)
    window = sum(parts)
    dense_shape = (window, 2 * size, window * size)
    pair_shape = (window * size, 2 * size)
    dense = []
    start = 0
    for part in parts:
        h_rows = gathered.send(dense[-1] if start else None)
        group = min(g for g in (2, 13) if part % g == 0)
        scratch = [
            pltpu.VMEM((part, count, size, size), f32),
            pltpu.VMEM((min(2, part // group), group) + dense_shape[1:], bf16),
            pltpu.VMEM((part, size, size), f32),
            pltpu.VMEM(pair_shape, bf16),
            dma((part,)),
            dma,
            dma,
            dma,
            dma((2,)),
            dma,
        ]
        if not start:
            scratch = [pltpu.VMEM((window, size, size), f32)] + scratch
        result = call(
            functools.partial(first_kernel, total, window, start, part, group),
            [drops, me[None], rows],
            [in_hbm(column), *h_rows, in_hbm(pair), term1] if start else [column, *h_rows],
            [
                jax.ShapeDtypeStruct((part,) + dense_shape[1:], bf16),
                jax.ShapeDtypeStruct((total, size, size), f32),
            ] + ([] if start else [jax.ShapeDtypeStruct(pair_shape, bf16)]),
            scratch,
            "first",
            24 if start else 60,
            {part + 5: 1} if start else {},
        )
        dense.append(result[0])
        term1 = result[1]
        if not start:
            pair = result[2]
        start += part
    back1 = exchange(term1)
    group = max(g for g in (3, 4) if window % g == 0)
    (terms,) = call(
        functools.partial(later_kernel, total, window, group, parts),
        [drops, me[None], rows],
        [*dense, column, term1],
        [jax.ShapeDtypeStruct((total, 2, size, size), f32)],
        [
            pltpu.VMEM(dense_shape, bf16),
            pltpu.VMEM((window, 2, size, size), f32),
            pltpu.VMEM((2,) + pair_shape, bf16),
            dma((window // group,)),
            dma,
            dma,
            dma,
        ],
        "later",
        60,
    )
    back = exchange(after(terms, back1))
    (sums,) = call(
        unpack_first_kernel,
        [t_cols[0], coefs],
        [back1, density_in[0]],
        [row],
        [row_scratch, row_scratch, dma((2,))],
        "unpack_first",
        60,
    )
    density, last, before = call(
        unpack_last_kernel,
        [t_cols[0], coefs],
        [back, sums],
        [row] * 3,
        [row_scratch, row_scratch, row_scratch, dma((3,))],
        "unpack_last",
        60,
    )
    return density[None], last[None], before[None]


def solution(mesh):
    blocks = P(("groups", "row"), None, None, None)
    cols = P(("groups", "row"), None)
    return jax.shard_map(
        per_device,
        mesh=mesh,
        in_specs=(blocks, cols, blocks, blocks, cols, blocks, P()),
        out_specs=(blocks, blocks, blocks),
        check_vma=False,
    )
```

```python
import functools

import jax
import jax.numpy as jnp
from jax import lax
from jax.experimental import pallas as pl
from jax.experimental.pallas import tpu as pltpu
from jax.sharding import PartitionSpec as P

REACH = 7
NOTE = 8
SMEM = pl.BlockSpec(memory_space=pltpu.SMEM)
ANY = pl.BlockSpec(memory_space=pl.ANY)


def permute(x, target):
    devices = lax.axis_size("row")
    return lax.ppermute(x, "row", [(i, target(i)) for i in range(devices)])


def after(x, *others):
    return lax.optimization_barrier((x, *others))[0]


RING = (0, 2, 4, 6, 7, 5, 3, 1)


def along_ring(device, by):
    if device % 2:
        by = -by
    return 2 * RING[(RING.index(device // 2) + by) % len(RING)] + device % 2


def window_table(total):
    if total != 16:
        steps = [0] + [by for hop in range(1, REACH + 1) for by in (-hop, hop)]
        return [[(i + by) % total for by in steps] for i in range(total)], (13, 2)
    order = (0, -1, 1, -2, 2, -3, 3, -4)
    table = [[along_ring(source, by) for by in order for source in (i, i ^ 1)] for i in range(total)]
    return table, (14, 2)


def gathered_rows(x, total, exchange):
    if total != 16:
        rows = [x]
        for hop in range(1, REACH + 1):
            for by in (hop, -hop):
                rows.append(permute(x, lambda i, by=by: (i + by) % total))
        yield exchange()
        yield rows[:13]
        yield rows[13:]
        return

    def other_core(row):
        return permute(row, lambda i: i ^ 1)

    def round_of(ahead, behind):
        ahead = permute(ahead, lambda i: along_ring(i, 1))
        behind = permute(behind, lambda i: along_ring(i, -1))
        return ahead, behind, [ahead, other_core(ahead), behind, other_core(behind)]

    rows = [x, other_core(x)]
    ahead, behind, first = round_of(x, x)
    ahead, behind, second = round_of(ahead, behind)
    column = exchange(ahead, behind, rows[1], first[1], first[3])
    yield column
    ahead, behind, third = round_of(ahead, behind)
    far = permute(after(ahead, column), lambda i: along_ring(i, 1))
    made = yield rows + first + second + third
    far = after(far, made)
    yield [far, other_core(far)]


def place_of(offset, dropped):
    named = jnp.logical_and(offset <= 2 * REACH, offset != dropped)
    slot = offset - jnp.where(offset > dropped, 1, 0)
    return jnp.clip(slot, 0, 2 * REACH - 1), named


def dropped_offset(cols, row, total):
    offsets = jnp.mod(cols - row + REACH, total)
    return REACH * (2 * REACH + 1) - jnp.sum(offsets, axis=1)


def pack_kernel(total, info_ref, cols_ref, cur_ref, prev_ref, send_ref, cur, prev, zeros, note, sems):
    row = info_ref[0]
    drop = info_ref[2]
    count, size = cur.shape[:2]
    loads = (
        pltpu.make_async_copy(cur_ref, cur, sems.at[0]),
        pltpu.make_async_copy(prev_ref, prev, sems.at[1]),
    )
    for load in loads:
        load.start()
    zeros[...] = jnp.zeros_like(zeros)
    line = lax.broadcasted_iota(jnp.int32, note.shape, 0)
    note[...] = jnp.where(line == 0, info_ref[1], drop).astype(jnp.float32)

    def fill(j, carry):
        offset = lax.rem(j - row + REACH + total, total)
        _, named = place_of(offset, drop)
        pltpu.make_async_copy(note, send_ref.at[j, pl.ds(2 * size, NOTE)], sems.at[2]).start()

        @pl.when(jnp.logical_not(named))
        def _():
            pltpu.make_async_copy(zeros, send_ref.at[j, pl.ds(0, 2 * size)], sems.at[2]).start()

        return carry

    lax.fori_loop(0, total, fill, 0)
    for which, held in enumerate((cur, prev)):
        loads[which].wait()
        for k in range(count):
            place = send_ref.at[cols_ref[k], pl.ds(which * size, size)]
            pltpu.make_async_copy(held.at[k], place, sems.at[2]).start()
    pltpu.make_async_copy(send_ref, send_ref, sems.at[2]).wait()


def split(x):
    high = x.astype(jnp.bfloat16)
    low = (x - high.astype(jnp.float32)).astype(jnp.bfloat16)
    return high, low


class Rows:
    def __init__(self, total, me_ref, table_ref):
        self.me = me_ref[0]
        self.table_ref = table_ref
        self.window = table_ref.shape[0] // total

    def __getitem__(self, w):
        return self.table_ref[self.me * self.window + w]


def kept_rows(total, rows, drops_ref, w):
    row = rows[w]
    offset = lax.rem(rows.me - row + REACH + total, total)
    _, named = place_of(offset, drops_ref[2 * row + 1])
    return named


def fill_pair(pair, block, w):
    size = block.shape[-1]
    high, low = split(block)
    at = pl.ds(pl.multiple_of(w * size, size), size)
    pair[at, pl.ds(0, size)] = high
    pair[at, pl.ds(size, size)] = low


def products_of(rows, pair):
    group, double = rows.shape[:2]
    size = double // 2
    products = jnp.dot(rows.reshape(group * double, rows.shape[2]), pair, preferred_element_type=jnp.float32)
    for r in range(group):
        parts = products[r * double:r * double + size] + products[r * double + size:(r + 1) * double]
        yield parts[:, :size] + parts[:, size:]


def first_kernel(total, window, start, count, group, drops_ref, me_ref, table_ref, t_ref, *refs):
    rows = Rows(total, me_ref, table_ref)
    h_refs = refs[:count]
    if start:
        pair_in, _ = refs[count:count + 2]
        dense_ref, out_ref = refs[count + 2:count + 4]
    else:
        dense_ref, out_ref, pair_out, blocks = refs[count:count + 4]
    stage, dense, prev, pair, h_sem, t_sem, prev_sem, pair_sem, dense_sem, out_sem = refs[-10:]
    size = t_ref.shape[-1]
    kept = functools.partial(kept_rows, total, rows, drops_ref)

    if start:
        pltpu.make_async_copy(pair_in, pair, pair_sem).start()
    else:
        for w in range(window):
            pltpu.make_async_copy(t_ref.at[rows[w], pl.ds(0, size)], blocks.at[w], t_sem).start()
    for r in range(count):
        pltpu.make_async_copy(h_refs[r], stage.at[r], h_sem.at[r]).start()
    for r in range(count):
        block = t_ref.at[rows[start + r], pl.ds(size, size)]
        pltpu.make_async_copy(block, prev.at[r], prev_sem).start()
    if not start:
        pltpu.make_async_copy(blocks, blocks, t_sem).wait()
        for w in range(window):
            fill_pair(pair, jnp.where(kept(w), blocks[w], 0.0), w)
        pltpu.make_async_copy(pair, pair_out, pair_sem).start()

    def densify(r, slot, place):
        row = rows[start + r]
        drop = drops_ref[2 * row]
        for p in range(window):
            offset = lax.rem(rows[p] - row + REACH + total, total)
            k, named = place_of(offset, drop)
            high, low = split(jnp.where(named, stage[r, k], 0.0))
            dense[slot, place, pl.ds(0, size), pl.ds(p * size, size)] = high
            dense[slot, place, pl.ds(size, size), pl.ds(p * size, size)] = low

    def store(g):
        return pltpu.make_async_copy(dense.at[g % 2], dense_ref.at[pl.ds(g * group, group)], dense_sem.at[g % 2])

    def arrive(g):
        if g >= 2:
            store(g - 2).wait()
        for r in range(g * group, (g + 1) * group):
            pltpu.make_async_copy(stage.at[r], stage.at[r], h_sem.at[r]).wait()

    def prepare(g):
        for place in range(group):
            densify(g * group + place, g % 2, place)
        store(g).start()

    groups = count // group
    arrive(0)
    prepare(0)
    if start:
        pltpu.make_async_copy(pair, pair, pair_sem).wait()
    pltpu.make_async_copy(prev, prev, prev_sem).wait()
    for g in range(groups):
        if g + 1 < groups:
            arrive(g + 1)
        products = list(products_of(dense[g % 2], pair[...]))
        if g + 1 < groups:
            prepare(g + 1)
        for place, product in enumerate(products):
            r = g * group + place
            prev[r] = jnp.where(kept(start + r), 2.0 * product - prev[r], 0.0)
            pltpu.make_async_copy(prev.at[r], out_ref.at[rows[start + r]], out_sem).start()
    for g in range(max(groups - 2, 0), groups):
        store(g).wait()
    if not start:
        pltpu.make_async_copy(pair, pair, pair_sem).wait()
    pltpu.make_async_copy(prev, prev, out_sem).wait()


def later_kernel(total, window, group, parts, drops_ref, me_ref, table_ref, *refs):
    rows = Rows(total, me_ref, table_ref)
    dense_refs = refs[:len(parts)]
    t_ref, first_ref, out_ref, dense, terms, pairs, dense_sem, t_sem, first_sem, out_sem = refs[len(parts):]
    size = terms.shape[-1]
    groups = window // group
    kept = functools.partial(kept_rows, total, rows, drops_ref)
    for w in range(window):
        pltpu.make_async_copy(first_ref.at[rows[w]], terms.at[w, 1], first_sem).start()
    start = 0
    for part, dense_ref in zip(parts, dense_refs):
        for w in range(start, start + part):
            pltpu.make_async_copy(dense_ref.at[w - start], dense.at[w], dense_sem.at[w // group]).start()
        start += part
    for w in range(window):
        pltpu.make_async_copy(t_ref.at[rows[w], pl.ds(0, size)], terms.at[w, 0], t_sem).start()
    pltpu.make_async_copy(terms.at[:, 1], terms.at[:, 1], first_sem).wait()
    for w in range(window):
        fill_pair(pairs.at[0], terms[w, 1], w)
    pltpu.make_async_copy(terms.at[:, 0], terms.at[:, 0], t_sem).wait()

    def one(g, carry, step):
        held = dense.at[pl.ds(g * group, group)]
        if step == 0:
            pltpu.make_async_copy(held, held, dense_sem.at[g]).wait()
        for r, product in enumerate(products_of(held[...], pairs[step])):
            w = g * group + r
            newest = jnp.where(kept(w), 2.0 * product - terms[w, step], 0.0)
            terms[w, step] = newest
            if step == 0:
                fill_pair(pairs.at[1], newest, w)
            pltpu.make_async_copy(terms.at[w, step], out_ref.at[rows[w], step], out_sem).start()
        return carry

    for step in range(2):
        lax.fori_loop(0, groups, functools.partial(one, step=step), 0)
    pltpu.make_async_copy(terms, terms, out_sem).wait()


def unpack_first_kernel(cols_ref, coefs_ref, first_ref, density_ref, out_ref, sums, one, sems):
    load = pltpu.make_async_copy(density_ref, sums, sems.at[0])
    load.start()
    for k in range(cols_ref.shape[0]):
        pltpu.make_async_copy(first_ref.at[cols_ref[k]], one.at[k], sems.at[1]).start()
    load.wait()
    pltpu.make_async_copy(one, one, sems.at[1]).wait()
    sums[...] += coefs_ref[0] * one[...]
    store = pltpu.make_async_copy(sums, out_ref, sems.at[0])
    store.start()
    store.wait()


def unpack_last_kernel(cols_ref, coefs_ref, held_ref, sum_ref, density_ref, last_ref, before_ref, sums, two, three, sems):
    load = pltpu.make_async_copy(sum_ref, sums, sems.at[0])
    load.start()
    for place, sem, which in ((two, 1, 0), (three, 2, 1)):
        for k in range(cols_ref.shape[0]):
            pltpu.make_async_copy(held_ref.at[cols_ref[k], which], place.at[k], sems.at[sem]).start()
    pltpu.make_async_copy(two, two, sems.at[1]).wait()
    before = pltpu.make_async_copy(two, before_ref, sems.at[1])
    before.start()
    pltpu.make_async_copy(three, three, sems.at[2]).wait()
    last = pltpu.make_async_copy(three, last_ref, sems.at[2])
    last.start()
    load.wait()
    sums[...] = sums[...] + coefs_ref[1] * two[...] + coefs_ref[2] * three[...]
    store = pltpu.make_async_copy(sums, density_ref, sems.at[0])
    store.start()
    before.wait()
    last.wait()
    store.wait()


def per_device(h_blocks, h_cols, term_prev, term_cur, t_cols, density_in, coefs):
    total = lax.axis_size("row")
    me = lax.axis_index("row")
    count, size = h_blocks.shape[1:3]
    drop_h = dropped_offset(h_cols, me, total)
    drop_t = dropped_offset(t_cols, me, total)
    f32, bf16 = jnp.float32, jnp.bfloat16
    dma = pltpu.SemaphoreType.DMA
    row = jax.ShapeDtypeStruct((count, size, size), f32)
    row_scratch = pltpu.VMEM(row.shape, f32)

    def call(kernel, smem, arrays, outs, scratch, name, megabytes, aliases={}):
        return pl.pallas_call(
            kernel,
            out_shape=[pltpu.HBM(out.shape, out.dtype) for out in outs],
            in_specs=[SMEM] * len(smem) + [ANY] * len(arrays),
            out_specs=[ANY] * len(outs),
            scratch_shapes=scratch,
            input_output_aliases=aliases,
            compiler_params=pltpu.CompilerParams(vmem_limit_bytes=megabytes * 1024 * 1024),
            name=name,
        )(*smem, *arrays)

    def in_hbm(x):
        return pltpu.with_memory_space_constraint(x, pltpu.HBM)

    def exchange(x):
        return lax.all_to_all(x, "row", 0, 0, tiled=True)

    (send,) = call(
        functools.partial(pack_kernel, total),
        [jnp.stack([me, drop_h[0], drop_t[0]]), t_cols[0]],
        [term_cur[0], term_prev[0]],
        [jax.ShapeDtypeStruct((total, 2 * size + NOTE, size), f32)],
        [
            row_scratch,
            row_scratch,
            pltpu.VMEM((2 * size, size), f32),
            pltpu.VMEM((NOTE, size), f32),
            dma((3,)),
        ],
        "pack",
        60,
    )
    table, parts = window_table(total)
    gathered = gathered_rows(h_blocks[0], total, lambda *others: exchange(after(send, *others)))
    column = next(gathered)
    drops = column[:, 2 * size:2 * size + 2, 0].astype(jnp.int32).reshape(-1)
    rows = jnp.array(table, jnp.int32).reshape(-1)
    window = sum(parts)
    dense_shape = (window, 2 * size, window * size)
    pair_shape = (window * size, 2 * size)
    dense = []
    start = 0
    for part in parts:
        h_rows = gathered.send(dense[-1] if start else None)
        group = max(g for g in (2, 7, 13) if part % g == 0)
        scratch = [
            pltpu.VMEM((part, count, size, size), f32),
            pltpu.VMEM((min(2, part // group), group) + dense_shape[1:], bf16),
            pltpu.VMEM((part, size, size), f32),
            pltpu.VMEM(pair_shape, bf16),
            dma((part,)),
            dma,
            dma,
            dma,
            dma((2,)),
            dma,
        ]
        if not start:
            scratch = [pltpu.VMEM((window, size, size), f32)] + scratch
        result = call(
            functools.partial(first_kernel, total, window, start, part, group),
            [drops, me[None], rows],
            [in_hbm(column), *h_rows, in_hbm(pair), term1] if start else [column, *h_rows],
            [
                jax.ShapeDtypeStruct((part,) + dense_shape[1:], bf16),
                jax.ShapeDtypeStruct((total, size, size), f32),
            ] + ([] if start else [jax.ShapeDtypeStruct(pair_shape, bf16)]),
            scratch,
            "first",
            24 if start else 60,
            {part + 5: 1} if start else {},
        )
        dense.append(result[0])
        term1 = result[1]
        if not start:
            pair = result[2]
        start += part
    back1 = exchange(term1)
    group = max(g for g in (3, 4) if window % g == 0)
    (terms,) = call(
        functools.partial(later_kernel, total, window, group, parts),
        [drops, me[None], rows],
        [*dense, column, term1],
        [jax.ShapeDtypeStruct((total, 2, size, size), f32)],
        [
            pltpu.VMEM(dense_shape, bf16),
            pltpu.VMEM((window, 2, size, size), f32),
            pltpu.VMEM((2,) + pair_shape, bf16),
            dma((window // group,)),
            dma,
            dma,
            dma,
        ],
        "later",
        60,
    )
    back = exchange(after(terms, back1))
    (sums,) = call(
        unpack_first_kernel,
        [t_cols[0], coefs],
        [back1, density_in[0]],
        [row],
        [row_scratch, row_scratch, dma((2,))],
        "unpack_first",
        60,
    )
    density, last, before = call(
        unpack_last_kernel,
        [t_cols[0], coefs],
        [back, sums],
        [row] * 3,
        [row_scratch, row_scratch, row_scratch, dma((3,))],
        "unpack_last",
        60,
    )
    return density[None], last[None], before[None]


def solution(mesh):
    blocks = P(("groups", "row"), None, None, None)
    cols = P(("groups", "row"), None)
    return jax.shard_map(
        per_device,
        mesh=mesh,
        in_specs=(blocks, cols, blocks, blocks, cols, blocks, P()),
        out_specs=(blocks, blocks, blocks),
        check_vma=False,
    )
```

```python
import functools

import jax
import jax.numpy as jnp
from jax import lax
from jax.experimental import pallas as pl
from jax.experimental.pallas import tpu as pltpu
from jax.sharding import PartitionSpec as P

REACH = 7
NOTE = 8
SMEM = pl.BlockSpec(memory_space=pltpu.SMEM)
ANY = pl.BlockSpec(memory_space=pl.ANY)


def permute(x, target):
    devices = lax.axis_size("row")
    return lax.ppermute(x, "row", [(i, target(i)) for i in range(devices)])


def after(x, *others):
    return lax.optimization_barrier((x, *others))[0]


RING = (0, 2, 4, 6, 7, 5, 3, 1)


def along_ring(device, by):
    if device % 2:
        by = -by
    return 2 * RING[(RING.index(device // 2) + by) % len(RING)] + device % 2


def window_table(total):
    if total != 16:
        steps = [0] + [by for hop in range(1, REACH + 1) for by in (-hop, hop)]
        return [[(i + by) % total for by in steps] for i in range(total)], (13, 2)
    order = (0, -1, 1, -2, 2, -3, 3, -4)
    table = [[along_ring(source, by) for by in order for source in (i, i ^ 1)] for i in range(total)]
    return table, (14, 2)


def gathered_rows(x, total, exchange):
    if total != 16:
        rows = [x]
        for hop in range(1, REACH + 1):
            for by in (hop, -hop):
                rows.append(permute(x, lambda i, by=by: (i + by) % total))
        yield exchange()
        yield rows[:13]
        yield rows[13:]
        return

    def other_core(row):
        return permute(row, lambda i: i ^ 1)

    def round_of(ahead, behind):
        ahead = permute(ahead, lambda i: along_ring(i, 1))
        behind = permute(behind, lambda i: along_ring(i, -1))
        return ahead, behind, [ahead, other_core(ahead), behind, other_core(behind)]

    rows = [x, other_core(x)]
    ahead, behind, first = round_of(x, x)
    ahead, behind, second = round_of(ahead, behind)
    column = exchange(ahead, behind, rows[1], first[1], first[3])
    yield column
    ahead, behind, third = round_of(ahead, behind)
    far = permute(after(ahead, column), lambda i: along_ring(i, 1))
    made = yield rows + first + second + third
    far = after(far, made)
    yield [far, other_core(far)]


def place_of(offset, dropped):
    named = jnp.logical_and(offset <= 2 * REACH, offset != dropped)
    slot = offset - jnp.where(offset > dropped, 1, 0)
    return jnp.clip(slot, 0, 2 * REACH - 1), named


def dropped_offset(cols, row, total):
    offsets = jnp.mod(cols - row + REACH, total)
    return REACH * (2 * REACH + 1) - jnp.sum(offsets, axis=1)


def pack_kernel(total, info_ref, cols_ref, cur_ref, prev_ref, send_ref, cur, prev, zeros, note, sems):
    row = info_ref[0]
    drop = info_ref[2]
    count, size = cur.shape[:2]
    loads = (
        pltpu.make_async_copy(cur_ref, cur, sems.at[0]),
        pltpu.make_async_copy(prev_ref, prev, sems.at[1]),
    )
    for load in loads:
        load.start()
    zeros[...] = jnp.zeros_like(zeros)
    line = lax.broadcasted_iota(jnp.int32, note.shape, 0)
    note[...] = jnp.where(line == 0, info_ref[1], drop).astype(jnp.float32)

    def fill(j, carry):
        offset = lax.rem(j - row + REACH + total, total)
        _, named = place_of(offset, drop)
        pltpu.make_async_copy(note, send_ref.at[j, pl.ds(2 * size, NOTE)], sems.at[2]).start()

        @pl.when(jnp.logical_not(named))
        def _():
            pltpu.make_async_copy(zeros, send_ref.at[j, pl.ds(0, 2 * size)], sems.at[2]).start()

        return carry

    lax.fori_loop(0, total, fill, 0)
    for which, held in enumerate((cur, prev)):
        loads[which].wait()
        for k in range(count):
            place = send_ref.at[cols_ref[k], pl.ds(which * size, size)]
            pltpu.make_async_copy(held.at[k], place, sems.at[2]).start()
    pltpu.make_async_copy(send_ref, send_ref, sems.at[2]).wait()


def split(x):
    high = x.astype(jnp.bfloat16)
    low = (x - high.astype(jnp.float32)).astype(jnp.bfloat16)
    return high, low


class Rows:
    def __init__(self, total, me_ref, table_ref):
        self.me = me_ref[0]
        self.table_ref = table_ref
        self.window = table_ref.shape[0] // total

    def __getitem__(self, w):
        return self.table_ref[self.me * self.window + w]


def kept_rows(total, rows, drops_ref, w):
    row = rows[w]
    offset = lax.rem(rows.me - row + REACH + total, total)
    _, named = place_of(offset, drops_ref[row, 1])
    return named


def fill_pair(pair, block, w):
    size = block.shape[-1]
    high, low = split(block)
    at = pl.ds(pl.multiple_of(w * size, size), size)
    pair[at, pl.ds(0, size)] = high
    pair[at, pl.ds(size, size)] = low


def products_of(rows, pair):
    group, double = rows.shape[:2]
    size = double // 2
    products = jnp.dot(rows.reshape(group * double, rows.shape[2]), pair, preferred_element_type=jnp.float32)
    for r in range(group):
        parts = products[r * double:r * double + size] + products[r * double + size:(r + 1) * double]
        yield parts[:, :size] + parts[:, size:]


def first_kernel(total, window, start, count, group, drops_ref, me_ref, table_ref, t_ref, *refs):
    rows = Rows(total, me_ref, table_ref)
    h_refs = refs[:count]
    if start:
        pair_in, _ = refs[count:count + 2]
        dense_ref, out_ref = refs[count + 2:count + 4]
    else:
        dense_ref, out_ref, pair_out, blocks = refs[count:count + 4]
    stage, dense, prev, pair, h_sem, t_sem, prev_sem, pair_sem, dense_sem, out_sem = refs[-10:]
    size = t_ref.shape[-1]
    kept = functools.partial(kept_rows, total, rows, drops_ref)

    if start:
        pltpu.make_async_copy(pair_in, pair, pair_sem).start()
    else:
        for w in range(window):
            pltpu.make_async_copy(t_ref.at[rows[w], pl.ds(0, size)], blocks.at[w], t_sem).start()
    for r in range(count):
        pltpu.make_async_copy(h_refs[r], stage.at[r], h_sem.at[r]).start()
    for r in range(count):
        block = t_ref.at[rows[start + r], pl.ds(size, size)]
        pltpu.make_async_copy(block, prev.at[r], prev_sem).start()
    if not start:
        pltpu.make_async_copy(blocks, blocks, t_sem).wait()
        for w in range(window):
            fill_pair(pair, jnp.where(kept(w), blocks[w], 0.0), w)
        pltpu.make_async_copy(pair, pair_out, pair_sem).start()

    def densify(r, slot, place):
        row = rows[start + r]
        drop = drops_ref[row, 0]
        for p in range(window):
            offset = lax.rem(rows[p] - row + REACH + total, total)
            k, named = place_of(offset, drop)
            high, low = split(jnp.where(named, stage[r, k], 0.0))
            dense[slot, place, pl.ds(0, size), pl.ds(p * size, size)] = high
            dense[slot, place, pl.ds(size, size), pl.ds(p * size, size)] = low

    def store(g, slot):
        return pltpu.make_async_copy(dense.at[slot], dense_ref.at[pl.ds(g * group, group)], dense_sem.at[slot])

    groups = count // group

    def one(g, carry):
        slot = lax.rem(g, 2)

        @pl.when(g >= 2)
        def _():
            store(g - 2, slot).wait()

        def ready(place, carry):
            r = g * group + place
            pltpu.make_async_copy(stage.at[r], stage.at[r], h_sem.at[r]).wait()
            densify(r, slot, place)
            return carry

        lax.fori_loop(0, group, ready, 0)
        store(g, slot).start()
        if start:

            @pl.when(g == 0)
            def _():
                pltpu.make_async_copy(pair, pair, pair_sem).wait()

        @pl.when(g == 0)
        def _():
            pltpu.make_async_copy(prev, prev, prev_sem).wait()

        for place, product in enumerate(products_of(dense[slot], pair[...])):
            r = g * group + place
            prev[r] = jnp.where(kept(start + r), 2.0 * product - prev[r], 0.0)
            pltpu.make_async_copy(prev.at[r], out_ref.at[rows[start + r]], out_sem).start()
        return carry

    lax.fori_loop(0, groups, one, 0)
    for g in range(max(groups - 2, 0), groups):
        store(g, g % 2).wait()
    if not start:
        pltpu.make_async_copy(pair, pair, pair_sem).wait()
    pltpu.make_async_copy(prev, prev, out_sem).wait()


def later_kernel(total, window, group, parts, drops_ref, me_ref, table_ref, *refs):
    rows = Rows(total, me_ref, table_ref)
    dense_refs = refs[:len(parts)]
    t_ref, first_ref, out_ref, dense, terms, pairs, dense_sem, t_sem, first_sem, out_sem = refs[len(parts):]
    size = terms.shape[-1]
    groups = window // group
    kept = functools.partial(kept_rows, total, rows, drops_ref)
    for w in range(window):
        pltpu.make_async_copy(first_ref.at[rows[w]], terms.at[w, 1], first_sem).start()
    start = 0
    for part, dense_ref in zip(parts, dense_refs):
        for w in range(start, start + part):
            pltpu.make_async_copy(dense_ref.at[w - start], dense.at[w], dense_sem.at[w // group]).start()
        start += part
    for w in range(window):
        pltpu.make_async_copy(t_ref.at[rows[w], pl.ds(0, size)], terms.at[w, 0], t_sem).start()
    pltpu.make_async_copy(terms.at[:, 1], terms.at[:, 1], first_sem).wait()
    for w in range(window):
        fill_pair(pairs.at[0], terms[w, 1], w)
    pltpu.make_async_copy(terms.at[:, 0], terms.at[:, 0], t_sem).wait()

    def one(g, carry, step):
        held = dense.at[pl.ds(g * group, group)]
        if step == 0:
            pltpu.make_async_copy(held, held, dense_sem.at[g]).wait()
        for r, product in enumerate(products_of(held[...], pairs[step])):
            w = g * group + r
            newest = jnp.where(kept(w), 2.0 * product - terms[w, step], 0.0)
            terms[w, step] = newest
            if step == 0:
                fill_pair(pairs.at[1], newest, w)
            pltpu.make_async_copy(terms.at[w, step], out_ref.at[rows[w], step], out_sem).start()
        return carry

    for step in range(2):
        lax.fori_loop(0, groups, functools.partial(one, step=step), 0)
    pltpu.make_async_copy(terms, terms, out_sem).wait()


def unpack_first_kernel(cols_ref, coefs_ref, first_ref, density_ref, out_ref, sums, one, sems):
    load = pltpu.make_async_copy(density_ref, sums, sems.at[0])
    load.start()
    for k in range(cols_ref.shape[0]):
        pltpu.make_async_copy(first_ref.at[cols_ref[k]], one.at[k], sems.at[1]).start()
    load.wait()
    pltpu.make_async_copy(one, one, sems.at[1]).wait()
    sums[...] += coefs_ref[0] * one[...]
    store = pltpu.make_async_copy(sums, out_ref, sems.at[0])
    store.start()
    store.wait()


def unpack_last_kernel(cols_ref, coefs_ref, held_ref, sum_ref, density_ref, last_ref, before_ref, sums, two, three, sems):
    load = pltpu.make_async_copy(sum_ref, sums, sems.at[0])
    load.start()
    for place, sem, which in ((two, 1, 0), (three, 2, 1)):
        for k in range(cols_ref.shape[0]):
            pltpu.make_async_copy(held_ref.at[cols_ref[k], which], place.at[k], sems.at[sem]).start()
    pltpu.make_async_copy(two, two, sems.at[1]).wait()
    before = pltpu.make_async_copy(two, before_ref, sems.at[1])
    before.start()
    pltpu.make_async_copy(three, three, sems.at[2]).wait()
    last = pltpu.make_async_copy(three, last_ref, sems.at[2])
    last.start()
    load.wait()
    sums[...] = sums[...] + coefs_ref[1] * two[...] + coefs_ref[2] * three[...]
    store = pltpu.make_async_copy(sums, density_ref, sems.at[0])
    store.start()
    before.wait()
    last.wait()
    store.wait()


def per_device(h_blocks, h_cols, term_prev, term_cur, t_cols, density_in, coefs):
    total = lax.axis_size("row")
    me = lax.axis_index("row")
    count, size = h_blocks.shape[1:3]
    drop_h = dropped_offset(h_cols, me, total)
    drop_t = dropped_offset(t_cols, me, total)
    f32, bf16 = jnp.float32, jnp.bfloat16
    dma = pltpu.SemaphoreType.DMA
    row = jax.ShapeDtypeStruct((count, size, size), f32)
    row_scratch = pltpu.VMEM(row.shape, f32)

    def call(kernel, smem, arrays, outs, scratch, name, megabytes, aliases={}):
        return pl.pallas_call(
            kernel,
            out_shape=[pltpu.HBM(out.shape, out.dtype) for out in outs],
            in_specs=[SMEM] * len(smem) + [ANY] * len(arrays),
            out_specs=[ANY] * len(outs),
            scratch_shapes=scratch,
            input_output_aliases=aliases,
            compiler_params=pltpu.CompilerParams(vmem_limit_bytes=megabytes * 1024 * 1024),
            name=name,
        )(*smem, *arrays)

    def in_hbm(x):
        return pltpu.with_memory_space_constraint(x, pltpu.HBM)

    def exchange(x):
        return lax.all_to_all(x, "row", 0, 0, tiled=True)

    (send,) = call(
        functools.partial(pack_kernel, total),
        [jnp.stack([me, drop_h[0], drop_t[0]]), t_cols[0]],
        [term_cur[0], term_prev[0]],
        [jax.ShapeDtypeStruct((total, 2 * size + NOTE, size), f32)],
        [
            row_scratch,
            row_scratch,
            pltpu.VMEM((2 * size, size), f32),
            pltpu.VMEM((NOTE, size), f32),
            dma((3,)),
        ],
        "pack",
        60,
    )
    table, parts = window_table(total)
    gathered = gathered_rows(h_blocks[0], total, lambda *others: exchange(after(send, *others)))
    column = next(gathered)
    drops = column[:, 2 * size:2 * size + 2, 0].astype(jnp.int32)
    rows = jnp.array(table, jnp.int32).reshape(-1)
    window = sum(parts)
    dense_shape = (window, 2 * size, window * size)
    pair_shape = (window * size, 2 * size)
    dense = []
    start = 0
    for part in parts:
        h_rows = gathered.send(dense[-1] if start else None)
        group = max(g for g in (2, 13, 14) if part % g == 0)
        scratch = [
            pltpu.VMEM((part, count, size, size), f32),
            pltpu.VMEM((min(2, part // group), group) + dense_shape[1:], bf16),
            pltpu.VMEM((part, size, size), f32),
            pltpu.VMEM(pair_shape, bf16),
            dma((part,)),
            dma,
            dma,
            dma,
            dma((2,)),
            dma,
        ]
        if not start:
            scratch = [pltpu.VMEM((window, size, size), f32)] + scratch
        result = call(
            functools.partial(first_kernel, total, window, start, part, group),
            [drops, me[None], rows],
            [in_hbm(column), *h_rows, in_hbm(pair), term1] if start else [column, *h_rows],
            [
                jax.ShapeDtypeStruct((part,) + dense_shape[1:], bf16),
                jax.ShapeDtypeStruct((total, size, size), f32),
            ] + ([] if start else [jax.ShapeDtypeStruct(pair_shape, bf16)]),
            scratch,
            "first",
            24 if start else 60,
            {part + 5: 1} if start else {},
        )
        dense.append(result[0])
        term1 = result[1]
        if not start:
            pair = result[2]
        start += part
    back1 = exchange(term1)
    group = max(g for g in (3, 4) if window % g == 0)
    (terms,) = call(
        functools.partial(later_kernel, total, window, group, parts),
        [drops, me[None], rows],
        [*dense, column, term1],
        [jax.ShapeDtypeStruct((total, 2, size, size), f32)],
        [
            pltpu.VMEM(dense_shape, bf16),
            pltpu.VMEM((window, 2, size, size), f32),
            pltpu.VMEM((2,) + pair_shape, bf16),
            dma((window // group,)),
            dma,
            dma,
            dma,
        ],
        "later",
        60,
    )
    back = exchange(after(terms, back1))
    (sums,) = call(
        unpack_first_kernel,
        [t_cols[0], coefs],
        [back1, density_in[0]],
        [row],
        [row_scratch, row_scratch, dma((2,))],
        "unpack_first",
        60,
    )
    density, last, before = call(
        unpack_last_kernel,
        [t_cols[0], coefs],
        [back, sums],
        [row] * 3,
        [row_scratch, row_scratch, row_scratch, dma((3,))],
        "unpack_last",
        60,
    )
    return density[None], last[None], before[None]


def solution(mesh):
    blocks = P(("groups", "row"), None, None, None)
    cols = P(("groups", "row"), None)
    return jax.shard_map(
        per_device,
        mesh=mesh,
        in_specs=(blocks, cols, blocks, blocks, cols, blocks, P()),
        out_specs=(blocks, blocks, blocks),
        check_vma=False,
    )
```

```python
import functools

import jax
import jax.numpy as jnp
from jax import lax
from jax.experimental import pallas as pl
from jax.experimental.pallas import tpu as pltpu
from jax.sharding import PartitionSpec as P

REACH = 7
NOTE = 8
SMEM = pl.BlockSpec(memory_space=pltpu.SMEM)
ANY = pl.BlockSpec(memory_space=pl.ANY)


def permute(x, target):
    devices = lax.axis_size("row")
    return lax.ppermute(x, "row", [(i, target(i)) for i in range(devices)])


def after(x, *others):
    return lax.optimization_barrier((x, *others))[0]


RING = (0, 2, 4, 6, 7, 5, 3, 1)


def along_ring(device, by):
    if device % 2:
        by = -by
    return 2 * RING[(RING.index(device // 2) + by) % len(RING)] + device % 2


def window_table(total):
    if total != 16:
        steps = [0] + [by for hop in range(1, REACH + 1) for by in (-hop, hop)]
        return [[(i + by) % total for by in steps] for i in range(total)], (13, 2)
    order = (0, -1, 1, -2, 2, -3, 3, -4)
    table = [[along_ring(source, by) for by in order for source in (i, i ^ 1)] for i in range(total)]
    return table, (14, 2)


def gathered_rows(x, total, exchange):
    if total != 16:
        rows = [x]
        for hop in range(1, REACH + 1):
            for by in (hop, -hop):
                rows.append(permute(x, lambda i, by=by: (i + by) % total))
        yield exchange()
        yield rows[:13]
        yield rows[13:]
        return

    def other_core(row):
        return permute(row, lambda i: i ^ 1)

    def round_of(ahead, behind):
        ahead = permute(ahead, lambda i: along_ring(i, 1))
        behind = permute(behind, lambda i: along_ring(i, -1))
        return ahead, behind, [ahead, other_core(ahead), behind, other_core(behind)]

    rows = [x, other_core(x)]
    ahead, behind, first = round_of(x, x)
    ahead, behind, second = round_of(ahead, behind)
    column = exchange(ahead, behind)
    yield column
    ahead, behind, third = round_of(ahead, behind)
    far = permute(after(ahead, column), lambda i: along_ring(i, 1))
    made = yield rows + first + second + third
    far = after(far, made)
    yield [far, other_core(far)]


def place_of(offset, dropped):
    named = jnp.logical_and(offset <= 2 * REACH, offset != dropped)
    slot = offset - jnp.where(offset > dropped, 1, 0)
    return jnp.clip(slot, 0, 2 * REACH - 1), named


def dropped_offset(cols, row, total):
    offsets = jnp.mod(cols - row + REACH, total)
    return REACH * (2 * REACH + 1) - jnp.sum(offsets, axis=1)


def pack_kernel(total, info_ref, cols_ref, cur_ref, prev_ref, send_ref, cur, prev, zeros, note, sems):
    row = info_ref[0]
    drop = info_ref[2]
    count, size = cur.shape[:2]
    loads = (
        pltpu.make_async_copy(cur_ref, cur, sems.at[0]),
        pltpu.make_async_copy(prev_ref, prev, sems.at[1]),
    )
    for load in loads:
        load.start()
    zeros[...] = jnp.zeros_like(zeros)
    line = lax.broadcasted_iota(jnp.int32, note.shape, 0)
    note[...] = jnp.where(line == 0, info_ref[1], drop).astype(jnp.float32)

    def fill(j, carry):
        offset = lax.rem(j - row + REACH + total, total)
        _, named = place_of(offset, drop)
        pltpu.make_async_copy(note, send_ref.at[j, pl.ds(2 * size, NOTE)], sems.at[2]).start()

        @pl.when(jnp.logical_not(named))
        def _():
            pltpu.make_async_copy(zeros, send_ref.at[j, pl.ds(0, 2 * size)], sems.at[2]).start()

        return carry

    lax.fori_loop(0, total, fill, 0)
    for which, held in enumerate((cur, prev)):
        loads[which].wait()
        for k in range(count):
            place = send_ref.at[cols_ref[k], pl.ds(which * size, size)]
            pltpu.make_async_copy(held.at[k], place, sems.at[2]).start()
    pltpu.make_async_copy(send_ref, send_ref, sems.at[2]).wait()


def split(x):
    high = x.astype(jnp.bfloat16)
    low = (x - high.astype(jnp.float32)).astype(jnp.bfloat16)
    return high, low


class Rows:
    def __init__(self, total, me_ref, table_ref):
        self.me = me_ref[0]
        self.table_ref = table_ref
        self.window = table_ref.shape[0] // total

    def __getitem__(self, w):
        return self.table_ref[self.me * self.window + w]


def kept_rows(total, rows, drops_ref, w):
    row = rows[w]
    offset = lax.rem(rows.me - row + REACH + total, total)
    _, named = place_of(offset, drops_ref[2 * row + 1])
    return named


def fill_pair(pair, block, w):
    size = block.shape[-1]
    high, low = split(block)
    at = pl.ds(pl.multiple_of(w * size, size), size)
    pair[at, pl.ds(0, size)] = high
    pair[at, pl.ds(size, size)] = low


def products_of(rows, pair):
    group, double = rows.shape[:2]
    size = double // 2
    products = jnp.dot(rows.reshape(group * double, rows.shape[2]), pair, preferred_element_type=jnp.float32)
    for r in range(group):
        parts = products[r * double:r * double + size] + products[r * double + size:(r + 1) * double]
        yield parts[:, :size] + parts[:, size:]


def first_kernel(total, window, start, count, group, drops_ref, me_ref, table_ref, t_ref, *refs):
    rows = Rows(total, me_ref, table_ref)
    h_refs = refs[:count]
    if start:
        pair_in, _ = refs[count:count + 2]
        dense_ref, out_ref = refs[count + 2:count + 4]
    else:
        dense_ref, out_ref, pair_out, blocks = refs[count:count + 4]
    stage, dense, prev, pair, h_sem, t_sem, prev_sem, pair_sem, dense_sem, out_sem = refs[-10:]
    size = t_ref.shape[-1]
    kept = functools.partial(kept_rows, total, rows, drops_ref)

    if start:
        pltpu.make_async_copy(pair_in, pair, pair_sem).start()
    else:
        for w in range(window):
            pltpu.make_async_copy(t_ref.at[rows[w], pl.ds(0, size)], blocks.at[w], t_sem).start()
    for r in range(count):
        pltpu.make_async_copy(h_refs[r], stage.at[r], h_sem.at[r]).start()
    for r in range(count):
        block = t_ref.at[rows[start + r], pl.ds(size, size)]
        pltpu.make_async_copy(block, prev.at[r], prev_sem).start()
    if not start:
        pltpu.make_async_copy(blocks, blocks, t_sem).wait()
        for w in range(window):
            fill_pair(pair, jnp.where(kept(w), blocks[w], 0.0), w)
        pltpu.make_async_copy(pair, pair_out, pair_sem).start()

    def densify(r, slot, place):
        row = rows[start + r]
        drop = drops_ref[2 * row]
        for p in range(window):
            offset = lax.rem(rows[p] - row + REACH + total, total)
            k, named = place_of(offset, drop)
            high, low = split(jnp.where(named, stage[r, k], 0.0))
            dense[slot, place, pl.ds(0, size), pl.ds(p * size, size)] = high
            dense[slot, place, pl.ds(size, size), pl.ds(p * size, size)] = low

    def store(g, slot):
        return pltpu.make_async_copy(dense.at[slot], dense_ref.at[pl.ds(g * group, group)], dense_sem.at[slot])

    groups = count // group

    def one(g, carry):
        slot = lax.rem(g, 2)

        @pl.when(g >= 2)
        def _():
            store(g - 2, slot).wait()

        def ready(place, carry):
            r = g * group + place
            pltpu.make_async_copy(stage.at[r], stage.at[r], h_sem.at[r]).wait()
            densify(r, slot, place)
            return carry

        lax.fori_loop(0, group, ready, 0)
        store(g, slot).start()
        if start:

            @pl.when(g == 0)
            def _():
                pltpu.make_async_copy(pair, pair, pair_sem).wait()

        @pl.when(g == 0)
        def _():
            pltpu.make_async_copy(prev, prev, prev_sem).wait()

        for place, product in enumerate(products_of(dense[slot], pair[...])):
            r = g * group + place
            prev[r] = jnp.where(kept(start + r), 2.0 * product - prev[r], 0.0)
            pltpu.make_async_copy(prev.at[r], out_ref.at[rows[start + r]], out_sem).start()
        return carry

    lax.fori_loop(0, groups, one, 0)
    for g in range(max(groups - 2, 0), groups):
        store(g, g % 2).wait()
    if not start:
        pltpu.make_async_copy(pair, pair, pair_sem).wait()
    pltpu.make_async_copy(prev, prev, out_sem).wait()


def later_kernel(total, window, group, parts, drops_ref, me_ref, table_ref, *refs):
    rows = Rows(total, me_ref, table_ref)
    dense_refs = refs[:len(parts)]
    t_ref, first_ref, out_ref, dense, terms, pairs, dense_sem, t_sem, first_sem, out_sem = refs[len(parts):]
    size = terms.shape[-1]
    groups = window // group
    kept = functools.partial(kept_rows, total, rows, drops_ref)
    for w in range(window):
        pltpu.make_async_copy(first_ref.at[rows[w]], terms.at[w, 1], first_sem).start()
    start = 0
    for part, dense_ref in zip(parts, dense_refs):
        for w in range(start, start + part):
            pltpu.make_async_copy(dense_ref.at[w - start], dense.at[w], dense_sem.at[w // group]).start()
        start += part
    for w in range(window):
        pltpu.make_async_copy(t_ref.at[rows[w], pl.ds(0, size)], terms.at[w, 0], t_sem).start()
    pltpu.make_async_copy(terms.at[:, 1], terms.at[:, 1], first_sem).wait()
    for w in range(window):
        fill_pair(pairs.at[0], terms[w, 1], w)
    pltpu.make_async_copy(terms.at[:, 0], terms.at[:, 0], t_sem).wait()

    def one(g, carry, step):
        held = dense.at[pl.ds(g * group, group)]
        if step == 0:
            pltpu.make_async_copy(held, held, dense_sem.at[g]).wait()
        for r, product in enumerate(products_of(held[...], pairs[step])):
            w = g * group + r
            newest = jnp.where(kept(w), 2.0 * product - terms[w, step], 0.0)
            terms[w, step] = newest
            if step == 0:
                fill_pair(pairs.at[1], newest, w)
            pltpu.make_async_copy(terms.at[w, step], out_ref.at[rows[w], step], out_sem).start()
        return carry

    for step in range(2):
        lax.fori_loop(0, groups, functools.partial(one, step=step), 0)
    pltpu.make_async_copy(terms, terms, out_sem).wait()


def unpack_first_kernel(cols_ref, coefs_ref, first_ref, density_ref, out_ref, sums, one, sems):
    load = pltpu.make_async_copy(density_ref, sums, sems.at[0])
    load.start()
    for k in range(cols_ref.shape[0]):
        pltpu.make_async_copy(first_ref.at[cols_ref[k]], one.at[k], sems.at[1]).start()
    load.wait()
    pltpu.make_async_copy(one, one, sems.at[1]).wait()
    sums[...] += coefs_ref[0] * one[...]
    store = pltpu.make_async_copy(sums, out_ref, sems.at[0])
    store.start()
    store.wait()


def unpack_last_kernel(cols_ref, coefs_ref, held_ref, sum_ref, density_ref, last_ref, before_ref, sums, two, three, sems):
    load = pltpu.make_async_copy(sum_ref, sums, sems.at[0])
    load.start()
    for place, sem, which in ((two, 1, 0), (three, 2, 1)):
        for k in range(cols_ref.shape[0]):
            pltpu.make_async_copy(held_ref.at[cols_ref[k], which], place.at[k], sems.at[sem]).start()
    pltpu.make_async_copy(two, two, sems.at[1]).wait()
    before = pltpu.make_async_copy(two, before_ref, sems.at[1])
    before.start()
    pltpu.make_async_copy(three, three, sems.at[2]).wait()
    last = pltpu.make_async_copy(three, last_ref, sems.at[2])
    last.start()
    load.wait()
    sums[...] = sums[...] + coefs_ref[1] * two[...] + coefs_ref[2] * three[...]
    store = pltpu.make_async_copy(sums, density_ref, sems.at[0])
    store.start()
    before.wait()
    last.wait()
    store.wait()


def per_device(h_blocks, h_cols, term_prev, term_cur, t_cols, density_in, coefs):
    total = lax.axis_size("row")
    me = lax.axis_index("row")
    count, size = h_blocks.shape[1:3]
    drop_h = dropped_offset(h_cols, me, total)
    drop_t = dropped_offset(t_cols, me, total)
    f32, bf16 = jnp.float32, jnp.bfloat16
    dma = pltpu.SemaphoreType.DMA
    row = jax.ShapeDtypeStruct((count, size, size), f32)
    row_scratch = pltpu.VMEM(row.shape, f32)

    def call(kernel, smem, arrays, outs, scratch, name, megabytes, aliases={}):
        return pl.pallas_call(
            kernel,
            out_shape=[pltpu.HBM(out.shape, out.dtype) for out in outs],
            in_specs=[SMEM] * len(smem) + [ANY] * len(arrays),
            out_specs=[ANY] * len(outs),
            scratch_shapes=scratch,
            input_output_aliases=aliases,
            compiler_params=pltpu.CompilerParams(vmem_limit_bytes=megabytes * 1024 * 1024),
            name=name,
        )(*smem, *arrays)

    def in_hbm(x):
        return pltpu.with_memory_space_constraint(x, pltpu.HBM)

    def exchange(x):
        return lax.all_to_all(x, "row", 0, 0, tiled=True)

    (send,) = call(
        functools.partial(pack_kernel, total),
        [jnp.stack([me, drop_h[0], drop_t[0]]), t_cols[0]],
        [term_cur[0], term_prev[0]],
        [jax.ShapeDtypeStruct((total, 2 * size + NOTE, size), f32)],
        [
            row_scratch,
            row_scratch,
            pltpu.VMEM((2 * size, size), f32),
            pltpu.VMEM((NOTE, size), f32),
            dma((3,)),
        ],
        "pack",
        60,
    )
    table, parts = window_table(total)
    gathered = gathered_rows(h_blocks[0], total, lambda *others: exchange(after(send, *others)))
    column = next(gathered)
    drops = column[:, 2 * size:2 * size + 2, 0].astype(jnp.int32).reshape(-1)
    rows = jnp.array(table, jnp.int32).reshape(-1)
    window = sum(parts)
    dense_shape = (window, 2 * size, window * size)
    pair_shape = (window * size, 2 * size)
    dense = []
    start = 0
    for part in parts:
        h_rows = gathered.send(dense[-1] if start else None)
        group = max(g for g in (2, 7, 13) if part % g == 0)
        scratch = [
            pltpu.VMEM((part, count, size, size), f32),
            pltpu.VMEM((min(2, part // group), group) + dense_shape[1:], bf16),
            pltpu.VMEM((part, size, size), f32),
            pltpu.VMEM(pair_shape, bf16),
            dma((part,)),
            dma,
            dma,
            dma,
            dma((2,)),
            dma,
        ]
        if not start:
            scratch = [pltpu.VMEM((window, size, size), f32)] + scratch
        result = call(
            functools.partial(first_kernel, total, window, start, part, group),
            [drops, me[None], rows],
            [in_hbm(column), *h_rows, in_hbm(pair), term1] if start else [column, *h_rows],
            [
                jax.ShapeDtypeStruct((part,) + dense_shape[1:], bf16),
                jax.ShapeDtypeStruct((total, size, size), f32),
            ] + ([] if start else [jax.ShapeDtypeStruct(pair_shape, bf16)]),
            scratch,
            "first",
            24 if start else 60,
            {part + 5: 1} if start else {},
        )
        dense.append(result[0])
        term1 = result[1]
        if not start:
            pair = result[2]
        start += part
    back1 = exchange(term1)
    group = max(g for g in (3, 4) if window % g == 0)
    (terms,) = call(
        functools.partial(later_kernel, total, window, group, parts),
        [drops, me[None], rows],
        [*dense, column, term1],
        [jax.ShapeDtypeStruct((total, 2, size, size), f32)],
        [
            pltpu.VMEM(dense_shape, bf16),
            pltpu.VMEM((window, 2, size, size), f32),
            pltpu.VMEM((2,) + pair_shape, bf16),
            dma((window // group,)),
            dma,
            dma,
            dma,
        ],
        "later",
        60,
    )
    back = exchange(after(terms, back1))
    (sums,) = call(
        unpack_first_kernel,
        [t_cols[0], coefs],
        [back1, density_in[0]],
        [row],
        [row_scratch, row_scratch, dma((2,))],
        "unpack_first",
        60,
    )
    density, last, before = call(
        unpack_last_kernel,
        [t_cols[0], coefs],
        [back, sums],
        [row] * 3,
        [row_scratch, row_scratch, row_scratch, dma((3,))],
        "unpack_last",
        60,
    )
    return density[None], last[None], before[None]


def solution(mesh):
    blocks = P(("groups", "row"), None, None, None)
    cols = P(("groups", "row"), None)
    return jax.shard_map(
        per_device,
        mesh=mesh,
        in_specs=(blocks, cols, blocks, blocks, cols, blocks, P()),
        out_specs=(blocks, blocks, blocks),
        check_vma=False,
    )
```
